256 devices in a mesh: gz: 256 (over y, z, x, core).
Axes of the slice: x: 4, y: 4, z: 8, core: 2. Of those that a mesh axis runs over, the one named last changes fastest.
Arguments:
- pressure_guess: float32 [2048, 64, 512], P('gz'), may hold values from -6 to 6
- source: float32 [2048, 64, 512], P('gz'), may hold values from -6 to 6
- conductance: float32 [2048, 64, 512], P('gz'), may hold values from 0.25 to 4
Outputs:
- pressure: float32 [2048, 64, 512], P('gz')
- correction_mid: float32 [1024, 32, 256], P('gz')
- correction_low: float32 [512, 16, 128], P('gz')
The draws below stay inside these ranges and needn't reach their ends.
All inputs are finite; a program needn't handle non-finite values.
Results may differ from the reference program's by a relative error of at most 0.00002.
Values sent between devices are 32-bit elements; how exact they have to be, the bound alone decides.
A program may use at most 192 MiB of HBM per device.

```python
import math
import jax
import jax.numpy as jnp
from jax import lax

NY = 64
NX = 512
NZ = 2048


def shard_levels(stream_key, extent, shards, smallest, high):
    def one(axis_at, blocks):
        heights = jax.random.uniform(jax.random.fold_in(jax.random.fold_in(stream_key, 6), axis_at), (blocks,), jnp.float32, smallest / len(shards), high / len(shards))
        return jnp.repeat(jnp.exp(heights), extent[axis_at] // blocks).reshape((-1,) + (1,) * (len(extent) - axis_at - 1))

    loudness = one(*shards[0])
    for cut in shards[1:]:
        loudness = loudness * one(*cut)
    return loudness


def normal_values(rng, dims, width, reach, split=(), kind=jnp.bfloat16):
    values = width * jax.random.normal(rng, dims, jnp.float32)
    if split:
        values = values * shard_levels(rng, dims, split, -0.22, 0.18)
    return jnp.clip(values, -reach, reach).astype(kind)


def setup_inputs(seed: int = 0) -> dict:
    arg_keys = jax.random.split(jax.random.key(seed), 4)
    return {
        "pressure_guess": normal_values(arg_keys[0], (NZ, NY, NX), 1.0, 6.0, ((0, 256),), jnp.float32),
        "source": normal_values(arg_keys[1], (NZ, NY, NX), 1.0, 6.0, ((0, 256),), jnp.float32),
        "conductance": jnp.clip(jnp.exp(math.log(4.0) - 2.7725887 * jax.random.uniform(arg_keys[2], (NZ, NY, NX), jnp.float32) ** shard_levels(arg_keys[2], (NZ, NY, NX), ((0, 256),), -0.2, 0.2)), 0.25, 4.0),
    }


def face_terms(cond_ext):
    padded = jnp.pad(cond_ext, ((0, 0), (1, 1), (1, 1)))
    centre = padded[1:-1, 1:-1, 1:-1]
    sides = [padded[2:, 1:-1, 1:-1], padded[:-2, 1:-1, 1:-1], padded[1:-1, 2:, 1:-1], padded[1:-1, :-2, 1:-1], padded[1:-1, 1:-1, 2:], padded[1:-1, 1:-1, :-2]]
    faces = [0.5 * (centre + other) for other in sides]
    diag = faces[0]
    for face in faces[1:]:
        diag = diag + face
    return faces, diag


def gather_off(faces, field_ext):
    padded = jnp.pad(field_ext, ((0, 0), (1, 1), (1, 1)))
    sides = [padded[2:, 1:-1, 1:-1], padded[:-2, 1:-1, 1:-1], padded[1:-1, 2:, 1:-1], padded[1:-1, :-2, 1:-1], padded[1:-1, 1:-1, 2:], padded[1:-1, 1:-1, :-2]]
    total = faces[0] * sides[0]
    for face, other in zip(faces[1:], sides[1:]):
        total = total + face * other
    return total


def red_mask(shape, offset):
    zpos = lax.broadcasted_iota(jnp.int32, shape, 0)
    ypos = lax.broadcasted_iota(jnp.int32, shape, 1)
    xpos = lax.broadcasted_iota(jnp.int32, shape, 2)
    return (zpos + ypos + xpos + offset) % 2 == 0


def restrict_axis(padded, axis):
    count = padded.shape[axis] - 2
    parts = [lax.slice_in_dim(padded, start, start + count - 1, 2, axis) for start in range(4)]
    return 0.125 * (parts[0] + 3.0 * parts[1] + 3.0 * parts[2] + parts[3])


def restrict(residual_ext):
    out = restrict_axis(residual_ext, 0)
    out = restrict_axis(jnp.pad(out, ((0, 0), (1, 1), (0, 0))), 1)
    return restrict_axis(jnp.pad(out, ((0, 0), (0, 0), (1, 1))), 2)


def coarsen(cond):
    depth, rows, cols = cond.shape
    grouped = cond.reshape(depth // 2, 2, rows // 2, 2, cols // 2, 2)
    return 0.125 * jnp.sum(grouped, axis=(1, 3, 5))


def zpad(field):
    return jnp.pad(field, ((1, 1), (0, 0), (0, 0)))


def sweep_whole(start, rhs, cond, scale):
    faces, diag = face_terms(zpad(cond))
    red = red_mask(start.shape, 0)
    off = gather_off(faces, zpad(start))
    field = jnp.where(red, (rhs / scale + off) / diag, start)
    off = gather_off(faces, zpad(field))
    field = jnp.where(red, field, (rhs / scale + off) / diag)
    return field, faces, diag


def residual_whole(field, rhs, faces, diag, scale):
    off = gather_off(faces, zpad(field))
    return rhs - scale * (diag * field - off)


def reference(pressure_guess, source, conductance):
    pressure, faces, diag = sweep_whole(pressure_guess, source, conductance, 1.0)
    rhs1 = restrict(zpad(residual_whole(pressure, source, faces, diag, 1.0)))
    cond1 = coarsen(conductance)
    correction_mid, faces, diag = sweep_whole(jnp.zeros_like(rhs1), rhs1, cond1, 0.25)
    rhs2 = restrict(zpad(residual_whole(correction_mid, rhs1, faces, diag, 0.25)))
    cond2 = coarsen(cond1)
    correction_low, faces, diag = sweep_whole(jnp.zeros_like(rhs2), rhs2, cond2, 0.0625)
    return pressure, correction_mid, correction_low
```

```python
import jax
import jax.numpy as jnp
from jax import lax
from jax.experimental import pallas as pl
from jax.experimental.pallas import tpu as pltpu
from jax.sharding import PartitionSpec as P

F32 = jnp.float32
BF16 = jnp.bfloat16


def parity(shape, offset):
    rows = lax.broadcasted_iota(jnp.int32, shape, 0)
    cols = lax.broadcasted_iota(jnp.int32, shape, 1)
    return ((rows + cols + offset) & 1) == 0


def shifts(plane):
    ny, nx = plane.shape
    return (
        pltpu.roll(plane, ny - 1, 0),
        pltpu.roll(plane, 1, 0),
        pltpu.roll(plane, nx - 1, 1),
        pltpu.roll(plane, 1, 1),
    )


def insides(shape):
    rows = lax.broadcasted_iota(jnp.int32, shape, 0)
    cols = lax.broadcasted_iota(jnp.int32, shape, 1)
    return (rows < shape[0] - 1, rows > 0, cols < shape[1] - 1, cols > 0)


def side_faces(centre, other):
    faces, total = [], None
    for near, inside in zip(shifts(other), insides(centre.shape)):
        near = jnp.where(inside, near, 0.0)
        faces.append(jnp.where(inside, centre + near, 0.0))
        total = near if total is None else total + near
    return faces, total


def dot_parts(rows, weights):
    count = rows.shape[0]
    high = rows.astype(BF16)
    rest = rows - high.astype(F32)
    middle = rest.astype(BF16)
    low = (rest - middle.astype(F32)).astype(BF16)
    out = jnp.dot(
        jnp.concatenate([high, middle, low], axis=0), weights, preferred_element_type=F32
    )
    return out[:count] + (out[count : 2 * count] + out[2 * count :])


def weights_of(shape, inner, outer):
    fine = lax.broadcasted_iota(jnp.int32, shape, 0)
    coarse = lax.broadcasted_iota(jnp.int32, shape, 1)
    apart = fine - 2 * coarse
    near = (apart == 0) | (apart == 1)
    far = (apart == -1) | (apart == 2)
    return jnp.where(near, inner, jnp.where(far, outer, 0.0)).astype(BF16)


def kernel(
    size,
    g_hbm, b_hbm, c_hbm,
    p_ref, mid_ref, low_ref,
    craw, graw, braw,
    cr, cb, gb, rr, dl, rho,
    fpair, fro, frs, fbo, fbs,
    dr, db, nr,
    zbuf, zmid, wres, wsum,
    send_m, send_q, send_c1, send_c2, send_2, send_3,
    halo_c, halo_m, halo_q, halo_c1, halo_c2, halo_2, halo_3,
    load_sem,
    s_c, s_m, s_q, s_c1, s_c2, s_2, s_3,
    r_c, r_m, r_q, r_c1, r_c2, r_2, r_3,
):
    me = lax.axis_index("gz")
    nz, ny, nx = craw.shape
    pairs = nz // 2
    plane = (ny, nx)
    plane1 = (ny // 2, nx // 2)
    plane2 = (ny // 4, nx // 4)
    has = (me > 0, me < size - 1)

    loads = [
        pltpu.make_async_copy(src, dst, load_sem.at[i])
        for i, (src, dst) in enumerate(((c_hbm, craw), (g_hbm, graw), (b_hbm, braw)))
    ]
    for load in loads:
        load.start()

    barrier = pltpu.get_barrier_semaphore()
    for side in range(2):
        @pl.when(has[side])
        def _(side=side):
            pl.semaphore_signal(
                barrier, inc=1, device_id=(me + 2 * side - 1,),
                device_id_type=pl.DeviceIdType.MESH,
            )

    for ref in (cr, cb, gb, rr, dl, rho):
        ref[0] = jnp.zeros(plane, F32)
        ref[pairs + 1] = jnp.zeros(plane, F32)
    dl[1] = jnp.zeros(plane, F32)
    dl[pairs] = jnp.zeros(plane, F32)
    for ref, depth in ((zbuf, ny), (zmid, ny // 2)):
        for i in range(ref.shape[0]):
            for j in range(ref.shape[1]):
                ref[i, j, 0:8] = jnp.zeros((8, 128), F32)
                ref[i, j, depth + 8 : depth + 16] = jnp.zeros((8, 128), F32)
    for side in range(2):
        @pl.when(jnp.logical_not(has[side]))
        def _(side=side):
            for ref in (halo_c, halo_q):
                ref[side] = jnp.zeros(ref.shape[1:], F32)
            for ref in (halo_m, halo_c1, halo_c2, halo_2, halo_3):
                for i in range(ref.shape[1]):
                    ref[side, i] = jnp.zeros(ref.shape[2:], F32)
    wres[...] = weights_of(wres.shape, 3.0, 1.0)
    wsum[...] = weights_of(wsum.shape, 1.0, 0.0)

    def copy_out(side, src, dst, s_sem, r_sem):
        return pltpu.make_async_remote_copy(
            src_ref=src, dst_ref=dst.at[1 - side], send_sem=s_sem.at[side],
            recv_sem=r_sem.at[1 - side], device_id=(me + 2 * side - 1,),
            device_id_type=pl.DeviceIdType.MESH,
        )

    def send(src_of, dst, s_sem, r_sem):
        for side in range(2):
            @pl.when(has[side])
            def _(side=side):
                copy_out(side, src_of(side), dst, s_sem, r_sem).start()

    def wait_recv(side, present, dst, s_sem, r_sem):
        @pl.when(present)
        def _():
            pltpu.make_async_remote_copy(
                src_ref=dst.at[side], dst_ref=dst.at[side], send_sem=s_sem.at[side],
                recv_sem=r_sem.at[side], device_id=(me + 2 * side - 1,),
                device_id_type=pl.DeviceIdType.MESH,
            ).wait_recv()

    even = parity(plane, 0)

    def even_first(first, second):
        return jnp.where(parity(plane, 0), first, second)

    loads[0].wait()

    def put_rows(ref, k, value):
        for j in range(ref.shape[1]):
            ref[k, j, 8 : value.shape[0] + 8] = value[:, 128 * j : 128 * j + 128]

    def get_rows(ref, k, start, count):
        return jnp.concatenate(
            [ref[k, j, pl.ds(start, count, stride=2), :] for j in range(ref.shape[1])], axis=1
        )

    def pack(k, carry):
        low, high = craw[2 * k], craw[2 * k + 1]
        cr[k + 1] = even_first(low, high)
        cb[k + 1] = even_first(high, low)
        put_rows(zbuf, k, low + high)
        return carry

    lax.fori_loop(0, pairs, pack, 0)
    pl.semaphore_wait(barrier, jnp.where(has[0] & has[1], 2, 1))
    send(lambda side: craw.at[(nz - 1) * side], halo_c, s_c, r_c)

    def faces(k, carry):
        own, other = cr[k + 1], cb[k + 1]
        fpair[k] = own + other
        outer = even_first(cb[k], cb[k + 2])
        sides, total = side_faces(own, other)
        fro[k] = own + outer
        for i in range(4):
            frs[k, i] = sides[i]
        dr[k] = 6.0 * own + other + outer + total
        outer = even_first(cr[k + 2], cr[k])
        sides, total = side_faces(other, own)
        fbo[k] = other + outer
        for i in range(4):
            fbs[k, i] = sides[i]
        db[k] = 6.0 * other + own + outer + total
        return carry

    lax.fori_loop(0, pairs, faces, 0)

    def gather(k, centre, outer, f_outer, f_sides):
        total = fpair[k] * centre + f_outer[k] * outer
        for i, near in enumerate(shifts(centre)):
            total = total + f_sides[k, i] * near
        return total

    loads[1].wait()
    loads[2].wait()

    def pack_g(k, carry):
        gb[k + 1] = even_first(graw[2 * k + 1], graw[2 * k])
        return carry

    lax.fori_loop(0, pairs, pack_g, 0)

    def red(k, carry):
        rhs = even_first(braw[2 * k], braw[2 * k + 1])
        off = gather(k, gb[k + 1], even_first(gb[k], gb[k + 2]), fro, frs)
        top = 2.0 * rhs + off
        nr[k] = top
        rr[k + 1] = top / dr[k]
        return carry

    lax.fori_loop(0, pairs, red, 0)

    for side in range(2):
        k = (pairs - 1) * side
        mine = parity(plane, side)
        send_m[side, 0] = jnp.where(mine, dr[k], db[k])
        send_m[side, 1] = jnp.where(mine, nr[k], gb[k + 1])
        rhs = even_first(braw[2 * k + 1], braw[2 * k])
        part = 2.0 * rhs + fpair[k] * rr[k + 1]
        half = ny // 2
        send_q[side] = jnp.where(
            parity((half, nx), side), pltpu.roll(part[half:], 1, 0), part[:half]
        )
    send(lambda side: send_m.at[side], halo_m, s_m, r_m)
    send(lambda side: send_q.at[side], halo_q, s_q, r_q)

    def put_pressure(k, reds, blacks):
        p_ref[2 * k] = even_first(reds, blacks)
        p_ref[2 * k + 1] = even_first(blacks, reds)

    def black(k, carry):
        rhs = even_first(braw[2 * k + 1], braw[2 * k])
        reds = rr[k + 1]
        off = gather(k, reds, even_first(rr[k + 2], rr[k]), fbo, fbs)
        new = (2.0 * rhs + off) / db[k]
        dl[k + 1] = new - gb[k + 1]
        put_pressure(k, reds, new)
        return carry

    lax.fori_loop(1, pairs - 1, black, 0)

    def residual(k, carry):
        rho[k + 1] = gather(k, dl[k + 1], even_first(dl[k], dl[k + 2]), fro, frs)
        return carry

    lax.fori_loop(1, pairs - 1, residual, 0)

    ny1, ny2 = ny // 2, ny // 4
    rows = [
        get_rows(zbuf, k, 8, ny1) + get_rows(zbuf, k, 9, ny1)
        for k in range(pairs)
    ]
    sums = 0.125 * dot_parts(jnp.concatenate(rows, axis=0), wsum[...])
    c1 = [sums[k * ny1 : (k + 1) * ny1] for k in range(pairs)]

    def plane_sum(value):
        total = None
        for near, inside in zip(shifts(value), insides(value.shape)):
            near = jnp.where(inside, near, 0.0)
            total = near if total is None else total + near
        return total

    def diagonals(coefs):
        out = []
        for k, coef in enumerate(coefs):
            total = 6.0 * coef + plane_sum(coef)
            if k > 0:
                total = total + coefs[k - 1]
            if k < len(coefs) - 1:
                total = total + coefs[k + 1]
            out.append(total)
        return out

    d1 = diagonals(c1)
    for k in range(pairs // 2):
        put_rows(zmid, k, c1[2 * k] + c1[2 * k + 1])
    rows = [
        get_rows(zmid, k, 8, ny2) + get_rows(zmid, k, 9, ny2)
        for k in range(pairs // 2)
    ]
    weights = wsum[0 : nx // 2, 0 : nx // 4]
    sums = 0.125 * dot_parts(jnp.concatenate(rows, axis=0), weights)
    c2 = [sums[k * ny2 : (k + 1) * ny2] for k in range(pairs // 2)]
    d2 = diagonals(c2)
    for side in range(2):
        send_c1[side, 0] = c1[-side]
        send_c1[side, 1] = d1[-side]
        send_c2[side, 0] = c2[-side]
        send_c2[side, 1] = d2[-side]
    send(lambda side: send_c1.at[side], halo_c1, s_c1, r_c1)
    send(lambda side: send_c2.at[side], halo_c2, s_c2, r_c2)

    def finish(step, carry):
        side = (step + 1 + me) % 2
        present = jnp.where(side == 0, me, size - 1 - me) > 0
        wait_recv(side, present, halo_c, s_c, r_c)
        wait_recv(side, present, halo_m, s_m, r_m)
        wait_recv(side, present, halo_q, s_q, r_q)
        k = (pairs - 1) * side
        here = (nz - 1) * side
        mine = parity(plane, side)
        inside = jnp.where(present, 1.0, 0.0)
        hc, hd, hm = halo_c[side], halo_m[side, 0], halo_m[side, 1]
        c0, g0 = craw[here], graw[here]
        face = c0 + hc
        top = jnp.where(mine, nr[k], hm) + face * jnp.where(mine, hm, g0)
        value = top / jnp.where(mine, dr[k] + hc, hd + c0)
        value = jnp.where(mine, value, inside * value)
        reds = jnp.where(mine, value, rr[k + 1])
        rr[k + 1] = reds
        hq = halo_q[side]
        off = jnp.concatenate([hq, pltpu.roll(hq, ny // 2 - 1, 0)], axis=0)
        off = off + face * value
        sides, _ = side_faces(hc, hc)
        for f, near in zip(sides, shifts(value)):
            off = off + f * near
        halo_delta = inside * (off / (hd + c0) - hm)

        rhs = even_first(braw[2 * k + 1], braw[2 * k])
        off = gather(k, reds, even_first(rr[k + 2], rr[k]), fbo, fbs)
        off = off + jnp.where(mine, 0.0, face * value)
        new = (2.0 * rhs + off) / (db[k] + jnp.where(mine, 0.0, hc))
        delta = new - gb[k + 1]
        dl[k + 1] = delta
        put_pressure(k, reds, new)

        off = gather(k, delta, even_first(dl[k], dl[k + 2]), fro, frs)
        rho[k + 1] = off + jnp.where(mine, face * halo_delta, 0.0)
        inner = k + 1 - 2 * side
        more = (cr[inner + 1] + cb[k + 1]) * delta
        rho[inner + 1] = rho[inner + 1] + jnp.where(mine, more, 0.0)
        return carry

    lax.fori_loop(0, 2, finish, 0)

    def thin(k, carry):
        put_rows(zbuf, k, 3.0 * rho[k + 1] + even_first(rho[k + 2], rho[k]))
        return carry

    lax.fori_loop(0, pairs, thin, 0)
    put_rows(zbuf, pairs, even_first(rho[1], 0.0))
    put_rows(zbuf, pairs + 1, even_first(0.0, rho[pairs]))

    def restrict(ref, count, out_rows, weights, scale):
        rows = [
            (get_rows(ref, k, 7, out_rows) + get_rows(ref, k, 10, out_rows))
            + 3.0 * (get_rows(ref, k, 8, out_rows) + get_rows(ref, k, 9, out_rows))
            for k in range(count)
        ]
        out = scale * dot_parts(jnp.concatenate(rows, axis=0), weights)
        return [out[k * out_rows : (k + 1) * out_rows] for k in range(count)]

    parts = restrict(zbuf, pairs + 2, ny1, wres[...], 0.5 ** 10)
    rhs1, edge1 = parts[:pairs], parts[pairs:]
    for side in range(2):
        k = (pairs - 1) * side
        inner = k + 1 - 2 * side
        send_2[side, 0] = rhs1[k]
        send_2[side, 1] = edge1[side]
        send_2[side, 2] = (c1[k] + c1[inner]) * (8.0 * rhs1[inner] / d1[inner])
    send(lambda side: send_2.at[side], halo_2, s_2, r_2)

    for side in range(2):
        wait_recv(side, has[side], halo_c1, s_c1, r_c1)
        wait_recv(side, has[side], halo_c2, s_c2, r_c2)
        wait_recv(side, has[side], halo_2, s_2, r_2)
    inside = [jnp.where(has[side], 1.0, 0.0) for side in range(2)]

    def with_ends(own, low, high):
        return [low] + list(own) + [high]

    def red_black(rhs, coefs, diags, seconds, factor, depth):
        masks = [parity(rhs[0].shape, i - 1) for i in range(depth + 2)]
        reds = []
        for i in range(depth + 2):
            value = jnp.where(masks[i], factor * rhs[i] / diags[i], 0.0)
            if i == 0:
                value = inside[0] * value
            if i == depth + 1:
                value = inside[1] * value
            reds.append(value)
        return masks, reds

    def off_of(coefs, fields, i):
        around = plane_sum(fields[i])
        weighted = plane_sum(coefs[i] * fields[i])
        for j in (i - 1, i + 1):
            if 0 <= j < len(fields):
                around = around + fields[j]
                weighted = weighted + coefs[j] * fields[j]
        return coefs[i] * around + weighted

    ends = [halo_2[0, 0] + edge1[0], halo_2[1, 0] + edge1[1]]
    rhs1[0] = rhs1[0] + halo_2[0, 1]
    rhs1[-1] = rhs1[-1] + halo_2[1, 1]
    d1 = with_ends(d1, halo_c1[0, 1] + c1[0], halo_c1[1, 1] + c1[-1])
    d1[1] = d1[1] + halo_c1[0, 0]
    d1[-2] = d1[-2] + halo_c1[1, 0]
    c1 = with_ends(c1, halo_c1[0, 0], halo_c1[1, 0])
    rhs1 = with_ends(rhs1, ends[0], ends[1])
    masks, reds = red_black(rhs1, c1, d1, None, 8.0, pairs)
    blacks = []
    for i in range(pairs + 2):
        top = 8.0 * rhs1[i] + off_of(c1, reds, i)
        if i == 0:
            top = inside[0] * (top + halo_2[0, 2])
        if i == pairs + 1:
            top = inside[1] * (top + halo_2[1, 2])
        blacks.append(jnp.where(masks[i], 0.0, top / d1[i]))
    for i in range(1, pairs + 1):
        mid_ref[i - 1] = reds[i] + blacks[i]
    res = [
        jnp.where(masks[i], off_of(c1, blacks, i), 0.0) for i in range(1, pairs + 1)
    ]

    put_rows(zmid, 0, 3.0 * (res[0] + res[1]) + res[2])
    put_rows(zmid, 1, 3.0 * (res[2] + res[3]) + res[1])
    put_rows(zmid, 2, res[0])
    put_rows(zmid, 3, res[3])
    parts = restrict(zmid, 4, ny2, wres[0 : nx // 2, 0 : nx // 4], 0.5 ** 12)
    rhs2, edge2 = parts[:2], parts[2:]
    for side in range(2):
        send_3[side, 0] = rhs2[side]
        send_3[side, 1] = edge2[side]
    send(lambda side: send_3.at[side], halo_3, s_3, r_3)
    for side in range(2):
        wait_recv(side, has[side], halo_3, s_3, r_3)
    ends = [halo_3[side, 0] + edge2[side] for side in range(2)]
    rhs2 = [rhs2[side] + halo_3[side, 1] for side in range(2)]
    d2 = with_ends(d2, halo_c2[0, 1] + c2[0], halo_c2[1, 1] + c2[1])
    d2[1] = d2[1] + halo_c2[0, 0]
    d2[2] = d2[2] + halo_c2[1, 0]
    c2 = with_ends(c2, halo_c2[0, 0], halo_c2[1, 0])
    rhs2 = with_ends(rhs2, ends[0], ends[1])
    masks, reds = red_black(rhs2, c2, d2, None, 32.0, 2)
    for i in (1, 2):
        top = 32.0 * rhs2[i] + off_of(c2, reds, i)
        low_ref[i - 1] = jnp.where(masks[i], reds[i], top / d2[i])

    for side in range(2):
        @pl.when(has[side])
        def _(side=side):
            for src, dst, s_sem, r_sem in (
                (craw.at[(nz - 1) * side], halo_c, s_c, r_c),
                (send_m.at[side], halo_m, s_m, r_m),
                (send_q.at[side], halo_q, s_q, r_q),
                (send_c1.at[side], halo_c1, s_c1, r_c1),
                (send_c2.at[side], halo_c2, s_c2, r_c2),
                (send_2.at[side], halo_2, s_2, r_2),
                (send_3.at[side], halo_3, s_3, r_3),
            ):
                copy_out(side, src, dst, s_sem, r_sem).wait_send()


def on_device(size, pressure_guess, source, conductance):
    nz, ny, nx = pressure_guess.shape
    pairs = nz // 2
    ny1, nx1, ny2, nx2 = ny // 2, nx // 2, ny // 4, nx // 4

    def vmem(*shape):
        return pltpu.VMEM(shape, F32)

    slab = [vmem(nz, ny, nx)] * 3
    padded = [vmem(pairs + 2, ny, nx)] * 6
    faces = [
        vmem(pairs, ny, nx), vmem(pairs, ny, nx), vmem(pairs, 4, ny, nx),
        vmem(pairs, ny, nx), vmem(pairs, 4, ny, nx),
    ]
    sums = [vmem(pairs, ny, nx)] * 3
    work = [
        vmem(pairs + 2, nx // 128, ny + 16, 128), vmem(4, nx1 // 128, ny1 + 16, 128),
        pltpu.VMEM((nx, nx1), BF16), pltpu.VMEM((nx, nx1), BF16),
    ]
    messages = [
        vmem(2, 2, ny, nx), vmem(2, ny1, nx), vmem(2, 2, ny1, nx1), vmem(2, 2, ny2, nx2),
        vmem(2, 3, ny1, nx1), vmem(2, 2, ny2, nx2),
    ]
    halos = [vmem(2, ny, nx)] + messages
    sems = [pltpu.SemaphoreType.DMA((3,))] + [pltpu.SemaphoreType.DMA((2,))] * 14

    def run(*refs):
        kernel(size, *refs)

    return pl.pallas_call(
        run,
        out_shape=(
            jax.ShapeDtypeStruct((nz, ny, nx), F32),
            jax.ShapeDtypeStruct((pairs, ny1, nx1), F32),
            jax.ShapeDtypeStruct((pairs // 2, ny2, nx2), F32),
        ),
        in_specs=[pl.BlockSpec(memory_space=pl.ANY)] * 3,
        out_specs=tuple([pl.BlockSpec(memory_space=pltpu.VMEM)] * 3),
        scratch_shapes=slab + padded + faces + sums + work + messages + halos + sems,
        compiler_params=pltpu.CompilerParams(
            collective_id=0, has_side_effects=True, vmem_limit_bytes=48 * 2 ** 20
        ),
    )(pressure_guess, source, conductance)


def solution(mesh):
    size = mesh.shape["gz"]
    spec = P("gz", None, None)
    return jax.shard_map(
        lambda *args: on_device(size, *args), mesh=mesh,
        in_specs=(spec, spec, spec), out_specs=(spec, spec, spec), check_vma=False,
    )
```

```python
import jax
import jax.numpy as jnp
from jax import lax
from jax.experimental import pallas as pl
from jax.experimental.pallas import tpu as pltpu
from jax.sharding import PartitionSpec as P

F32 = jnp.float32
BF16 = jnp.bfloat16


def parity(shape, offset):
    rows = lax.broadcasted_iota(jnp.int32, shape, 0)
    cols = lax.broadcasted_iota(jnp.int32, shape, 1)
    return ((rows + cols + offset) & 1) == 0


def shifts(plane):
    ny, nx = plane.shape
    return (
        pltpu.roll(plane, ny - 1, 0),
        pltpu.roll(plane, 1, 0),
        pltpu.roll(plane, nx - 1, 1),
        pltpu.roll(plane, 1, 1),
    )


def insides(shape):
    rows = lax.broadcasted_iota(jnp.int32, shape, 0)
    cols = lax.broadcasted_iota(jnp.int32, shape, 1)
    return (rows < shape[0] - 1, rows > 0, cols < shape[1] - 1, cols > 0)


def side_faces(centre, other):
    faces, total = [], None
    for near, inside in zip(shifts(other), insides(centre.shape)):
        near = jnp.where(inside, near, 0.0)
        faces.append(jnp.where(inside, centre + near, 0.0))
        total = near if total is None else total + near
    return faces, total


def dot_parts(rows, weights):
    count = rows.shape[0]
    high = rows.astype(BF16)
    rest = rows - high.astype(F32)
    middle = rest.astype(BF16)
    low = (rest - middle.astype(F32)).astype(BF16)
    out = jnp.dot(
        jnp.concatenate([high, middle, low], axis=0), weights, preferred_element_type=F32
    )
    return out[:count] + (out[count : 2 * count] + out[2 * count :])


def weights_of(shape, inner, outer):
    fine = lax.broadcasted_iota(jnp.int32, shape, 0)
    coarse = lax.broadcasted_iota(jnp.int32, shape, 1)
    apart = fine - 2 * coarse
    near = (apart == 0) | (apart == 1)
    far = (apart == -1) | (apart == 2)
    return jnp.where(near, inner, jnp.where(far, outer, 0.0)).astype(BF16)


def kernel(
    size,
    g_hbm, b_hbm, c_hbm,
    p_ref, mid_ref, low_ref,
    craw, graw, braw,
    cr, cb, gb, rr, dl, rho,
    fpair, fro, frs, fbo, fbs,
    dr, db, nr,
    zbuf, zmid, wres, wsum,
    v1, cof1, dia1,
    send_d, send_m, send_q, send_c1, send_c2, send_2, send_3,
    halo_c, halo_d, halo_m, halo_q, halo_c1, halo_c2, halo_2, halo_3,
    load_sem,
    s_c, s_d, s_m, s_q, s_c1, s_c2, s_2, s_3,
    r_c, r_d, r_m, r_q, r_c1, r_c2, r_2, r_3,
):
    me = lax.axis_index("gz")
    nz, ny, nx = craw.shape
    pairs = nz // 2
    plane = (ny, nx)
    plane1 = (ny // 2, nx // 2)
    plane2 = (ny // 4, nx // 4)
    has = (me > 0, me < size - 1)

    loads = [
        pltpu.make_async_copy(src, dst, load_sem.at[i])
        for i, (src, dst) in enumerate(((c_hbm, craw), (g_hbm, graw), (b_hbm, braw)))
    ]
    for load in loads:
        load.start()

    barrier = pltpu.get_barrier_semaphore()
    for side in range(2):
        @pl.when(has[side])
        def _(side=side):
            pl.semaphore_signal(
                barrier, inc=1, device_id=(me + 2 * side - 1,),
                device_id_type=pl.DeviceIdType.MESH,
            )

    for ref in (cr, cb, gb, rr, dl, rho):
        ref[0] = jnp.zeros(plane, F32)
        ref[pairs + 1] = jnp.zeros(plane, F32)
    dl[1] = jnp.zeros(plane, F32)
    dl[pairs] = jnp.zeros(plane, F32)
    for ref, depth in ((zbuf, ny), (zmid, ny // 2)):
        for i in range(ref.shape[0]):
            for j in range(ref.shape[1]):
                ref[i, j, 0:8] = jnp.zeros((8, 128), F32)
                ref[i, j, depth + 8 : depth + 16] = jnp.zeros((8, 128), F32)
    for side in range(2):
        @pl.when(jnp.logical_not(has[side]))
        def _(side=side):
            for ref in (halo_c, halo_d, halo_m, halo_q):
                ref[side] = jnp.zeros(ref.shape[1:], F32)
            for ref in (halo_c1, halo_c2, halo_2, halo_3):
                for i in range(ref.shape[1]):
                    ref[side, i] = jnp.zeros(ref.shape[2:], F32)
    wres[...] = weights_of(wres.shape, 3.0, 1.0)
    wsum[...] = weights_of(wsum.shape, 1.0, 0.0)

    def copy_out(side, src, dst, s_sem, r_sem):
        return pltpu.make_async_remote_copy(
            src_ref=src, dst_ref=dst.at[1 - side], send_sem=s_sem.at[side],
            recv_sem=r_sem.at[1 - side], device_id=(me + 2 * side - 1,),
            device_id_type=pl.DeviceIdType.MESH,
        )

    def send(src_of, dst, s_sem, r_sem):
        for side in range(2):
            @pl.when(has[side])
            def _(side=side):
                copy_out(side, src_of(side), dst, s_sem, r_sem).start()

    def wait_recv(side, present, dst, s_sem, r_sem):
        @pl.when(present)
        def _():
            pltpu.make_async_remote_copy(
                src_ref=dst.at[side], dst_ref=dst.at[side], send_sem=s_sem.at[side],
                recv_sem=r_sem.at[side], device_id=(me + 2 * side - 1,),
                device_id_type=pl.DeviceIdType.MESH,
            ).wait_recv()

    even = parity(plane, 0)

    def even_first(first, second):
        return jnp.where(parity(plane, 0), first, second)

    loads[0].wait()

    def put_rows(ref, k, value):
        for j in range(ref.shape[1]):
            ref[k, j, 8 : value.shape[0] + 8] = value[:, 128 * j : 128 * j + 128]

    def get_rows(ref, k, start, count):
        return jnp.concatenate(
            [ref[k, j, pl.ds(start, count, stride=2), :] for j in range(ref.shape[1])], axis=1
        )

    def pack(k, carry):
        low, high = craw[2 * k], craw[2 * k + 1]
        cr[k + 1] = even_first(low, high)
        cb[k + 1] = even_first(high, low)
        put_rows(zbuf, k, low + high)
        return carry

    lax.fori_loop(0, pairs, pack, 0)
    pl.semaphore_wait(barrier, jnp.where(has[0] & has[1], 2, 1))
    send(lambda side: craw.at[(nz - 1) * side], halo_c, s_c, r_c)

    def faces(k, carry):
        own, other = cr[k + 1], cb[k + 1]
        fpair[k] = own + other
        outer = even_first(cb[k], cb[k + 2])
        sides, total = side_faces(own, other)
        fro[k] = own + outer
        for i in range(4):
            frs[k, i] = sides[i]
        dr[k] = 6.0 * own + other + outer + total
        outer = even_first(cr[k + 2], cr[k])
        sides, total = side_faces(other, own)
        fbo[k] = other + outer
        for i in range(4):
            fbs[k, i] = sides[i]
        db[k] = 6.0 * other + own + outer + total
        return carry

    def gather(k, centre, outer, f_outer, f_sides):
        total = fpair[k] * centre + f_outer[k] * outer
        for i, near in enumerate(shifts(centre)):
            total = total + f_sides[k, i] * near
        return total

    def pack_g(k, carry):
        gb[k + 1] = even_first(graw[2 * k + 1], graw[2 * k])
        return carry

    def red(k, carry):
        rhs = even_first(braw[2 * k], braw[2 * k + 1])
        off = gather(k, gb[k + 1], even_first(gb[k], gb[k + 2]), fro, frs)
        top = 2.0 * rhs + off
        nr[k] = top
        rr[k + 1] = top / dr[k]
        return carry

    def put_diagonal(side, carry):
        k = (pairs - 1) * side
        send_d[side] = jnp.where(parity(plane, side), dr[k], db[k])
        return carry

    def put_field(side, carry):
        k = (pairs - 1) * side
        send_m[side] = jnp.where(parity(plane, side), nr[k], gb[k + 1])
        return carry

    def put_second(side, carry):
        k = (pairs - 1) * side
        rhs = even_first(braw[2 * k + 1], braw[2 * k])
        part = 2.0 * rhs + fpair[k] * rr[k + 1]
        half = ny // 2
        send_q[side] = jnp.where(
            parity((half, nx), side), pltpu.roll(part[half:], 1, 0), part[:half]
        )
        return carry

    def at_ends(body):
        lax.fori_loop(0, 2, lambda i, carry: body((pairs - 1) * i, carry), 0)

    at_ends(faces)
    lax.fori_loop(0, 2, put_diagonal, 0)
    send(lambda side: send_d.at[side], halo_d, s_d, r_d)
    loads[1].wait()
    lax.fori_loop(0, pairs, pack_g, 0)
    loads[2].wait()
    at_ends(red)
    lax.fori_loop(0, 2, put_field, 0)
    send(lambda side: send_m.at[side], halo_m, s_m, r_m)
    lax.fori_loop(0, 2, put_second, 0)
    send(lambda side: send_q.at[side], halo_q, s_q, r_q)

    lax.fori_loop(1, pairs - 1, faces, 0)
    lax.fori_loop(1, pairs - 1, red, 0)

    def put_pressure(k, reds, blacks):
        p_ref[2 * k] = even_first(reds, blacks)
        p_ref[2 * k + 1] = even_first(blacks, reds)

    def black(k, carry):
        rhs = even_first(braw[2 * k + 1], braw[2 * k])
        reds = rr[k + 1]
        off = gather(k, reds, even_first(rr[k + 2], rr[k]), fbo, fbs)
        new = (2.0 * rhs + off) / db[k]
        dl[k + 1] = new - gb[k + 1]
        put_pressure(k, reds, new)
        return carry

    lax.fori_loop(1, pairs - 1, black, 0)

    def residual(k, carry):
        rho[k + 1] = gather(k, dl[k + 1], even_first(dl[k], dl[k + 2]), fro, frs)
        return carry

    lax.fori_loop(1, pairs - 1, residual, 0)

    ny1, ny2 = ny // 2, ny // 4
    rows = [
        get_rows(zbuf, k, 8, ny1) + get_rows(zbuf, k, 9, ny1)
        for k in range(pairs)
    ]
    sums = 0.125 * dot_parts(jnp.concatenate(rows, axis=0), wsum[...])
    c1 = [sums[k * ny1 : (k + 1) * ny1] for k in range(pairs)]

    def plane_sum(value):
        total = None
        for near, inside in zip(shifts(value), insides(value.shape)):
            near = jnp.where(inside, near, 0.0)
            total = near if total is None else total + near
        return total

    def diagonals(coefs):
        out = []
        for k, coef in enumerate(coefs):
            total = 6.0 * coef + plane_sum(coef)
            if k > 0:
                total = total + coefs[k - 1]
            if k < len(coefs) - 1:
                total = total + coefs[k + 1]
            out.append(total)
        return out

    d1 = diagonals(c1)
    for k in range(pairs):
        cof1[k] = c1[k]
        dia1[k] = d1[k]
    for k in range(pairs // 2):
        put_rows(zmid, k, c1[2 * k] + c1[2 * k + 1])
    rows = [
        get_rows(zmid, k, 8, ny2) + get_rows(zmid, k, 9, ny2)
        for k in range(pairs // 2)
    ]
    weights = wsum[0 : nx // 2, 0 : nx // 4]
    sums = 0.125 * dot_parts(jnp.concatenate(rows, axis=0), weights)
    c2 = [sums[k * ny2 : (k + 1) * ny2] for k in range(pairs // 2)]
    d2 = diagonals(c2)
    for side in range(2):
        send_c1[side, 0] = c1[-side]
        send_c1[side, 1] = d1[-side]
        send_c2[side, 0] = c2[-side]
        send_c2[side, 1] = d2[-side]
    send(lambda side: send_c1.at[side], halo_c1, s_c1, r_c1)
    send(lambda side: send_c2.at[side], halo_c2, s_c2, r_c2)

    def restrict(ref, count, out_rows, weights, scale):
        rows = [
            (get_rows(ref, k, 7, out_rows) + get_rows(ref, k, 10, out_rows))
            + 3.0 * (get_rows(ref, k, 8, out_rows) + get_rows(ref, k, 9, out_rows))
            for k in range(count)
        ]
        out = scale * dot_parts(jnp.concatenate(rows, axis=0), weights)
        return [out[k * out_rows : (k + 1) * out_rows] for k in range(count)]

    def finish(step, carry):
        side = (step + 1 + me) % 2
        present = jnp.where(side == 0, me, size - 1 - me) > 0
        wait_recv(side, present, halo_c, s_c, r_c)
        wait_recv(side, present, halo_d, s_d, r_d)
        wait_recv(side, present, halo_m, s_m, r_m)
        wait_recv(side, present, halo_q, s_q, r_q)
        k = (pairs - 1) * side
        here = (nz - 1) * side
        mine = parity(plane, side)
        inside = jnp.where(present, 1.0, 0.0)
        hc, hd, hm = halo_c[side], halo_d[side], halo_m[side]
        c0, g0 = craw[here], graw[here]
        face = c0 + hc
        top = jnp.where(mine, nr[k], hm) + face * jnp.where(mine, hm, g0)
        value = top / jnp.where(mine, dr[k] + hc, hd + c0)
        value = jnp.where(mine, value, inside * value)
        reds = jnp.where(mine, value, rr[k + 1])
        rr[k + 1] = reds
        hq = halo_q[side]
        off = jnp.concatenate([hq, pltpu.roll(hq, ny // 2 - 1, 0)], axis=0)
        off = off + face * value
        sides, _ = side_faces(hc, hc)
        for f, near in zip(sides, shifts(value)):
            off = off + f * near
        halo_delta = inside * (off / (hd + c0) - hm)

        rhs = even_first(braw[2 * k + 1], braw[2 * k])
        off = gather(k, reds, even_first(rr[k + 2], rr[k]), fbo, fbs)
        off = off + jnp.where(mine, 0.0, face * value)
        new = (2.0 * rhs + off) / (db[k] + jnp.where(mine, 0.0, hc))
        delta = new - gb[k + 1]
        dl[k + 1] = delta
        put_pressure(k, reds, new)

        off = gather(k, delta, even_first(dl[k], dl[k + 2]), fro, frs)
        rho[k + 1] = off + jnp.where(mine, face * halo_delta, 0.0)
        inner = k + 1 - 2 * side
        more = (cr[inner + 1] + cb[k + 1]) * delta
        rho[inner + 1] = rho[inner + 1] + jnp.where(mine, more, 0.0)

        for i, at in enumerate((k, inner)):
            put_rows(zbuf, i, 3.0 * rho[at + 1] + even_first(rho[at + 2], rho[at]))
        put_rows(zbuf, 2, jnp.where(mine, rho[k + 1], 0.0))
        parts = restrict(zbuf, 3, ny1, wres[...], 0.5 ** 10)
        for i in range(3):
            v1[side, i] = parts[i]
        send_2[side, 0] = parts[0]
        send_2[side, 1] = parts[2]
        send_2[side, 2] = (cof1[k] + cof1[inner]) * (8.0 * parts[1] / dia1[inner])

        @pl.when(present)
        def _():
            copy_out(side, send_2.at[side], halo_2, s_2, r_2).start()

        return carry

    lax.fori_loop(0, 2, finish, 0)

    rhs1 = [v1[0, 0], v1[0, 1], v1[1, 1], v1[1, 0]]
    edge1 = [v1[0, 2], v1[1, 2]]
    for side in range(2):
        wait_recv(side, has[side], halo_c1, s_c1, r_c1)
        wait_recv(side, has[side], halo_c2, s_c2, r_c2)
        wait_recv(side, has[side], halo_2, s_2, r_2)
    inside = [jnp.where(has[side], 1.0, 0.0) for side in range(2)]

    def with_ends(own, low, high):
        return [low] + list(own) + [high]

    def red_black(rhs, coefs, diags, seconds, factor, depth):
        masks = [parity(rhs[0].shape, i - 1) for i in range(depth + 2)]
        reds = []
        for i in range(depth + 2):
            value = jnp.where(masks[i], factor * rhs[i] / diags[i], 0.0)
            if i == 0:
                value = inside[0] * value
            if i == depth + 1:
                value = inside[1] * value
            reds.append(value)
        return masks, reds

    def off_of(coefs, fields, i):
        around = plane_sum(fields[i])
        weighted = plane_sum(coefs[i] * fields[i])
        for j in (i - 1, i + 1):
            if 0 <= j < len(fields):
                around = around + fields[j]
                weighted = weighted + coefs[j] * fields[j]
        return coefs[i] * around + weighted

    ends = [halo_2[0, 0] + edge1[0], halo_2[1, 0] + edge1[1]]
    rhs1[0] = rhs1[0] + halo_2[0, 1]
    rhs1[-1] = rhs1[-1] + halo_2[1, 1]
    d1 = with_ends(d1, halo_c1[0, 1] + c1[0], halo_c1[1, 1] + c1[-1])
    d1[1] = d1[1] + halo_c1[0, 0]
    d1[-2] = d1[-2] + halo_c1[1, 0]
    c1 = with_ends(c1, halo_c1[0, 0], halo_c1[1, 0])
    rhs1 = with_ends(rhs1, ends[0], ends[1])
    masks, reds = red_black(rhs1, c1, d1, None, 8.0, pairs)
    blacks = []
    for i in range(pairs + 2):
        top = 8.0 * rhs1[i] + off_of(c1, reds, i)
        if i == 0:
            top = inside[0] * (top + halo_2[0, 2])
        if i == pairs + 1:
            top = inside[1] * (top + halo_2[1, 2])
        blacks.append(jnp.where(masks[i], 0.0, top / d1[i]))
    for i in range(1, pairs + 1):
        mid_ref[i - 1] = reds[i] + blacks[i]
    res = [
        jnp.where(masks[i], off_of(c1, blacks, i), 0.0) for i in range(1, pairs + 1)
    ]

    put_rows(zmid, 0, 3.0 * (res[0] + res[1]) + res[2])
    put_rows(zmid, 1, 3.0 * (res[2] + res[3]) + res[1])
    put_rows(zmid, 2, res[0])
    put_rows(zmid, 3, res[3])
    parts = restrict(zmid, 4, ny2, wres[0 : nx // 2, 0 : nx // 4], 0.5 ** 12)
    rhs2, edge2 = parts[:2], parts[2:]
    for side in range(2):
        send_3[side, 0] = rhs2[side]
        send_3[side, 1] = edge2[side]
    send(lambda side: send_3.at[side], halo_3, s_3, r_3)
    for side in range(2):
        wait_recv(side, has[side], halo_3, s_3, r_3)
    ends = [halo_3[side, 0] + edge2[side] for side in range(2)]
    rhs2 = [rhs2[side] + halo_3[side, 1] for side in range(2)]
    d2 = with_ends(d2, halo_c2[0, 1] + c2[0], halo_c2[1, 1] + c2[1])
    d2[1] = d2[1] + halo_c2[0, 0]
    d2[2] = d2[2] + halo_c2[1, 0]
    c2 = with_ends(c2, halo_c2[0, 0], halo_c2[1, 0])
    rhs2 = with_ends(rhs2, ends[0], ends[1])
    masks, reds = red_black(rhs2, c2, d2, None, 32.0, 2)
    for i in (1, 2):
        top = 32.0 * rhs2[i] + off_of(c2, reds, i)
        low_ref[i - 1] = jnp.where(masks[i], reds[i], top / d2[i])

    for side in range(2):
        @pl.when(has[side])
        def _(side=side):
            for src, dst, s_sem, r_sem in (
                (craw.at[(nz - 1) * side], halo_c, s_c, r_c),
                (send_d.at[side], halo_d, s_d, r_d),
                (send_m.at[side], halo_m, s_m, r_m),
                (send_q.at[side], halo_q, s_q, r_q),
                (send_c1.at[side], halo_c1, s_c1, r_c1),
                (send_c2.at[side], halo_c2, s_c2, r_c2),
                (send_2.at[side], halo_2, s_2, r_2),
                (send_3.at[side], halo_3, s_3, r_3),
            ):
                copy_out(side, src, dst, s_sem, r_sem).wait_send()


def on_device(size, pressure_guess, source, conductance):
    nz, ny, nx = pressure_guess.shape
    pairs = nz // 2
    ny1, nx1, ny2, nx2 = ny // 2, nx // 2, ny // 4, nx // 4

    def vmem(*shape):
        return pltpu.VMEM(shape, F32)

    slab = [vmem(nz, ny, nx)] * 3
    padded = [vmem(pairs + 2, ny, nx)] * 6
    faces = [
        vmem(pairs, ny, nx), vmem(pairs, ny, nx), vmem(pairs, 4, ny, nx),
        vmem(pairs, ny, nx), vmem(pairs, 4, ny, nx),
    ]
    sums = [vmem(pairs, ny, nx)] * 3
    work = [
        vmem(pairs + 2, nx // 128, ny + 16, 128), vmem(4, nx1 // 128, ny1 + 16, 128),
        pltpu.VMEM((nx, nx1), BF16), pltpu.VMEM((nx, nx1), BF16),
        vmem(2, 3, ny1, nx1), vmem(pairs, ny1, nx1), vmem(pairs, ny1, nx1),
    ]
    messages = [
        vmem(2, ny, nx), vmem(2, ny, nx), vmem(2, ny1, nx), vmem(2, 2, ny1, nx1), vmem(2, 2, ny2, nx2),
        vmem(2, 3, ny1, nx1), vmem(2, 2, ny2, nx2),
    ]
    halos = [vmem(2, ny, nx)] + messages
    sems = [pltpu.SemaphoreType.DMA((3,))] + [pltpu.SemaphoreType.DMA((2,))] * 16

    def run(*refs):
        kernel(size, *refs)

    shapes = ((nz, ny, nx), (pairs, ny1, nx1), (pairs // 2, ny2, nx2))
    inputs = [
        pltpu.with_memory_space_constraint(value, pltpu.HBM)
        for value in (pressure_guess, source, conductance)
    ]
    results = pl.pallas_call(
        run,
        out_shape=tuple(pltpu.VMEM(shape, F32) for shape in shapes),
        in_specs=[pl.BlockSpec(memory_space=pl.ANY)] * 3,
        out_specs=tuple([pl.BlockSpec(memory_space=pltpu.VMEM)] * 3),
        scratch_shapes=slab + padded + faces + sums + work + messages + halos + sems,
        compiler_params=pltpu.CompilerParams(
            collective_id=0, has_side_effects=True, vmem_limit_bytes=48 * 2 ** 20
        ),
    )(*inputs)
    return pl.pallas_call(
        write_out,
        out_shape=tuple(jax.ShapeDtypeStruct(shape, F32) for shape in shapes),
        in_specs=[pl.BlockSpec(memory_space=pl.ANY)] * 3,
        out_specs=tuple([pl.BlockSpec(memory_space=pl.ANY)] * 3),
        scratch_shapes=[pltpu.SemaphoreType.DMA((3,))],
    )(*[pltpu.with_memory_space_constraint(value, pltpu.VMEM) for value in results])


def write_out(p_src, mid_src, low_src, p_dst, mid_dst, low_dst, sem):
    copies = [
        pltpu.make_async_copy(src, dst, sem.at[i])
        for i, (src, dst) in enumerate(((p_src, p_dst), (mid_src, mid_dst), (low_src, low_dst)))
    ]
    for copy in copies:
        copy.start()
    for copy in copies:
        copy.wait()


def solution(mesh):
    size = mesh.shape["gz"]
    spec = P("gz", None, None)
    return jax.shard_map(
        lambda *args: on_device(size, *args), mesh=mesh,
        in_specs=(spec, spec, spec), out_specs=(spec, spec, spec), check_vma=False,
    )
```

```python
import jax
import jax.numpy as jnp
from jax import lax
from jax.experimental import pallas as pl
from jax.experimental.pallas import tpu as pltpu
from jax.sharding import PartitionSpec as P

F32 = jnp.float32
BF16 = jnp.bfloat16


def parity(shape, offset):
    rows = lax.broadcasted_iota(jnp.int32, shape, 0)
    cols = lax.broadcasted_iota(jnp.int32, shape, 1)
    return ((rows + cols + offset) & 1) == 0


def shifts(plane):
    ny, nx = plane.shape
    return (
        pltpu.roll(plane, ny - 1, 0),
        pltpu.roll(plane, 1, 0),
        pltpu.roll(plane, nx - 1, 1),
        pltpu.roll(plane, 1, 1),
    )


def insides(shape):
    rows = lax.broadcasted_iota(jnp.int32, shape, 0)
    cols = lax.broadcasted_iota(jnp.int32, shape, 1)
    return (rows < shape[0] - 1, rows > 0, cols < shape[1] - 1, cols > 0)


def side_faces(centre, other):
    faces, total = [], None
    for near, inside in zip(shifts(other), insides(centre.shape)):
        near = jnp.where(inside, near, 0.0)
        faces.append(jnp.where(inside, centre + near, 0.0))
        total = near if total is None else total + near
    return faces, total


def dot_parts(rows, weights):
    count = rows.shape[0]
    high = rows.astype(BF16)
    rest = rows - high.astype(F32)
    middle = rest.astype(BF16)
    low = (rest - middle.astype(F32)).astype(BF16)
    out = jnp.dot(
        jnp.concatenate([high, middle, low], axis=0), weights, preferred_element_type=F32
    )
    return out[:count] + (out[count : 2 * count] + out[2 * count :])


def weights_of(shape, inner, outer):
    fine = lax.broadcasted_iota(jnp.int32, shape, 0)
    coarse = lax.broadcasted_iota(jnp.int32, shape, 1)
    apart = fine - 2 * coarse
    near = (apart == 0) | (apart == 1)
    far = (apart == -1) | (apart == 2)
    return jnp.where(near, inner, jnp.where(far, outer, 0.0)).astype(BF16)


def kernel(
    size,
    g_hbm, b_hbm, c_hbm,
    p_ref, mid_ref, low_ref,
    craw, graw, braw,
    cr, cb, gb, rr, dl, rho,
    fpair, fro, frs, fbo, fbs,
    dr, db, nr,
    zbuf, zmid, wres, wsum,
    v1, cof1, dia1,
    cof2, dia2,
    send_d, send_m, send_q, send_c1, send_c2, send_2, send_3,
    halo_c, halo_d, halo_m, halo_q, halo_c1, halo_c2, halo_2, halo_n, halo_f, halo_3,
    load_sem,
    s_c, s_d, s_m, s_q, s_c1, s_c2, s_2, s_n, s_f, s_3,
    r_c, r_d, r_m, r_q, r_c1, r_c2, r_2, r_n, r_f, r_3,
):
    me = lax.axis_index("gz")
    nz, ny, nx = craw.shape
    pairs = nz // 2
    plane = (ny, nx)
    plane1 = (ny // 2, nx // 2)
    plane2 = (ny // 4, nx // 4)
    has = (me > 0, me < size - 1)
    far = me % 2
    near = 1 - far
    has_far = jnp.where(far == 0, me, size - 1 - me) > 0

    loads = [
        pltpu.make_async_copy(src, dst, load_sem.at[i])
        for i, (src, dst) in enumerate(((c_hbm, craw), (g_hbm, graw), (b_hbm, braw)))
    ]
    for load in loads:
        load.start()

    barrier = pltpu.get_barrier_semaphore()
    for side in range(2):
        @pl.when(has[side])
        def _(side=side):
            pl.semaphore_signal(
                barrier, inc=1, device_id=(me + 2 * side - 1,),
                device_id_type=pl.DeviceIdType.MESH,
            )

    for ref in (cr, cb, gb, rr, dl, rho):
        ref[0] = jnp.zeros(plane, F32)
        ref[pairs + 1] = jnp.zeros(plane, F32)
    dl[1] = jnp.zeros(plane, F32)
    dl[pairs] = jnp.zeros(plane, F32)
    for ref, depth in ((zbuf, ny), (zmid, ny // 2)):
        for i in range(ref.shape[0]):
            for j in range(ref.shape[1]):
                ref[i, j, 0:8] = jnp.zeros((8, 128), F32)
                ref[i, j, depth + 8 : depth + 16] = jnp.zeros((8, 128), F32)
    for side in range(2):
        @pl.when(jnp.logical_not(has[side]))
        def _(side=side):
            for ref in (halo_c, halo_d, halo_m, halo_q):
                ref[side] = jnp.zeros(ref.shape[1:], F32)
            for ref in (halo_c1, halo_c2, halo_2, halo_f):
                for i in range(ref.shape[1]):
                    ref[side, i] = jnp.zeros(ref.shape[2:], F32)
    wres[...] = weights_of(wres.shape, 3.0, 1.0)
    wsum[...] = weights_of(wsum.shape, 1.0, 0.0)

    def copy_out(side, src, dst, s_sem, r_sem):
        return pltpu.make_async_remote_copy(
            src_ref=src, dst_ref=dst.at[1 - side], send_sem=s_sem.at[side],
            recv_sem=r_sem.at[1 - side], device_id=(me + 2 * side - 1,),
            device_id_type=pl.DeviceIdType.MESH,
        )

    def send(src_of, dst, s_sem, r_sem):
        for side in range(2):
            @pl.when(has[side])
            def _(side=side):
                copy_out(side, src_of(side), dst, s_sem, r_sem).start()

    def wait_recv(side, present, dst, s_sem, r_sem):
        @pl.when(present)
        def _():
            pltpu.make_async_remote_copy(
                src_ref=dst.at[side], dst_ref=dst.at[side], send_sem=s_sem.at[side],
                recv_sem=r_sem.at[side], device_id=(me + 2 * side - 1,),
                device_id_type=pl.DeviceIdType.MESH,
            ).wait_recv()

    even = parity(plane, 0)

    def even_first(first, second):
        return jnp.where(parity(plane, 0), first, second)

    loads[0].wait()

    def put_rows(ref, k, value):
        for j in range(ref.shape[1]):
            ref[k, j, 8 : value.shape[0] + 8] = value[:, 128 * j : 128 * j + 128]

    def get_rows(ref, k, start, count):
        return jnp.concatenate(
            [ref[k, j, pl.ds(start, count, stride=2), :] for j in range(ref.shape[1])], axis=1
        )

    def pack(k, carry):
        low, high = craw[2 * k], craw[2 * k + 1]
        cr[k + 1] = even_first(low, high)
        cb[k + 1] = even_first(high, low)
        put_rows(zbuf, k, low + high)
        return carry

    lax.fori_loop(0, pairs, pack, 0)
    pl.semaphore_wait(barrier, jnp.where(has[0] & has[1], 2, 1))
    send(lambda side: craw.at[(nz - 1) * side], halo_c, s_c, r_c)

    def faces(k, carry):
        own, other = cr[k + 1], cb[k + 1]
        fpair[k] = own + other
        outer = even_first(cb[k], cb[k + 2])
        sides, total = side_faces(own, other)
        fro[k] = own + outer
        for i in range(4):
            frs[k, i] = sides[i]
        dr[k] = 6.0 * own + other + outer + total
        outer = even_first(cr[k + 2], cr[k])
        sides, total = side_faces(other, own)
        fbo[k] = other + outer
        for i in range(4):
            fbs[k, i] = sides[i]
        db[k] = 6.0 * other + own + outer + total
        return carry

    def gather(k, centre, outer, f_outer, f_sides):
        total = fpair[k] * centre + f_outer[k] * outer
        for i, near in enumerate(shifts(centre)):
            total = total + f_sides[k, i] * near
        return total

    def pack_g(k, carry):
        gb[k + 1] = even_first(graw[2 * k + 1], graw[2 * k])
        return carry

    def red(k, carry):
        rhs = even_first(braw[2 * k], braw[2 * k + 1])
        off = gather(k, gb[k + 1], even_first(gb[k], gb[k + 2]), fro, frs)
        top = 2.0 * rhs + off
        nr[k] = top
        rr[k + 1] = top / dr[k]
        return carry

    def put_diagonal(side, carry):
        k = (pairs - 1) * side
        send_d[side] = jnp.where(parity(plane, side), dr[k], db[k])
        return carry

    def put_field(side, carry):
        k = (pairs - 1) * side
        send_m[side] = jnp.where(parity(plane, side), nr[k], gb[k + 1])
        return carry

    def put_second(side, carry):
        k = (pairs - 1) * side
        rhs = even_first(braw[2 * k + 1], braw[2 * k])
        part = 2.0 * rhs + fpair[k] * rr[k + 1]
        half = ny // 2
        send_q[side] = jnp.where(
            parity((half, nx), side), pltpu.roll(part[half:], 1, 0), part[:half]
        )
        return carry

    def at_ends(body):
        lax.fori_loop(0, 2, lambda i, carry: body((pairs - 1) * i, carry), 0)

    at_ends(faces)
    lax.fori_loop(0, 2, put_diagonal, 0)
    send(lambda side: send_d.at[side], halo_d, s_d, r_d)
    loads[1].wait()
    lax.fori_loop(0, pairs, pack_g, 0)
    loads[2].wait()
    at_ends(red)
    lax.fori_loop(0, 2, put_field, 0)
    send(lambda side: send_m.at[side], halo_m, s_m, r_m)
    lax.fori_loop(0, 2, put_second, 0)
    send(lambda side: send_q.at[side], halo_q, s_q, r_q)

    lax.fori_loop(1, pairs - 1, faces, 0)
    lax.fori_loop(1, pairs - 1, red, 0)

    def put_pressure(k, reds, blacks):
        p_ref[2 * k] = even_first(reds, blacks)
        p_ref[2 * k + 1] = even_first(blacks, reds)

    def black(k, carry):
        rhs = even_first(braw[2 * k + 1], braw[2 * k])
        reds = rr[k + 1]
        off = gather(k, reds, even_first(rr[k + 2], rr[k]), fbo, fbs)
        new = (2.0 * rhs + off) / db[k]
        dl[k + 1] = new - gb[k + 1]
        put_pressure(k, reds, new)
        return carry

    lax.fori_loop(1, pairs - 1, black, 0)

    def residual(k, carry):
        rho[k + 1] = gather(k, dl[k + 1], even_first(dl[k], dl[k + 2]), fro, frs)
        return carry

    lax.fori_loop(1, pairs - 1, residual, 0)

    ny1, ny2 = ny // 2, ny // 4
    rows = [
        get_rows(zbuf, k, 8, ny1) + get_rows(zbuf, k, 9, ny1)
        for k in range(pairs)
    ]
    sums = 0.125 * dot_parts(jnp.concatenate(rows, axis=0), wsum[...])
    c1 = [sums[k * ny1 : (k + 1) * ny1] for k in range(pairs)]

    def plane_sum(value):
        total = None
        for near, inside in zip(shifts(value), insides(value.shape)):
            near = jnp.where(inside, near, 0.0)
            total = near if total is None else total + near
        return total

    def diagonals(coefs):
        out = []
        for k, coef in enumerate(coefs):
            total = 6.0 * coef + plane_sum(coef)
            if k > 0:
                total = total + coefs[k - 1]
            if k < len(coefs) - 1:
                total = total + coefs[k + 1]
            out.append(total)
        return out

    d1 = diagonals(c1)
    for k in range(pairs):
        cof1[k] = c1[k]
        dia1[k] = d1[k]
    for k in range(pairs // 2):
        put_rows(zmid, k, c1[2 * k] + c1[2 * k + 1])
    rows = [
        get_rows(zmid, k, 8, ny2) + get_rows(zmid, k, 9, ny2)
        for k in range(pairs // 2)
    ]
    weights = wsum[0 : nx // 2, 0 : nx // 4]
    sums = 0.125 * dot_parts(jnp.concatenate(rows, axis=0), weights)
    c2 = [sums[k * ny2 : (k + 1) * ny2] for k in range(pairs // 2)]
    d2 = diagonals(c2)
    for k in range(2):
        cof2[k] = c2[k]
        dia2[k] = d2[k]
    for side in range(2):
        ends = (3 * side, 1 + side, 2 - side)
        for i, value in enumerate((c1[ends[0]], d1[ends[0]], c1[ends[1]], d1[ends[1]], c1[ends[2]])):
            send_c1[side, i] = value
        send_c2[side, 0] = c2[side]
        send_c2[side, 1] = d2[side]
    send(lambda side: send_c1.at[side], halo_c1, s_c1, r_c1)
    send(lambda side: send_c2.at[side], halo_c2, s_c2, r_c2)

    def restrict(ref, count, out_rows, weights, scale):
        rows = [
            (get_rows(ref, k, 7, out_rows) + get_rows(ref, k, 10, out_rows))
            + 3.0 * (get_rows(ref, k, 8, out_rows) + get_rows(ref, k, 9, out_rows))
            for k in range(count)
        ]
        out = scale * dot_parts(jnp.concatenate(rows, axis=0), weights)
        return [out[k * out_rows : (k + 1) * out_rows] for k in range(count)]

    def finish(step, carry):
        side = jnp.where(step == 0, near, far)
        present = (step == 0) | has_far
        wait_recv(side, present, halo_c, s_c, r_c)
        wait_recv(side, present, halo_d, s_d, r_d)
        wait_recv(side, present, halo_m, s_m, r_m)
        wait_recv(side, present, halo_q, s_q, r_q)
        k = (pairs - 1) * side
        here = (nz - 1) * side
        mine = parity(plane, side)
        inside = jnp.where(present, 1.0, 0.0)
        hc, hd, hm = halo_c[side], halo_d[side], halo_m[side]
        c0, g0 = craw[here], graw[here]
        face = c0 + hc
        top = jnp.where(mine, nr[k], hm) + face * jnp.where(mine, hm, g0)
        value = top / jnp.where(mine, dr[k] + hc, hd + c0)
        value = jnp.where(mine, value, inside * value)
        reds = jnp.where(mine, value, rr[k + 1])
        rr[k + 1] = reds
        hq = halo_q[side]
        off = jnp.concatenate([hq, pltpu.roll(hq, ny // 2 - 1, 0)], axis=0)
        off = off + face * value
        sides, _ = side_faces(hc, hc)
        for f, shifted in zip(sides, shifts(value)):
            off = off + f * shifted
        halo_delta = inside * (off / (hd + c0) - hm)

        rhs = even_first(braw[2 * k + 1], braw[2 * k])
        off = gather(k, reds, even_first(rr[k + 2], rr[k]), fbo, fbs)
        off = off + jnp.where(mine, 0.0, face * value)
        new = (2.0 * rhs + off) / (db[k] + jnp.where(mine, 0.0, hc))
        delta = new - gb[k + 1]
        dl[k + 1] = delta
        put_pressure(k, reds, new)

        off = gather(k, delta, even_first(dl[k], dl[k + 2]), fro, frs)
        rho[k + 1] = off + jnp.where(mine, face * halo_delta, 0.0)
        inner = k + 1 - 2 * side
        more = (cr[inner + 1] + cb[k + 1]) * delta
        rho[inner + 1] = rho[inner + 1] + jnp.where(mine, more, 0.0)

        for i, at in enumerate((k, inner)):
            put_rows(zbuf, i, 3.0 * rho[at + 1] + even_first(rho[at + 2], rho[at]))
        put_rows(zbuf, 2, jnp.where(mine, rho[k + 1], 0.0))
        parts = restrict(zbuf, 3, ny1, wres[...], 0.5 ** 10)
        for i in range(3):
            v1[side, i] = parts[i]
        send_2[side, 0] = parts[0]
        send_2[side, 1] = parts[2]
        send_2[side, 2] = (cof1[k] + cof1[inner]) * (8.0 * parts[1] / dia1[inner])

        @pl.when(present)
        def _():
            copy_out(side, send_2.at[side, 0:2], halo_2, s_2, r_2).start()

        @pl.when(step == 0)
        def _():
            copy_out(side, send_2.at[side, 2], halo_n, s_n, r_n).start()

        return carry

    lax.fori_loop(0, 2, finish, 0)

    def mask1(j):
        return parity(plane1, j + far + 4)

    def at1(j):
        return 3 * far + j * (1 - 2 * far)

    inside = jnp.where(has_far, 1.0, 0.0)
    true = me >= 0
    cof = {j: cof1[at1(j)] for j in range(4)}
    dia = {j: dia1[at1(j)] for j in range(4)}

    def flat(j, field):
        return cof[j] * plane_sum(field) + plane_sum(cof[j] * field)

    def across(i, j, field):
        return (cof[i] + cof[j]) * field

    def red_of(j, right):
        return jnp.where(mask1(j), 8.0 * right / dia[j], 0.0)

    def black_of(j, top):
        return jnp.where(mask1(j), 0.0, top / dia[j])

    wait_recv(near, true, halo_c1, s_c1, r_c1)
    wait_recv(near, true, halo_2, s_2, r_2)
    wait_recv(near, true, halo_n, s_n, r_n)
    cof[4] = halo_c1[near, 0]
    dia[4] = halo_c1[near, 1] + cof[3]
    dia[3] = dia[3] + cof[4]
    rhs = {
        4: halo_2[near, 0] + v1[near, 2],
        3: v1[near, 0] + halo_2[near, 1],
        2: v1[near, 1],
        1: v1[far, 1],
    }
    red = {j: red_of(j, rhs[j]) for j in (1, 2, 3, 4)}
    black = {}
    black[4] = black_of(4, 8.0 * rhs[4] + halo_n[near] + flat(4, red[4]) + across(4, 3, red[3]))
    for j in (3, 2):
        black[j] = black_of(
            j, 8.0 * rhs[j] + flat(j, red[j]) + across(j, j + 1, red[j + 1]) + across(j, j - 1, red[j - 1])
        )
    part1 = 8.0 * rhs[1] + flat(1, red[1]) + across(1, 2, red[2])
    part2 = flat(2, black[2]) + across(2, 3, black[3])
    cross = across(1, 2, black[2])
    send_2[far, 2] = jnp.where(mask1(0), part2, across(0, 1, red[1]))
    send_2[far, 3] = jnp.where(mask1(1), cross, part1)

    @pl.when(has_far)
    def _():
        copy_out(far, send_2.at[far, 2:4], halo_f, s_f, r_f).start()

    wait_recv(far, has_far, halo_c1, s_c1, r_c1)
    cof.update({-1: halo_c1[far, 0], -2: halo_c1[far, 2], -3: halo_c1[far, 4]})
    dia.update({-1: halo_c1[far, 1] + cof[0], -2: halo_c1[far, 3], 0: dia[0] + cof[-1]})
    wait_recv(far, has_far, halo_2, s_2, r_2)
    rhs[0] = v1[far, 0] + halo_2[far, 1]
    rhs[-1] = halo_2[far, 0] + v1[far, 2]
    red[0] = red_of(0, rhs[0])
    red[-1] = inside * red_of(-1, rhs[-1])
    black[0] = black_of(0, 8.0 * rhs[0] + flat(0, red[0]) + across(0, -1, red[-1]) + across(0, 1, red[1]))
    black[1] = black_of(1, part1 + across(1, 0, red[0]))
    wait_recv(far, has_far, halo_f, s_f, r_f)
    black[-1] = inside * black_of(-1, 8.0 * rhs[-1] + halo_f[far, 0] + flat(-1, red[-1]) + across(-1, 0, red[0]))
    black[-2] = inside * black_of(-2, halo_f[far, 1] + across(-2, -1, red[-1]))
    res = {
        3: flat(3, black[3]) + across(3, 2, black[2]) + across(3, 4, black[4]),
        2: part2 + across(2, 1, black[1]),
        1: flat(1, black[1]) + across(1, 0, black[0]) + cross,
        0: flat(0, black[0]) + across(0, -1, black[-1]) + across(0, 1, black[1]),
        -1: flat(-1, black[-1]) + across(-1, -2, black[-2]) + across(-1, 0, black[0]),
        -2: halo_f[far, 1] + flat(-2, black[-2]) + across(-2, -1, black[-1]),
        -3: halo_f[far, 0] + across(-3, -2, black[-2]),
    }
    res = {
        j: jnp.where(mask1(j) if j >= 0 else mask1(j) & has_far, value, 0.0)
        for j, value in res.items()
    }

    put_rows(zmid, 0, 3.0 * (res[3] + res[2]) + res[1])
    put_rows(zmid, 1, res[3])
    put_rows(zmid, 2, 3.0 * (res[0] + res[1]) + (res[-1] + res[2]))
    put_rows(zmid, 3, 3.0 * (res[-1] + res[-2]) + (res[0] + res[-3]))
    parts = restrict(zmid, 4, ny2, wres[0 : nx // 2, 0 : nx // 4], 0.5 ** 12)
    send_3[0] = parts[0]
    send_3[1] = parts[1]
    copy_out(near, send_3, halo_3, s_3, r_3).start()
    for j in range(4):
        mid_ref[at1(j)] = red[j] + black[j]

    wait_recv(near, true, halo_c2, s_c2, r_c2)
    wait_recv(far, has_far, halo_c2, s_c2, r_c2)
    wait_recv(near, true, halo_3, s_3, r_3)

    def mask2(j):
        return parity(plane2, j + far + 4)

    def at2(j):
        return far + j * (1 - 2 * far)

    cof = {-1: halo_c2[far, 0], 0: cof2[at2(0)], 1: cof2[at2(1)], 2: halo_c2[near, 0]}
    dia = {
        -1: halo_c2[far, 1] + cof[0], 0: dia2[at2(0)] + cof[-1],
        1: dia2[at2(1)] + cof[2], 2: halo_c2[near, 1] + cof[1],
    }
    rhs = {
        -1: parts[3], 0: parts[2], 1: parts[0] + halo_3[near, 1], 2: halo_3[near, 0] + parts[1],
    }
    red = {j: jnp.where(mask2(j), 32.0 * rhs[j] / dia[j], 0.0) for j in rhs}
    red[-1] = inside * red[-1]
    for j in (0, 1):
        top = 32.0 * rhs[j] + flat(j, red[j]) + across(j, j - 1, red[j - 1]) + across(j, j + 1, red[j + 1])
        low_ref[at2(j)] = jnp.where(mask2(j), red[j], top / dia[j])

    def wait_sent(side, present, messages):
        @pl.when(present)
        def _():
            for src, dst, s_sem, r_sem in messages:
                copy_out(side, src, dst, s_sem, r_sem).wait_send()

    for side in range(2):
        wait_sent(side, has[side], (
            (craw.at[(nz - 1) * side], halo_c, s_c, r_c),
            (send_d.at[side], halo_d, s_d, r_d),
            (send_m.at[side], halo_m, s_m, r_m),
            (send_q.at[side], halo_q, s_q, r_q),
            (send_c1.at[side], halo_c1, s_c1, r_c1),
            (send_c2.at[side], halo_c2, s_c2, r_c2),
            (send_2.at[side, 0:2], halo_2, s_2, r_2),
        ))
    wait_sent(near, true, (
        (send_2.at[near, 2], halo_n, s_n, r_n), (send_3, halo_3, s_3, r_3),
    ))
    wait_sent(far, has_far, ((send_2.at[far, 2:4], halo_f, s_f, r_f),))


def on_device(size, pressure_guess, source, conductance):
    nz, ny, nx = pressure_guess.shape
    pairs = nz // 2
    ny1, nx1, ny2, nx2 = ny // 2, nx // 2, ny // 4, nx // 4

    def vmem(*shape):
        return pltpu.VMEM(shape, F32)

    slab = [vmem(nz, ny, nx)] * 3
    padded = [vmem(pairs + 2, ny, nx)] * 6
    faces = [
        vmem(pairs, ny, nx), vmem(pairs, ny, nx), vmem(pairs, 4, ny, nx),
        vmem(pairs, ny, nx), vmem(pairs, 4, ny, nx),
    ]
    sums = [vmem(pairs, ny, nx)] * 3
    work = [
        vmem(pairs + 2, nx // 128, ny + 16, 128), vmem(4, nx1 // 128, ny1 + 16, 128),
        pltpu.VMEM((nx, nx1), BF16), pltpu.VMEM((nx, nx1), BF16),
        vmem(2, 3, ny1, nx1), vmem(pairs, ny1, nx1), vmem(pairs, ny1, nx1),
        vmem(2, ny2, nx2), vmem(2, ny2, nx2),
    ]
    messages = [
        vmem(2, ny, nx), vmem(2, ny, nx), vmem(2, ny1, nx), vmem(2, 5, ny1, nx1), vmem(2, 2, ny2, nx2),
    ]
    sent = messages + [vmem(2, 4, ny1, nx1), vmem(2, ny2, nx2)]
    halos = [vmem(2, ny, nx)] + messages + [
        vmem(2, 2, ny1, nx1), vmem(2, ny1, nx1), vmem(2, 2, ny1, nx1), vmem(2, 2, ny2, nx2),
    ]
    sems = [pltpu.SemaphoreType.DMA((3,))] + [pltpu.SemaphoreType.DMA((2,))] * 20

    def run(*refs):
        kernel(size, *refs)

    shapes = ((nz, ny, nx), (pairs, ny1, nx1), (pairs // 2, ny2, nx2))
    inputs = [
        pltpu.with_memory_space_constraint(value, pltpu.HBM)
        for value in (pressure_guess, source, conductance)
    ]
    results = pl.pallas_call(
        run,
        out_shape=tuple(pltpu.VMEM(shape, F32) for shape in shapes),
        in_specs=[pl.BlockSpec(memory_space=pl.ANY)] * 3,
        out_specs=tuple([pl.BlockSpec(memory_space=pltpu.VMEM)] * 3),
        scratch_shapes=slab + padded + faces + sums + work + sent + halos + sems,
        compiler_params=pltpu.CompilerParams(
            collective_id=0, has_side_effects=True, vmem_limit_bytes=48 * 2 ** 20
        ),
    )(*inputs)
    return pl.pallas_call(
        write_out,
        out_shape=tuple(jax.ShapeDtypeStruct(shape, F32) for shape in shapes),
        in_specs=[pl.BlockSpec(memory_space=pl.ANY)] * 3,
        out_specs=tuple([pl.BlockSpec(memory_space=pl.ANY)] * 3),
        scratch_shapes=[pltpu.SemaphoreType.DMA((3,))],
    )(*[pltpu.with_memory_space_constraint(value, pltpu.VMEM) for value in results])


def write_out(p_src, mid_src, low_src, p_dst, mid_dst, low_dst, sem):
    copies = [
        pltpu.make_async_copy(src, dst, sem.at[i])
        for i, (src, dst) in enumerate(((p_src, p_dst), (mid_src, mid_dst), (low_src, low_dst)))
    ]
    for copy in copies:
        copy.start()
    for copy in copies:
        copy.wait()


def solution(mesh):
    size = mesh.shape["gz"]
    spec = P("gz", None, None)
    return jax.shard_map(
        lambda *args: on_device(size, *args), mesh=mesh,
        in_specs=(spec, spec, spec), out_specs=(spec, spec, spec), check_vma=False,
    )
```

```python
import jax
import jax.numpy as jnp
from jax import lax
from jax.experimental import pallas as pl
from jax.experimental.pallas import tpu as pltpu
from jax.sharding import PartitionSpec as P

F32 = jnp.float32
BF16 = jnp.bfloat16


def parity(shape, offset):
    rows = lax.broadcasted_iota(jnp.int32, shape, 0)
    cols = lax.broadcasted_iota(jnp.int32, shape, 1)
    return ((rows + cols + offset) & 1) == 0


def shifts(plane):
    ny, nx = plane.shape
    return (
        pltpu.roll(plane, ny - 1, 0),
        pltpu.roll(plane, 1, 0),
        pltpu.roll(plane, nx - 1, 1),
        pltpu.roll(plane, 1, 1),
    )


def insides(shape):
    rows = lax.broadcasted_iota(jnp.int32, shape, 0)
    cols = lax.broadcasted_iota(jnp.int32, shape, 1)
    return (rows < shape[0] - 1, rows > 0, cols < shape[1] - 1, cols > 0)


def side_faces(centre, other):
    faces, total = [], None
    for near, inside in zip(shifts(other), insides(centre.shape)):
        near = jnp.where(inside, near, 0.0)
        faces.append(jnp.where(inside, centre + near, 0.0))
        total = near if total is None else total + near
    return faces, total


def dot_parts(rows, weights):
    count = rows.shape[0]
    high = rows.astype(BF16)
    rest = rows - high.astype(F32)
    middle = rest.astype(BF16)
    low = (rest - middle.astype(F32)).astype(BF16)
    out = jnp.dot(
        jnp.concatenate([high, middle, low], axis=0), weights, preferred_element_type=F32
    )
    return out[:count] + (out[count : 2 * count] + out[2 * count :])


def weights_of(shape, inner, outer):
    fine = lax.broadcasted_iota(jnp.int32, shape, 0)
    coarse = lax.broadcasted_iota(jnp.int32, shape, 1)
    apart = fine - 2 * coarse
    near = (apart == 0) | (apart == 1)
    far = (apart == -1) | (apart == 2)
    return jnp.where(near, inner, jnp.where(far, outer, 0.0)).astype(BF16)


def kernel(
    size,
    g_hbm, b_hbm, c_hbm,
    p_ref, mid_ref, low_ref,
    craw, graw, braw,
    cr, cb, gb, rr, dl, rho,
    fpair, fro, frs, fbo, fbs,
    dr, db, nr,
    zbuf, zmid, wres, wsum,
    v1, val, cof1, dia1,
    cof2, dia2,
    send_d, send_m, send_q, send_c1, send_c2, send_2, send_3,
    halo_c, halo_d, halo_m, halo_q, halo_c1, halo_c2, halo_2, halo_n, halo_f, halo_3,
    load_sem,
    s_c, s_d, s_m, s_q, s_c1, s_c2, s_2, s_n, s_f, s_3,
    r_c, r_d, r_m, r_q, r_c1, r_c2, r_2, r_n, r_f, r_3,
):
    me = lax.axis_index("gz")
    nz, ny, nx = craw.shape
    pairs = nz // 2
    plane = (ny, nx)
    plane1 = (ny // 2, nx // 2)
    plane2 = (ny // 4, nx // 4)
    has = (me > 0, me < size - 1)
    far = me % 2
    near = 1 - far
    has_far = jnp.where(far == 0, me, size - 1 - me) > 0

    loads = [
        pltpu.make_async_copy(src, dst, load_sem.at[i])
        for i, (src, dst) in enumerate(((c_hbm, craw), (g_hbm, graw), (b_hbm, braw)))
    ]
    for load in loads:
        load.start()

    barrier = pltpu.get_barrier_semaphore()
    for side in range(2):
        @pl.when(has[side])
        def _(side=side):
            pl.semaphore_signal(
                barrier, inc=1, device_id=(me + 2 * side - 1,),
                device_id_type=pl.DeviceIdType.MESH,
            )

    for ref in (cr, cb, gb, rr, dl, rho):
        ref[0] = jnp.zeros(plane, F32)
        ref[pairs + 1] = jnp.zeros(plane, F32)
    dl[1] = jnp.zeros(plane, F32)
    dl[pairs] = jnp.zeros(plane, F32)
    for ref, depth in ((zbuf, ny), (zmid, ny // 2)):
        for i in range(ref.shape[0]):
            for j in range(ref.shape[1]):
                ref[i, j, 0:8] = jnp.zeros((8, 128), F32)
                ref[i, j, depth + 8 : depth + 16] = jnp.zeros((8, 128), F32)
    for side in range(2):
        @pl.when(jnp.logical_not(has[side]))
        def _(side=side):
            for ref in (halo_c, halo_d, halo_m, halo_q):
                ref[side] = jnp.zeros(ref.shape[1:], F32)
            for ref in (halo_c1, halo_c2, halo_2, halo_f):
                for i in range(ref.shape[1]):
                    ref[side, i] = jnp.zeros(ref.shape[2:], F32)
    wres[...] = weights_of(wres.shape, 3.0, 1.0)
    wsum[...] = weights_of(wsum.shape, 1.0, 0.0)

    def copy_out(side, src, dst, s_sem, r_sem):
        return pltpu.make_async_remote_copy(
            src_ref=src, dst_ref=dst.at[1 - side], send_sem=s_sem.at[side],
            recv_sem=r_sem.at[1 - side], device_id=(me + 2 * side - 1,),
            device_id_type=pl.DeviceIdType.MESH,
        )

    def send(src_of, dst, s_sem, r_sem):
        for side in range(2):
            @pl.when(has[side])
            def _(side=side):
                copy_out(side, src_of(side), dst, s_sem, r_sem).start()

    def wait_recv(side, present, dst, s_sem, r_sem):
        @pl.when(present)
        def _():
            pltpu.make_async_remote_copy(
                src_ref=dst.at[side], dst_ref=dst.at[side], send_sem=s_sem.at[side],
                recv_sem=r_sem.at[side], device_id=(me + 2 * side - 1,),
                device_id_type=pl.DeviceIdType.MESH,
            ).wait_recv()

    even = parity(plane, 0)

    def even_first(first, second):
        return jnp.where(parity(plane, 0), first, second)

    loads[0].wait()

    def put_rows(ref, k, value):
        for j in range(ref.shape[1]):
            ref[k, j, 8 : value.shape[0] + 8] = value[:, 128 * j : 128 * j + 128]

    def get_rows(ref, k, start, count):
        return jnp.concatenate(
            [ref[k, j, pl.ds(start, count, stride=2), :] for j in range(ref.shape[1])], axis=1
        )

    def pack(k, carry):
        low, high = craw[2 * k], craw[2 * k + 1]
        cr[k + 1] = even_first(low, high)
        cb[k + 1] = even_first(high, low)
        put_rows(zbuf, k, low + high)
        return carry

    lax.fori_loop(0, pairs, pack, 0)
    pl.semaphore_wait(barrier, jnp.where(has[0] & has[1], 2, 1))
    send(lambda side: craw.at[(nz - 1) * side], halo_c, s_c, r_c)

    def faces(k, carry):
        own, other = cr[k + 1], cb[k + 1]
        fpair[k] = own + other
        outer = even_first(cb[k], cb[k + 2])
        sides, total = side_faces(own, other)
        fro[k] = own + outer
        for i in range(4):
            frs[k, i] = sides[i]
        dr[k] = 6.0 * own + other + outer + total
        outer = even_first(cr[k + 2], cr[k])
        sides, total = side_faces(other, own)
        fbo[k] = other + outer
        for i in range(4):
            fbs[k, i] = sides[i]
        db[k] = 6.0 * other + own + outer + total
        return carry

    def gather(k, centre, outer, f_outer, f_sides):
        total = fpair[k] * centre + f_outer[k] * outer
        for i, near in enumerate(shifts(centre)):
            total = total + f_sides[k, i] * near
        return total

    def pack_g(k, carry):
        gb[k + 1] = even_first(graw[2 * k + 1], graw[2 * k])
        return carry

    def red(k, carry):
        rhs = even_first(braw[2 * k], braw[2 * k + 1])
        off = gather(k, gb[k + 1], even_first(gb[k], gb[k + 2]), fro, frs)
        top = 2.0 * rhs + off
        nr[k] = top
        rr[k + 1] = top / dr[k]
        return carry

    def put_diagonal(side, carry):
        k = (pairs - 1) * side
        half = ny // 2
        send_d[side] = jnp.where(
            parity((half, nx), side), dr[k, 0:half], pltpu.roll(dr[k, half:ny], 1, 0)
        )
        return carry

    def put_field(side, carry):
        k = (pairs - 1) * side
        send_m[side] = jnp.where(parity(plane, side), nr[k], gb[k + 1])
        return carry

    def put_second(side, carry):
        k = (pairs - 1) * side
        rhs = even_first(braw[2 * k + 1], braw[2 * k])
        part = 2.0 * rhs + fpair[k] * rr[k + 1]
        send_q[side] = jnp.where(parity(plane, side), pltpu.roll(db[k], 1, 0), part)
        return carry

    def at_ends(body):
        lax.fori_loop(0, 2, lambda i, carry: body((pairs - 1) * i, carry), 0)

    at_ends(faces)
    lax.fori_loop(0, 2, put_diagonal, 0)
    send(lambda side: send_d.at[side], halo_d, s_d, r_d)
    loads[1].wait()
    lax.fori_loop(0, pairs, pack_g, 0)
    loads[2].wait()
    at_ends(red)
    lax.fori_loop(0, 2, put_field, 0)
    send(lambda side: send_m.at[side], halo_m, s_m, r_m)
    lax.fori_loop(0, 2, put_second, 0)
    send(lambda side: send_q.at[side], halo_q, s_q, r_q)

    lax.fori_loop(1, pairs - 1, faces, 0)
    lax.fori_loop(1, pairs - 1, red, 0)

    def put_pressure(k, reds, blacks):
        p_ref[2 * k] = even_first(reds, blacks)
        p_ref[2 * k + 1] = even_first(blacks, reds)

    def black(k, carry):
        rhs = even_first(braw[2 * k + 1], braw[2 * k])
        reds = rr[k + 1]
        off = gather(k, reds, even_first(rr[k + 2], rr[k]), fbo, fbs)
        new = (2.0 * rhs + off) / db[k]
        dl[k + 1] = new - gb[k + 1]
        put_pressure(k, reds, new)
        return carry

    lax.fori_loop(1, pairs - 1, black, 0)

    def residual(k, carry):
        rho[k + 1] = gather(k, dl[k + 1], even_first(dl[k], dl[k + 2]), fro, frs)
        return carry

    lax.fori_loop(1, pairs - 1, residual, 0)

    ny1, ny2 = ny // 2, ny // 4
    rows = [
        get_rows(zbuf, k, 8, ny1) + get_rows(zbuf, k, 9, ny1)
        for k in range(pairs)
    ]
    sums = 0.125 * dot_parts(jnp.concatenate(rows, axis=0), wsum[...])
    c1 = [sums[k * ny1 : (k + 1) * ny1] for k in range(pairs)]

    def plane_sum(value):
        total = None
        for near, inside in zip(shifts(value), insides(value.shape)):
            near = jnp.where(inside, near, 0.0)
            total = near if total is None else total + near
        return total

    def diagonals(coefs):
        out = []
        for k, coef in enumerate(coefs):
            total = 6.0 * coef + plane_sum(coef)
            if k > 0:
                total = total + coefs[k - 1]
            if k < len(coefs) - 1:
                total = total + coefs[k + 1]
            out.append(total)
        return out

    d1 = diagonals(c1)
    for k in range(pairs):
        cof1[k] = c1[k]
        dia1[k] = d1[k]
    for k in range(pairs // 2):
        put_rows(zmid, k, c1[2 * k] + c1[2 * k + 1])
    rows = [
        get_rows(zmid, k, 8, ny2) + get_rows(zmid, k, 9, ny2)
        for k in range(pairs // 2)
    ]
    weights = wsum[0 : nx // 2, 0 : nx // 4]
    sums = 0.125 * dot_parts(jnp.concatenate(rows, axis=0), weights)
    c2 = [sums[k * ny2 : (k + 1) * ny2] for k in range(pairs // 2)]
    d2 = diagonals(c2)
    for k in range(2):
        cof2[k] = c2[k]
        dia2[k] = d2[k]
    for side in range(2):
        ends = (3 * side, 1 + side, 2 - side)
        for i, value in enumerate((c1[ends[0]], d1[ends[0]], c1[ends[1]], d1[ends[1]], c1[ends[2]])):
            send_c1[side, i] = value
        send_c2[side, 0] = c2[side]
        send_c2[side, 1] = d2[side]
    send(lambda side: send_c1.at[side], halo_c1, s_c1, r_c1)
    send(lambda side: send_c2.at[side], halo_c2, s_c2, r_c2)

    def restrict(ref, first, count, out_rows, weights, scale):
        rows = [
            (get_rows(ref, k, 7, out_rows) + get_rows(ref, k, 10, out_rows))
            + 3.0 * (get_rows(ref, k, 8, out_rows) + get_rows(ref, k, 9, out_rows))
            for k in range(first, first + count)
        ]
        out = scale * dot_parts(jnp.concatenate(rows, axis=0), weights)
        return [out[k * out_rows : (k + 1) * out_rows] for k in range(count)]

    def finish(step, carry):
        side = jnp.where(step == 0, near, far)
        present = (step == 0) | has_far
        wait_recv(side, present, halo_c, s_c, r_c)
        wait_recv(side, present, halo_d, s_d, r_d)
        wait_recv(side, present, halo_m, s_m, r_m)
        k = (pairs - 1) * side
        here = (nz - 1) * side
        mine = parity(plane, side)
        inside = jnp.where(present, 1.0, 0.0)
        hc, hd, hm = halo_c[side], halo_d[side], halo_m[side]
        hd = jnp.concatenate([hd, pltpu.roll(hd, ny // 2 - 1, 0)], axis=0)
        c0, g0 = craw[here], graw[here]
        face = c0 + hc
        top = jnp.where(mine, nr[k], hm) + face * jnp.where(mine, hm, g0)
        value = top / jnp.where(mine, dr[k] + hc, hd + c0)
        value = jnp.where(mine, value, inside * value)
        reds = jnp.where(mine, value, rr[k + 1])
        rr[k + 1] = reds
        val[side] = value

        rhs = even_first(braw[2 * k + 1], braw[2 * k])
        off = gather(k, reds, even_first(rr[k + 2], rr[k]), fbo, fbs)
        off = off + jnp.where(mine, 0.0, face * value)
        new = (2.0 * rhs + off) / (db[k] + jnp.where(mine, 0.0, hc))
        delta = new - gb[k + 1]
        dl[k + 1] = delta
        put_pressure(k, reds, new)

        rho[k + 1] = gather(k, delta, even_first(dl[k], dl[k + 2]), fro, frs)
        inner = k + 1 - 2 * side
        more = (cr[inner + 1] + cb[k + 1]) * delta
        rho[inner + 1] = rho[inner + 1] + jnp.where(mine, more, 0.0)

        for i, at in enumerate((k, inner)):
            put_rows(zbuf, i, 3.0 * rho[at + 1] + even_first(rho[at + 2], rho[at]))
        put_rows(zbuf, 2, jnp.where(mine, rho[k + 1], 0.0))
        parts = restrict(zbuf, 0, 3, ny1, wres[...], 0.5 ** 10)
        for i in range(3):
            v1[side, i] = parts[i]
        send_2[side, 0] = parts[0]
        send_2[side, 1] = parts[2]
        send_2[side, 2] = (cof1[k] + cof1[inner]) * (8.0 * parts[1] / dia1[inner])

        @pl.when(present)
        def _():
            copy_out(side, send_2.at[side, 0:2], halo_2, s_2, r_2).start()

        @pl.when(step == 0)
        def _():
            copy_out(side, send_2.at[side, 2], halo_n, s_n, r_n).start()

        return carry

    def beyond(side, present):
        wait_recv(side, present, halo_q, s_q, r_q)
        k = (pairs - 1) * side
        mine = parity(plane, side)
        inside = jnp.where(present, 1.0, 0.0)
        hc, hq, value = halo_c[side], halo_q[side], val[side]
        c0 = craw[(nz - 1) * side]
        face = c0 + hc
        off = hq + face * value
        sides, _ = side_faces(hc, hc)
        for f, shifted in zip(sides, shifts(value)):
            off = off + f * shifted
        delta = off / (pltpu.roll(hq, ny - 1, 0) + c0) - halo_m[side]
        put_rows(zbuf, 0, jnp.where(mine, inside * (face * delta), 0.0))
        put_rows(zbuf, 1, jnp.where(mine, 0.0, inside * (face * dl[k + 1])))
        here, there = restrict(zbuf, 0, 2, ny1, wres[...], 0.5 ** 10)
        v1[side, 0] = v1[side, 0] + 3.0 * here
        v1[side, 2] = v1[side, 2] + here
        v1[side, 3] = there

    lax.fori_loop(0, 2, finish, 0)
    beyond(near, me >= 0)

    def mask1(j):
        return parity(plane1, j + far + 4)

    def at1(j):
        return 3 * far + j * (1 - 2 * far)

    inside = jnp.where(has_far, 1.0, 0.0)
    true = me >= 0
    cof = {j: cof1[at1(j)] for j in range(4)}
    dia = {j: dia1[at1(j)] for j in range(4)}

    def flat(j, field):
        return cof[j] * plane_sum(field) + plane_sum(cof[j] * field)

    def across(i, j, field):
        return (cof[i] + cof[j]) * field

    def red_of(j, right):
        return jnp.where(mask1(j), 8.0 * right / dia[j], 0.0)

    def black_of(j, top):
        return jnp.where(mask1(j), 0.0, top / dia[j])

    wait_recv(near, true, halo_c1, s_c1, r_c1)
    wait_recv(near, true, halo_2, s_2, r_2)
    wait_recv(near, true, halo_n, s_n, r_n)
    cof[4] = halo_c1[near, 0]
    dia[4] = halo_c1[near, 1] + cof[3]
    dia[3] = dia[3] + cof[4]
    rhs = {
        4: halo_2[near, 0] + 3.0 * v1[near, 3] + v1[near, 2],
        3: v1[near, 0] + (halo_2[near, 1] + v1[near, 3]),
        2: v1[near, 1],
        1: v1[far, 1],
    }
    red = {j: red_of(j, rhs[j]) for j in (1, 2, 3, 4)}
    black = {}
    black[4] = black_of(4, 8.0 * rhs[4] + halo_n[near] + flat(4, red[4]) + across(4, 3, red[3]))
    for j in (3, 2):
        black[j] = black_of(
            j, 8.0 * rhs[j] + flat(j, red[j]) + across(j, j + 1, red[j + 1]) + across(j, j - 1, red[j - 1])
        )
    part1 = 8.0 * rhs[1] + flat(1, red[1]) + across(1, 2, red[2])
    part2 = flat(2, black[2]) + across(2, 3, black[3])
    cross = across(1, 2, black[2])
    send_2[far, 2] = jnp.where(mask1(0), part2, across(0, 1, red[1]))
    send_2[far, 3] = jnp.where(mask1(1), cross, part1)

    @pl.when(has_far)
    def _():
        copy_out(far, send_2.at[far, 2:4], halo_f, s_f, r_f).start()

    beyond(far, has_far)
    wait_recv(far, has_far, halo_c1, s_c1, r_c1)
    cof.update({-1: halo_c1[far, 0], -2: halo_c1[far, 2], -3: halo_c1[far, 4]})
    dia.update({-1: halo_c1[far, 1] + cof[0], -2: halo_c1[far, 3], 0: dia[0] + cof[-1]})
    wait_recv(far, has_far, halo_2, s_2, r_2)
    rhs[0] = v1[far, 0] + (halo_2[far, 1] + v1[far, 3])
    rhs[-1] = halo_2[far, 0] + 3.0 * v1[far, 3] + v1[far, 2]
    red[0] = red_of(0, rhs[0])
    red[-1] = inside * red_of(-1, rhs[-1])
    black[0] = black_of(0, 8.0 * rhs[0] + flat(0, red[0]) + across(0, -1, red[-1]) + across(0, 1, red[1]))
    black[1] = black_of(1, part1 + across(1, 0, red[0]))
    res = {
        3: flat(3, black[3]) + across(3, 2, black[2]) + across(3, 4, black[4]),
        2: part2 + across(2, 1, black[1]),
        1: flat(1, black[1]) + across(1, 0, black[0]) + cross,
    }
    res = {j: jnp.where(mask1(j), value, 0.0) for j, value in res.items()}
    weights2 = wres[0 : nx // 2, 0 : nx // 4]
    put_rows(zmid, 0, 3.0 * (res[3] + res[2]) + res[1])
    put_rows(zmid, 1, res[3])
    parts = restrict(zmid, 0, 2, ny2, weights2, 0.5 ** 12)
    send_3[0] = parts[0]
    send_3[1] = parts[1]
    copy_out(near, send_3, halo_3, s_3, r_3).start()

    wait_recv(far, has_far, halo_f, s_f, r_f)
    black[-1] = inside * black_of(-1, 8.0 * rhs[-1] + halo_f[far, 0] + flat(-1, red[-1]) + across(-1, 0, red[0]))
    black[-2] = inside * black_of(-2, halo_f[far, 1] + across(-2, -1, red[-1]))
    more = {
        0: flat(0, black[0]) + across(0, -1, black[-1]) + across(0, 1, black[1]),
        -1: flat(-1, black[-1]) + across(-1, -2, black[-2]) + across(-1, 0, black[0]),
        -2: halo_f[far, 1] + flat(-2, black[-2]) + across(-2, -1, black[-1]),
        -3: halo_f[far, 0] + across(-3, -2, black[-2]),
    }
    for j, value in more.items():
        res[j] = jnp.where(mask1(j) if j == 0 else mask1(j) & has_far, value, 0.0)

    put_rows(zmid, 2, 3.0 * (res[0] + res[1]) + (res[-1] + res[2]))
    put_rows(zmid, 3, 3.0 * (res[-1] + res[-2]) + (res[0] + res[-3]))
    parts = parts + restrict(zmid, 2, 2, ny2, weights2, 0.5 ** 12)
    for j in range(4):
        mid_ref[at1(j)] = red[j] + black[j]

    wait_recv(near, true, halo_c2, s_c2, r_c2)
    wait_recv(far, has_far, halo_c2, s_c2, r_c2)
    wait_recv(near, true, halo_3, s_3, r_3)

    def mask2(j):
        return parity(plane2, j + far + 4)

    def at2(j):
        return far + j * (1 - 2 * far)

    cof = {-1: halo_c2[far, 0], 0: cof2[at2(0)], 1: cof2[at2(1)], 2: halo_c2[near, 0]}
    dia = {
        -1: halo_c2[far, 1] + cof[0], 0: dia2[at2(0)] + cof[-1],
        1: dia2[at2(1)] + cof[2], 2: halo_c2[near, 1] + cof[1],
    }
    rhs = {
        -1: parts[3], 0: parts[2], 1: parts[0] + halo_3[near, 1], 2: halo_3[near, 0] + parts[1],
    }
    red = {j: jnp.where(mask2(j), 32.0 * rhs[j] / dia[j], 0.0) for j in rhs}
    red[-1] = inside * red[-1]
    for j in (0, 1):
        top = 32.0 * rhs[j] + flat(j, red[j]) + across(j, j - 1, red[j - 1]) + across(j, j + 1, red[j + 1])
        low_ref[at2(j)] = jnp.where(mask2(j), red[j], top / dia[j])

    def wait_sent(side, present, messages):
        @pl.when(present)
        def _():
            for src, dst, s_sem, r_sem in messages:
                copy_out(side, src, dst, s_sem, r_sem).wait_send()

    for side in range(2):
        wait_sent(side, has[side], (
            (craw.at[(nz - 1) * side], halo_c, s_c, r_c),
            (send_d.at[side], halo_d, s_d, r_d),
            (send_m.at[side], halo_m, s_m, r_m),
            (send_q.at[side], halo_q, s_q, r_q),
            (send_c1.at[side], halo_c1, s_c1, r_c1),
            (send_c2.at[side], halo_c2, s_c2, r_c2),
            (send_2.at[side, 0:2], halo_2, s_2, r_2),
        ))
    wait_sent(near, true, (
        (send_2.at[near, 2], halo_n, s_n, r_n), (send_3, halo_3, s_3, r_3),
    ))
    wait_sent(far, has_far, ((send_2.at[far, 2:4], halo_f, s_f, r_f),))


def on_device(size, pressure_guess, source, conductance):
    nz, ny, nx = pressure_guess.shape
    pairs = nz // 2
    ny1, nx1, ny2, nx2 = ny // 2, nx // 2, ny // 4, nx // 4

    def vmem(*shape):
        return pltpu.VMEM(shape, F32)

    slab = [vmem(nz, ny, nx)] * 3
    padded = [vmem(pairs + 2, ny, nx)] * 6
    faces = [
        vmem(pairs, ny, nx), vmem(pairs, ny, nx), vmem(pairs, 4, ny, nx),
        vmem(pairs, ny, nx), vmem(pairs, 4, ny, nx),
    ]
    sums = [vmem(pairs, ny, nx)] * 3
    work = [
        vmem(pairs + 2, nx // 128, ny + 16, 128), vmem(4, nx1 // 128, ny1 + 16, 128),
        pltpu.VMEM((nx, nx1), BF16), pltpu.VMEM((nx, nx1), BF16),
        vmem(2, 4, ny1, nx1), vmem(2, ny, nx), vmem(pairs, ny1, nx1), vmem(pairs, ny1, nx1),
        vmem(2, ny2, nx2), vmem(2, ny2, nx2),
    ]
    messages = [
        vmem(2, ny1, nx), vmem(2, ny, nx), vmem(2, ny, nx), vmem(2, 5, ny1, nx1), vmem(2, 2, ny2, nx2),
    ]
    sent = messages + [vmem(2, 4, ny1, nx1), vmem(2, ny2, nx2)]
    halos = [vmem(2, ny, nx)] + messages + [
        vmem(2, 2, ny1, nx1), vmem(2, ny1, nx1), vmem(2, 2, ny1, nx1), vmem(2, 2, ny2, nx2),
    ]
    sems = [pltpu.SemaphoreType.DMA((3,))] + [pltpu.SemaphoreType.DMA((2,))] * 20

    def run(*refs):
        kernel(size, *refs)

    shapes = ((nz, ny, nx), (pairs, ny1, nx1), (pairs // 2, ny2, nx2))
    inputs = [
        pltpu.with_memory_space_constraint(value, pltpu.HBM)
        for value in (pressure_guess, source, conductance)
    ]
    results = pl.pallas_call(
        run,
        out_shape=tuple(pltpu.VMEM(shape, F32) for shape in shapes),
        in_specs=[pl.BlockSpec(memory_space=pl.ANY)] * 3,
        out_specs=tuple([pl.BlockSpec(memory_space=pltpu.VMEM)] * 3),
        scratch_shapes=slab + padded + faces + sums + work + sent + halos + sems,
        compiler_params=pltpu.CompilerParams(
            collective_id=0, has_side_effects=True, vmem_limit_bytes=48 * 2 ** 20
        ),
    )(*inputs)
    return pl.pallas_call(
        write_out,
        out_shape=tuple(jax.ShapeDtypeStruct(shape, F32) for shape in shapes),
        in_specs=[pl.BlockSpec(memory_space=pl.ANY)] * 3,
        out_specs=tuple([pl.BlockSpec(memory_space=pl.ANY)] * 3),
        scratch_shapes=[pltpu.SemaphoreType.DMA((3,))],
    )(*[pltpu.with_memory_space_constraint(value, pltpu.VMEM) for value in results])


def write_out(p_src, mid_src, low_src, p_dst, mid_dst, low_dst, sem):
    copies = [
        pltpu.make_async_copy(src, dst, sem.at[i])
        for i, (src, dst) in enumerate(((p_src, p_dst), (mid_src, mid_dst), (low_src, low_dst)))
    ]
    for copy in copies:
        copy.start()
    for copy in copies:
        copy.wait()


def solution(mesh):
    size = mesh.shape["gz"]
    spec = P("gz", None, None)
    return jax.shard_map(
        lambda *args: on_device(size, *args), mesh=mesh,
        in_specs=(spec, spec, spec), out_specs=(spec, spec, spec), check_vma=False,
    )
```

```python
import jax
import jax.numpy as jnp
from jax import lax
from jax.experimental import pallas as pl
from jax.experimental.pallas import tpu as pltpu
from jax.sharding import PartitionSpec as P

F32 = jnp.float32
BF16 = jnp.bfloat16


def parity(shape, offset):
    rows = lax.broadcasted_iota(jnp.int32, shape, 0)
    cols = lax.broadcasted_iota(jnp.int32, shape, 1)
    return ((rows + cols + offset) & 1) == 0


def shifts(plane):
    ny, nx = plane.shape
    return (
        pltpu.roll(plane, ny - 1, 0),
        pltpu.roll(plane, 1, 0),
        pltpu.roll(plane, nx - 1, 1),
        pltpu.roll(plane, 1, 1),
    )


def insides(shape):
    rows = lax.broadcasted_iota(jnp.int32, shape, 0)
    cols = lax.broadcasted_iota(jnp.int32, shape, 1)
    return (rows < shape[0] - 1, rows > 0, cols < shape[1] - 1, cols > 0)


def side_faces(centre, other):
    faces, total = [], None
    for near, inside in zip(shifts(other), insides(centre.shape)):
        near = jnp.where(inside, near, 0.0)
        faces.append(jnp.where(inside, centre + near, 0.0))
        total = near if total is None else total + near
    return faces, total


def dot_parts(rows, weights):
    count = rows.shape[0]
    high = rows.astype(BF16)
    rest = rows - high.astype(F32)
    middle = rest.astype(BF16)
    low = (rest - middle.astype(F32)).astype(BF16)
    out = jnp.dot(
        jnp.concatenate([high, middle, low], axis=0), weights, preferred_element_type=F32
    )
    return out[:count] + (out[count : 2 * count] + out[2 * count :])


def weights_of(shape, inner, outer):
    fine = lax.broadcasted_iota(jnp.int32, shape, 0)
    coarse = lax.broadcasted_iota(jnp.int32, shape, 1)
    apart = fine - 2 * coarse
    near = (apart == 0) | (apart == 1)
    far = (apart == -1) | (apart == 2)
    return jnp.where(near, inner, jnp.where(far, outer, 0.0)).astype(BF16)


def kernel(
    size,
    g_hbm, b_hbm, c_hbm,
    p_ref, mid_ref, low_ref,
    craw, graw, braw,
    cr, cb, gb, rr, dl, rho,
    fpair, fro, frs, fbo, fbs,
    dr, db, nr,
    zbuf, zmid, wres, wsum,
    v1, topb, cof1, dia1,
    cof2, dia2,
    send_a, send_d, send_q, send_c1, send_c2, send_2, send_3,
    halo_a, halo_d, halo_q, halo_c1, halo_c2, halo_2, halo_n, halo_f, halo_3,
    load_sem,
    s_a, s_d, s_q, s_c1, s_c2, s_2, s_n, s_f, s_3,
    r_a, r_d, r_q, r_c1, r_c2, r_2, r_n, r_f, r_3,
):
    me = lax.axis_index("gz")
    nz, ny, nx = craw.shape
    pairs = nz // 2
    plane = (ny, nx)
    plane1 = (ny // 2, nx // 2)
    plane2 = (ny // 4, nx // 4)
    has = (me > 0, me < size - 1)
    far = me % 2
    near = 1 - far
    has_far = jnp.where(far == 0, me, size - 1 - me) > 0

    loads = [
        pltpu.make_async_copy(src, dst, load_sem.at[i])
        for i, (src, dst) in enumerate(((c_hbm, craw), (g_hbm, graw), (b_hbm, braw)))
    ]
    for load in loads:
        load.start()

    barrier = pltpu.get_barrier_semaphore()
    for side in range(2):
        @pl.when(has[side])
        def _(side=side):
            pl.semaphore_signal(
                barrier, inc=1, device_id=(me + 2 * side - 1,),
                device_id_type=pl.DeviceIdType.MESH,
            )

    for ref in (cr, cb, gb, rr, dl, rho):
        ref[0] = jnp.zeros(plane, F32)
        ref[pairs + 1] = jnp.zeros(plane, F32)
    dl[1] = jnp.zeros(plane, F32)
    dl[pairs] = jnp.zeros(plane, F32)
    for ref, depth in ((zbuf, ny), (zmid, ny // 2)):
        for i in range(ref.shape[0]):
            for j in range(ref.shape[1]):
                ref[i, j, 0:8] = jnp.zeros((8, 128), F32)
                ref[i, j, depth + 8 : depth + 16] = jnp.zeros((8, 128), F32)
    for side in range(2):
        @pl.when(jnp.logical_not(has[side]))
        def _(side=side):
            for ref in (halo_a, halo_q):
                ref[side] = jnp.zeros(ref.shape[1:], F32)
            for ref in (halo_d, halo_c1, halo_c2, halo_2, halo_f):
                for i in range(ref.shape[1]):
                    ref[side, i] = jnp.zeros(ref.shape[2:], F32)
    wres[...] = weights_of(wres.shape, 3.0, 1.0)
    wsum[...] = weights_of(wsum.shape, 1.0, 0.0)

    def copy_out(side, src, dst, s_sem, r_sem):
        return pltpu.make_async_remote_copy(
            src_ref=src, dst_ref=dst.at[1 - side], send_sem=s_sem.at[side],
            recv_sem=r_sem.at[1 - side], device_id=(me + 2 * side - 1,),
            device_id_type=pl.DeviceIdType.MESH,
        )

    def send(src_of, dst, s_sem, r_sem, allowed=True):
        for side in range(2):
            @pl.when(has[side] & allowed)
            def _(side=side):
                copy_out(side, src_of(side), dst, s_sem, r_sem).start()

    def wait_recv(side, present, dst, s_sem, r_sem):
        @pl.when(present)
        def _():
            pltpu.make_async_remote_copy(
                src_ref=dst.at[side], dst_ref=dst.at[side], send_sem=s_sem.at[side],
                recv_sem=r_sem.at[side], device_id=(me + 2 * side - 1,),
                device_id_type=pl.DeviceIdType.MESH,
            ).wait_recv()

    even = parity(plane, 0)

    def even_first(first, second):
        return jnp.where(parity(plane, 0), first, second)

    loads[0].wait()

    def put_rows(ref, k, value):
        for j in range(ref.shape[1]):
            ref[k, j, 8 : value.shape[0] + 8] = value[:, 128 * j : 128 * j + 128]

    def get_rows(ref, k, start, count):
        return jnp.concatenate(
            [ref[k, j, pl.ds(start, count, stride=2), :] for j in range(ref.shape[1])], axis=1
        )

    def pack(k, carry):
        low, high = craw[2 * k], craw[2 * k + 1]
        cr[k + 1] = even_first(low, high)
        cb[k + 1] = even_first(high, low)
        put_rows(zbuf, k, low + high)
        return carry

    lax.fori_loop(0, pairs, pack, 0)

    def faces(k, carry):
        own, other = cr[k + 1], cb[k + 1]
        fpair[k] = own + other
        outer = even_first(cb[k], cb[k + 2])
        sides, total = side_faces(own, other)
        fro[k] = own + outer
        for i in range(4):
            frs[k, i] = sides[i]
        dr[k] = 6.0 * own + other + outer + total
        outer = even_first(cr[k + 2], cr[k])
        sides, total = side_faces(other, own)
        fbo[k] = other + outer
        for i in range(4):
            fbs[k, i] = sides[i]
        db[k] = 6.0 * other + own + outer + total
        return carry

    def gather(k, centre, outer, f_outer, f_sides):
        total = fpair[k] * centre + f_outer[k] * outer
        for i, near in enumerate(shifts(centre)):
            total = total + f_sides[k, i] * near
        return total

    def pack_g(k, carry):
        gb[k + 1] = even_first(graw[2 * k + 1], graw[2 * k])
        return carry

    def red(k, carry):
        rhs = even_first(braw[2 * k], braw[2 * k + 1])
        off = gather(k, gb[k + 1], even_first(gb[k], gb[k + 2]), fro, frs)
        top = 2.0 * rhs + off
        nr[k] = top
        rr[k + 1] = top / dr[k]
        return carry

    def put_first(side, carry):
        here = (nz - 1) * side
        send_a[side] = jnp.where(parity(plane, side), pltpu.roll(craw[here], 1, 0), graw[here])
        return carry

    def put_diagonal(side, carry):
        k = (pairs - 1) * side
        mine = parity(plane, side)
        send_d[side, 0] = jnp.where(mine, dr[k], db[k])
        send_d[side, 1] = jnp.where(mine, craw[(nz - 1) * side], fpair[k])
        return carry

    def put_tops(side, carry):
        k = (pairs - 1) * side
        rhs = even_first(braw[2 * k + 1], braw[2 * k])
        send_q[side] = jnp.where(parity(plane, side), nr[k], 2.0 * rhs + fpair[k] * rr[k + 1])
        return carry

    def at_ends(body):
        lax.fori_loop(0, 2, lambda i, carry: body((pairs - 1) * i, carry), 0)

    def enter(allowed):
        @pl.when(allowed)
        def _():
            pl.semaphore_wait(barrier, jnp.where(has[0] & has[1], 2, 1))

    odd = far == 1
    at_ends(faces)
    lax.fori_loop(0, 2, put_diagonal, 0)
    enter(odd)
    send(lambda side: send_d.at[side], halo_d, s_d, r_d, odd)
    loads[1].wait()
    lax.fori_loop(0, 2, put_first, 0)
    send(lambda side: send_a.at[side], halo_a, s_a, r_a, odd)
    lax.fori_loop(0, pairs, pack_g, 0)
    loads[2].wait()
    at_ends(red)
    lax.fori_loop(0, 2, put_tops, 0)
    send(lambda side: send_q.at[side], halo_q, s_q, r_q, odd)
    even_core = far == 0
    enter(even_core)
    send(lambda side: send_a.at[side], halo_a, s_a, r_a, even_core)
    send(lambda side: send_d.at[side], halo_d, s_d, r_d, even_core)
    send(lambda side: send_q.at[side], halo_q, s_q, r_q, even_core)

    lax.fori_loop(1, pairs - 1, faces, 0)
    lax.fori_loop(1, pairs - 1, red, 0)

    def put_pressure(k, reds, blacks):
        p_ref[2 * k] = even_first(reds, blacks)
        p_ref[2 * k + 1] = even_first(blacks, reds)

    def black(k, carry):
        rhs = even_first(braw[2 * k + 1], braw[2 * k])
        reds = rr[k + 1]
        off = gather(k, reds, even_first(rr[k + 2], rr[k]), fbo, fbs)
        new = (2.0 * rhs + off) / db[k]
        dl[k + 1] = new - gb[k + 1]
        put_pressure(k, reds, new)
        return carry

    lax.fori_loop(1, pairs - 1, black, 0)

    def residual(k, carry):
        rho[k + 1] = gather(k, dl[k + 1], even_first(dl[k], dl[k + 2]), fro, frs)
        return carry

    lax.fori_loop(1, pairs - 1, residual, 0)

    ny1, ny2 = ny // 2, ny // 4
    rows = [
        get_rows(zbuf, k, 8, ny1) + get_rows(zbuf, k, 9, ny1)
        for k in range(pairs)
    ]
    sums = 0.125 * dot_parts(jnp.concatenate(rows, axis=0), wsum[...])
    c1 = [sums[k * ny1 : (k + 1) * ny1] for k in range(pairs)]

    def plane_sum(value):
        total = None
        for near, inside in zip(shifts(value), insides(value.shape)):
            near = jnp.where(inside, near, 0.0)
            total = near if total is None else total + near
        return total

    def diagonals(coefs):
        out = []
        for k, coef in enumerate(coefs):
            total = 6.0 * coef + plane_sum(coef)
            if k > 0:
                total = total + coefs[k - 1]
            if k < len(coefs) - 1:
                total = total + coefs[k + 1]
            out.append(total)
        return out

    d1 = diagonals(c1)
    for k in range(pairs):
        cof1[k] = c1[k]
        dia1[k] = d1[k]
    for k in range(pairs // 2):
        put_rows(zmid, k, c1[2 * k] + c1[2 * k + 1])
    rows = [
        get_rows(zmid, k, 8, ny2) + get_rows(zmid, k, 9, ny2)
        for k in range(pairs // 2)
    ]
    weights = wsum[0 : nx // 2, 0 : nx // 4]
    sums = 0.125 * dot_parts(jnp.concatenate(rows, axis=0), weights)
    c2 = [sums[k * ny2 : (k + 1) * ny2] for k in range(pairs // 2)]
    d2 = diagonals(c2)
    for k in range(2):
        cof2[k] = c2[k]
        dia2[k] = d2[k]
    for side in range(2):
        ends = (3 * side, 1 + side, 2 - side)
        for i, end in enumerate(ends):
            send_c1[side, 2 * i] = c1[end]
            send_c1[side, 2 * i + 1] = d1[end]
        send_c2[side, 0] = c2[side]
        send_c2[side, 1] = d2[side]
    send(lambda side: send_c1.at[side], halo_c1, s_c1, r_c1)
    send(lambda side: send_c2.at[side], halo_c2, s_c2, r_c2)

    def restrict(ref, first, count, out_rows, weights, scale):
        rows = [
            (get_rows(ref, k, 7, out_rows) + get_rows(ref, k, 10, out_rows))
            + 3.0 * (get_rows(ref, k, 8, out_rows) + get_rows(ref, k, 9, out_rows))
            for k in range(first, first + count)
        ]
        out = scale * dot_parts(jnp.concatenate(rows, axis=0), weights)
        return [out[k * out_rows : (k + 1) * out_rows] for k in range(count)]

    def first_stage(side, present, is_near):
        wait_recv(side, present, halo_a, s_a, r_a)
        k = (pairs - 1) * side
        mine = parity(plane, side)
        field = halo_a[side]
        coef = pltpu.roll(field, ny - 1, 0)
        face = craw[(nz - 1) * side] + coef
        value = (nr[k] + face * field) / (dr[k] + coef)
        reds = jnp.where(mine, value, rr[k + 1])
        rr[k + 1] = reds
        rhs = even_first(braw[2 * k + 1], braw[2 * k])
        top = 2.0 * rhs + gather(k, reds, even_first(rr[k + 2], rr[k]), fbo, fbs)
        topb[side] = top
        new = top / db[k]
        delta = new - gb[k + 1]
        dl[k + 1] = delta
        put_pressure(k, reds, new)
        own = gather(k, delta, even_first(dl[k], dl[k + 2]), fro, frs)
        rho[k + 1] = own
        inner = k + 1 - 2 * side
        more = (cr[inner + 1] + cb[k + 1]) * delta
        rho[inner + 1] = rho[inner + 1] + jnp.where(mine, more, 0.0)

        for i, at in enumerate((k, inner)):
            put_rows(zbuf, i, 3.0 * rho[at + 1] + even_first(rho[at + 2], rho[at]))
        put_rows(zbuf, 2, jnp.where(mine, own, 0.0))
        parts = restrict(zbuf, 0, 3, ny1, wres[...], 0.5 ** 10)
        for i in range(3):
            v1[side, i] = parts[i]
        send_2[side, 0] = parts[0]
        send_2[side, 1] = parts[2]

        @pl.when(present)
        def _():
            copy_out(side, send_2.at[side, 0:2], halo_2, s_2, r_2).start()

        if is_near:
            send_2[side, 2] = (cof1[k] + cof1[inner]) * (8.0 * parts[1] / dia1[inner])
            copy_out(side, send_2.at[side, 2], halo_n, s_n, r_n).start()

    def second_stage(side, present):
        wait_recv(side, present, halo_d, s_d, r_d)
        wait_recv(side, present, halo_q, s_q, r_q)
        k = (pairs - 1) * side
        here = (nz - 1) * side
        mine = parity(plane, side)
        black_there = mine & present
        field = halo_a[side]
        diagonal, coef, tops = halo_d[side, 0], halo_d[side, 1], halo_q[side]
        c0, g0 = craw[here], graw[here]
        hc = jnp.where(mine, pltpu.roll(field, ny - 1, 0), coef)
        face = c0 + hc
        value = jnp.where(present, (tops + face * g0) / (diagonal + c0), 0.0)
        sides, _ = side_faces(hc, hc)
        short = tops
        for f, shifted in zip(sides, shifts(value)):
            short = short + f * shifted
        reds = rr[k + 1]
        new = (jnp.where(mine, short, topb[side]) + face * jnp.where(mine, reds, value)) / (
            jnp.where(mine, diagonal + c0, db[k] + hc)
        )
        old = dl[k + 1]
        delta = new - gb[k + 1]
        change = jnp.where(mine, 0.0, delta - old)
        dl[k + 1] = jnp.where(mine, old, delta)
        p_ref[here] = jnp.where(mine, reds, new)
        delta_there = jnp.where(black_there, new - field, 0.0)
        change_there = jnp.where(black_there, new - short / diagonal, 0.0)
        add = fpair[k] * change
        for i, shifted in enumerate(shifts(change)):
            add = add + frs[k, i] * shifted
        put_rows(zbuf, 0, jnp.where(mine, add + face * delta_there, 0.0))
        put_rows(zbuf, 1, jnp.where(mine, 0.0, add))
        add = face * delta
        for f, shifted in zip(sides, shifts(change_there)):
            add = add + f * shifted
        put_rows(zbuf, 2, jnp.where(mine | jnp.logical_not(present), 0.0, add))
        put_rows(zbuf, 3, jnp.where(black_there, coef * change_there, 0.0))
        parts = restrict(zbuf, 0, 4, ny1, wres[...], 0.5 ** 10)
        v1[side, 0] = v1[side, 0] + 3.0 * (parts[0] + parts[1])
        v1[side, 1] = v1[side, 1] + parts[1]
        v1[side, 2] = v1[side, 2] + parts[0]
        v1[side, 3] = parts[2]
        v1[side, 4] = parts[3]

    true = me >= 0
    first_stage(near, true, True)
    second_stage(near, true)

    def mask1(j):
        return parity(plane1, j + far + 4)

    def at1(j):
        return 3 * far + j * (1 - 2 * far)

    inside = jnp.where(has_far, 1.0, 0.0)
    cof = {j: cof1[at1(j)] for j in range(4)}
    dia = {j: dia1[at1(j)] for j in range(4)}

    def flat(j, field):
        return cof[j] * plane_sum(field) + plane_sum(cof[j] * field)

    def across(i, j, field):
        return (cof[i] + cof[j]) * field

    def red_of(j, right):
        return jnp.where(mask1(j), 8.0 * right / dia[j], 0.0)

    def black_of(j, top):
        return jnp.where(mask1(j), 0.0, top / dia[j])

    wait_recv(near, true, halo_c1, s_c1, r_c1)
    wait_recv(near, true, halo_2, s_2, r_2)
    wait_recv(near, true, halo_n, s_n, r_n)
    cof.update({4: halo_c1[near, 0], 5: halo_c1[near, 2]})
    dia.update({3: dia[3] + cof[4], 4: halo_c1[near, 1] + cof[3], 5: halo_c1[near, 3]})
    rhs = {
        4: halo_2[near, 0] + 3.0 * (v1[near, 3] + v1[near, 4]) + v1[near, 2],
        3: v1[near, 0] + (halo_2[near, 1] + v1[near, 3]),
        2: v1[near, 1],
    }
    red = {j: red_of(j, rhs[j]) for j in (2, 3, 4)}
    black = {}
    beyond = halo_n[near] + across(4, 5, red_of(5, v1[near, 4]))
    black[4] = black_of(4, 8.0 * rhs[4] + beyond + flat(4, red[4]) + across(4, 3, red[3]))
    black[3] = black_of(
        3, 8.0 * rhs[3] + flat(3, red[3]) + across(3, 4, red[4]) + across(3, 2, red[2])
    )
    base1 = across(1, 2, red[2])
    base2 = 8.0 * rhs[2] + flat(2, red[2]) + across(2, 3, red[3])
    base3 = across(2, 3, black[3])

    def middle():
        right = v1[far, 1]
        red1 = red_of(1, right)
        black2 = black_of(2, base2 + across(2, 1, red1))
        part1 = 8.0 * right + flat(1, red1) + base1
        part2 = flat(2, black2) + base3
        return red1, black2, part1, part2, across(1, 2, black2)

    first_stage(far, has_far, False)
    red1, black2, part1, part2, cross = middle()
    send_2[far, 2] = jnp.where(mask1(0), part2, across(0, 1, red1))
    send_2[far, 3] = jnp.where(mask1(1), cross, part1)

    @pl.when(has_far)
    def _():
        copy_out(far, send_2.at[far, 2:4], halo_f, s_f, r_f).start()

    second_stage(far, has_far)
    red[1], black[2], part1, part2, cross = middle()
    wait_recv(far, has_far, halo_c1, s_c1, r_c1)
    cof.update({-1: halo_c1[far, 0], -2: halo_c1[far, 2], -3: halo_c1[far, 4]})
    dia.update({
        -1: halo_c1[far, 1] + cof[0], -2: halo_c1[far, 3], -3: halo_c1[far, 5], 0: dia[0] + cof[-1],
    })
    there1, there2 = v1[far, 3], v1[far, 4]
    more_red = jnp.where(has_far, red_of(-2, there2), 0.0)
    more_black = jnp.where(has_far, black_of(-3, across(-3, -2, more_red)), 0.0)
    fix1 = jnp.where(mask1(-1), flat(-3, more_black), across(-1, -2, more_red))
    fix2 = jnp.where(mask1(-2), across(-2, -3, more_black), 8.0 * there2 + flat(-2, more_red))
    end0 = v1[far, 0] + there1
    end1 = 3.0 * (there1 + there2) + v1[far, 2]
    wait_recv(far, has_far, halo_2, s_2, r_2)
    rhs[0] = halo_2[far, 1] + end0
    rhs[-1] = halo_2[far, 0] + end1
    red[0] = red_of(0, rhs[0])
    red[-1] = inside * red_of(-1, rhs[-1])
    black[0] = black_of(0, 8.0 * rhs[0] + flat(0, red[0]) + across(0, -1, red[-1]) + across(0, 1, red[1]))
    black[1] = black_of(1, part1 + across(1, 0, red[0]))
    res = {
        3: flat(3, black[3]) + across(3, 2, black[2]) + across(3, 4, black[4]),
        2: part2 + across(2, 1, black[1]),
        1: flat(1, black[1]) + across(1, 0, black[0]) + cross,
    }
    res = {j: jnp.where(mask1(j), value, 0.0) for j, value in res.items()}
    weights2 = wres[0 : nx // 2, 0 : nx // 4]
    put_rows(zmid, 0, 3.0 * (res[3] + res[2]) + res[1])
    put_rows(zmid, 1, res[3])
    parts = restrict(zmid, 0, 2, ny2, weights2, 0.5 ** 12)
    send_3[0] = parts[0]
    send_3[1] = parts[1]
    copy_out(near, send_3, halo_3, s_3, r_3).start()

    wait_recv(far, has_far, halo_f, s_f, r_f)
    seconds = (halo_f[far, 0] + fix1, halo_f[far, 1] + fix2)
    black[-1] = inside * black_of(-1, 8.0 * rhs[-1] + seconds[0] + flat(-1, red[-1]) + across(-1, 0, red[0]))
    black[-2] = inside * black_of(-2, seconds[1] + across(-2, -1, red[-1]))
    more = {
        0: flat(0, black[0]) + across(0, -1, black[-1]) + across(0, 1, black[1]),
        -1: flat(-1, black[-1]) + across(-1, -2, black[-2]) + across(-1, 0, black[0]),
        -2: seconds[1] + flat(-2, black[-2]) + across(-2, -1, black[-1]),
        -3: seconds[0] + across(-3, -2, black[-2]),
    }
    for j, value in more.items():
        res[j] = jnp.where(mask1(j) if j == 0 else mask1(j) & has_far, value, 0.0)

    put_rows(zmid, 2, 3.0 * (res[0] + res[1]) + (res[-1] + res[2]))
    put_rows(zmid, 3, 3.0 * (res[-1] + res[-2]) + (res[0] + res[-3]))
    parts = parts + restrict(zmid, 2, 2, ny2, weights2, 0.5 ** 12)
    for j in range(4):
        mid_ref[at1(j)] = red[j] + black[j]

    wait_recv(near, true, halo_c2, s_c2, r_c2)
    wait_recv(far, has_far, halo_c2, s_c2, r_c2)
    wait_recv(near, true, halo_3, s_3, r_3)

    def mask2(j):
        return parity(plane2, j + far + 4)

    def at2(j):
        return far + j * (1 - 2 * far)

    cof = {-1: halo_c2[far, 0], 0: cof2[at2(0)], 1: cof2[at2(1)], 2: halo_c2[near, 0]}
    dia = {
        -1: halo_c2[far, 1] + cof[0], 0: dia2[at2(0)] + cof[-1],
        1: dia2[at2(1)] + cof[2], 2: halo_c2[near, 1] + cof[1],
    }
    rhs = {
        -1: parts[3], 0: parts[2], 1: parts[0] + halo_3[near, 1], 2: halo_3[near, 0] + parts[1],
    }
    red = {j: jnp.where(mask2(j), 32.0 * rhs[j] / dia[j], 0.0) for j in rhs}
    red[-1] = inside * red[-1]
    for j in (0, 1):
        top = 32.0 * rhs[j] + flat(j, red[j]) + across(j, j - 1, red[j - 1]) + across(j, j + 1, red[j + 1])
        low_ref[at2(j)] = jnp.where(mask2(j), red[j], top / dia[j])

    def wait_sent(side, present, messages):
        @pl.when(present)
        def _():
            for src, dst, s_sem, r_sem in messages:
                copy_out(side, src, dst, s_sem, r_sem).wait_send()

    for side in range(2):
        wait_sent(side, has[side], (
            (send_a.at[side], halo_a, s_a, r_a),
            (send_d.at[side], halo_d, s_d, r_d),
            (send_q.at[side], halo_q, s_q, r_q),
            (send_c1.at[side], halo_c1, s_c1, r_c1),
            (send_c2.at[side], halo_c2, s_c2, r_c2),
            (send_2.at[side, 0:2], halo_2, s_2, r_2),
        ))
    wait_sent(near, true, (
        (send_2.at[near, 2], halo_n, s_n, r_n), (send_3, halo_3, s_3, r_3),
    ))
    wait_sent(far, has_far, ((send_2.at[far, 2:4], halo_f, s_f, r_f),))


def on_device(size, pressure_guess, source, conductance):
    nz, ny, nx = pressure_guess.shape
    pairs = nz // 2
    ny1, nx1, ny2, nx2 = ny // 2, nx // 2, ny // 4, nx // 4

    def vmem(*shape):
        return pltpu.VMEM(shape, F32)

    slab = [vmem(nz, ny, nx)] * 3
    padded = [vmem(pairs + 2, ny, nx)] * 6
    faces = [
        vmem(pairs, ny, nx), vmem(pairs, ny, nx), vmem(pairs, 4, ny, nx),
        vmem(pairs, ny, nx), vmem(pairs, 4, ny, nx),
    ]
    sums = [vmem(pairs, ny, nx)] * 3
    work = [
        vmem(pairs + 2, nx // 128, ny + 16, 128), vmem(4, nx1 // 128, ny1 + 16, 128),
        pltpu.VMEM((nx, nx1), BF16), pltpu.VMEM((nx, nx1), BF16),
        vmem(2, 5, ny1, nx1), vmem(2, ny, nx), vmem(pairs, ny1, nx1), vmem(pairs, ny1, nx1),
        vmem(2, ny2, nx2), vmem(2, ny2, nx2),
    ]
    messages = [
        vmem(2, ny, nx), vmem(2, 2, ny, nx), vmem(2, ny, nx), vmem(2, 6, ny1, nx1), vmem(2, 2, ny2, nx2),
    ]
    sent = messages + [vmem(2, 4, ny1, nx1), vmem(2, ny2, nx2)]
    halos = messages + [
        vmem(2, 2, ny1, nx1), vmem(2, ny1, nx1), vmem(2, 2, ny1, nx1), vmem(2, 2, ny2, nx2),
    ]
    sems = [pltpu.SemaphoreType.DMA((3,))] + [pltpu.SemaphoreType.DMA((2,))] * 18

    def run(*refs):
        kernel(size, *refs)

    shapes = ((nz, ny, nx), (pairs, ny1, nx1), (pairs // 2, ny2, nx2))
    inputs = [
        pltpu.with_memory_space_constraint(value, pltpu.HBM)
        for value in (pressure_guess, source, conductance)
    ]
    results = pl.pallas_call(
        run,
        out_shape=tuple(pltpu.VMEM(shape, F32) for shape in shapes),
        in_specs=[pl.BlockSpec(memory_space=pl.ANY)] * 3,
        out_specs=tuple([pl.BlockSpec(memory_space=pltpu.VMEM)] * 3),
        scratch_shapes=slab + padded + faces + sums + work + sent + halos + sems,
        compiler_params=pltpu.CompilerParams(
            collective_id=0, has_side_effects=True, vmem_limit_bytes=48 * 2 ** 20
        ),
    )(*inputs)
    return pl.pallas_call(
        write_out,
        out_shape=tuple(jax.ShapeDtypeStruct(shape, F32) for shape in shapes),
        in_specs=[pl.BlockSpec(memory_space=pl.ANY)] * 3,
        out_specs=tuple([pl.BlockSpec(memory_space=pl.ANY)] * 3),
        scratch_shapes=[pltpu.SemaphoreType.DMA((3,))],
    )(*[pltpu.with_memory_space_constraint(value, pltpu.VMEM) for value in results])


def write_out(p_src, mid_src, low_src, p_dst, mid_dst, low_dst, sem):
    copies = [
        pltpu.make_async_copy(src, dst, sem.at[i])
        for i, (src, dst) in enumerate(((p_src, p_dst), (mid_src, mid_dst), (low_src, low_dst)))
    ]
    for copy in copies:
        copy.start()
    for copy in copies:
        copy.wait()


def solution(mesh):
    size = mesh.shape["gz"]
    spec = P("gz", None, None)
    return jax.shard_map(
        lambda *args: on_device(size, *args), mesh=mesh,
        in_specs=(spec, spec, spec), out_specs=(spec, spec, spec), check_vma=False,
    )
```

```python
import jax
import jax.numpy as jnp
from jax import lax
from jax.experimental import pallas as pl
from jax.experimental.pallas import tpu as pltpu
from jax.sharding import PartitionSpec as P

F32 = jnp.float32
BF16 = jnp.bfloat16


def parity(shape, offset):
    rows = lax.broadcasted_iota(jnp.int32, shape, 0)
    cols = lax.broadcasted_iota(jnp.int32, shape, 1)
    return ((rows + cols + offset) & 1) == 0


def shifts(plane):
    ny, nx = plane.shape
    return (
        pltpu.roll(plane, ny - 1, 0),
        pltpu.roll(plane, 1, 0),
        pltpu.roll(plane, nx - 1, 1),
        pltpu.roll(plane, 1, 1),
    )


def insides(shape):
    rows = lax.broadcasted_iota(jnp.int32, shape, 0)
    cols = lax.broadcasted_iota(jnp.int32, shape, 1)
    return (rows < shape[0] - 1, rows > 0, cols < shape[1] - 1, cols > 0)


def side_faces(centre, other):
    faces, total = [], None
    for near, inside in zip(shifts(other), insides(centre.shape)):
        near = jnp.where(inside, near, 0.0)
        faces.append(jnp.where(inside, centre + near, 0.0))
        total = near if total is None else total + near
    return faces, total


def dot_parts(rows, weights):
    count = rows.shape[0]
    high = rows.astype(BF16)
    rest = rows - high.astype(F32)
    middle = rest.astype(BF16)
    low = (rest - middle.astype(F32)).astype(BF16)
    out = jnp.dot(
        jnp.concatenate([high, middle, low], axis=0), weights, preferred_element_type=F32
    )
    return out[:count] + (out[count : 2 * count] + out[2 * count :])


def weights_of(shape, inner, outer):
    fine = lax.broadcasted_iota(jnp.int32, shape, 0)
    coarse = lax.broadcasted_iota(jnp.int32, shape, 1)
    apart = fine - 2 * coarse
    near = (apart == 0) | (apart == 1)
    far = (apart == -1) | (apart == 2)
    return jnp.where(near, inner, jnp.where(far, outer, 0.0)).astype(BF16)


def kernel(
    size,
    g_hbm, b_hbm, c_hbm,
    p_ref, mid_ref, low_ref,
    craw, graw, braw,
    cr, cb, gb, rr, dl, rho,
    fpair, fro, frs, fbo, fbs,
    dr, db, nr,
    zbuf, zmid, wres, wsum,
    v1, topb, cof1, dia1,
    cof2, dia2,
    send_a, send_h, send_d, send_q, send_c1, send_c2, send_2, send_3,
    halo_a, halo_h, halo_d, halo_q, halo_c1, halo_c2, halo_2, halo_n, halo_f, halo_3,
    load_sem,
    s_a, s_h, s_d, s_q, s_c1, s_c2, s_2, s_n, s_f, s_3,
    r_a, r_h, r_d, r_q, r_c1, r_c2, r_2, r_n, r_f, r_3,
):
    me = lax.axis_index("gz")
    nz, ny, nx = craw.shape
    pairs = nz // 2
    plane = (ny, nx)
    plane1 = (ny // 2, nx // 2)
    plane2 = (ny // 4, nx // 4)
    has = (me > 0, me < size - 1)
    far = me % 2
    near = 1 - far
    has_far = jnp.where(far == 0, me, size - 1 - me) > 0

    barrier = pltpu.get_barrier_semaphore()
    for side in range(2):
        @pl.when(has[side])
        def _(side=side):
            pl.semaphore_signal(
                barrier, inc=1, device_id=(me + 2 * side - 1,),
                device_id_type=pl.DeviceIdType.MESH,
            )

    loads = [
        pltpu.make_async_copy(src, dst, load_sem.at[i])
        for i, (src, dst) in enumerate(((c_hbm, craw), (g_hbm, graw), (b_hbm, braw)))
    ]
    for load in loads:
        load.start()

    for ref in (cr, cb, gb, rr, dl, rho):
        ref[0] = jnp.zeros(plane, F32)
        ref[pairs + 1] = jnp.zeros(plane, F32)
    dl[1] = jnp.zeros(plane, F32)
    dl[pairs] = jnp.zeros(plane, F32)
    for ref, depth in ((zbuf, ny), (zmid, ny // 2)):
        for i in range(ref.shape[0]):
            for j in range(ref.shape[1]):
                ref[i, j, 0:8] = jnp.zeros((8, 128), F32)
                ref[i, j, depth + 8 : depth + 16] = jnp.zeros((8, 128), F32)
    for side in range(2):
        @pl.when(jnp.logical_not(has[side]))
        def _(side=side):
            for ref in (halo_a, halo_h, halo_d, halo_q):
                ref[side] = jnp.zeros(ref.shape[1:], F32)
            for ref in (halo_c1, halo_c2, halo_2, halo_f):
                for i in range(ref.shape[1]):
                    ref[side, i] = jnp.zeros(ref.shape[2:], F32)
    wres[...] = weights_of(wres.shape, 3.0, 1.0)
    wsum[...] = weights_of(wsum.shape, 1.0, 0.0)

    def copy_out(side, src, dst, s_sem, r_sem):
        return pltpu.make_async_remote_copy(
            src_ref=src, dst_ref=dst.at[1 - side], send_sem=s_sem.at[side],
            recv_sem=r_sem.at[1 - side], device_id=(me + 2 * side - 1,),
            device_id_type=pl.DeviceIdType.MESH,
        )

    def send(src_of, dst, s_sem, r_sem, allowed=True):
        for side in range(2):
            @pl.when(has[side] & allowed)
            def _(side=side):
                copy_out(side, src_of(side), dst, s_sem, r_sem).start()

    def wait_recv(side, present, dst, s_sem, r_sem):
        @pl.when(present)
        def _():
            pltpu.make_async_remote_copy(
                src_ref=dst.at[side], dst_ref=dst.at[side], send_sem=s_sem.at[side],
                recv_sem=r_sem.at[side], device_id=(me + 2 * side - 1,),
                device_id_type=pl.DeviceIdType.MESH,
            ).wait_recv()

    even = parity(plane, 0)

    def even_first(first, second):
        return jnp.where(parity(plane, 0), first, second)

    loads[0].wait()

    def put_rows(ref, k, value):
        for j in range(ref.shape[1]):
            ref[k, j, 8 : value.shape[0] + 8] = value[:, 128 * j : 128 * j + 128]

    def get_rows(ref, k, start, count):
        return jnp.concatenate(
            [ref[k, j, pl.ds(start, count, stride=2), :] for j in range(ref.shape[1])], axis=1
        )

    def pack(k, carry):
        low, high = craw[2 * k], craw[2 * k + 1]
        cr[k + 1] = even_first(low, high)
        cb[k + 1] = even_first(high, low)
        put_rows(zbuf, k, low + high)
        return carry

    lax.fori_loop(0, pairs, pack, 0)

    def faces(k, carry):
        own, other = cr[k + 1], cb[k + 1]
        fpair[k] = own + other
        outer = even_first(cb[k], cb[k + 2])
        sides, total = side_faces(own, other)
        fro[k] = own + outer
        for i in range(4):
            frs[k, i] = sides[i]
        dr[k] = 6.0 * own + other + outer + total
        outer = even_first(cr[k + 2], cr[k])
        sides, total = side_faces(other, own)
        fbo[k] = other + outer
        for i in range(4):
            fbs[k, i] = sides[i]
        db[k] = 6.0 * other + own + outer + total
        return carry

    def gather(k, centre, outer, f_outer, f_sides):
        total = fpair[k] * centre + f_outer[k] * outer
        for i, near in enumerate(shifts(centre)):
            total = total + f_sides[k, i] * near
        return total

    def pack_g(k, carry):
        gb[k + 1] = even_first(graw[2 * k + 1], graw[2 * k])
        return carry

    def red(k, carry):
        rhs = even_first(braw[2 * k], braw[2 * k + 1])
        off = gather(k, gb[k + 1], even_first(gb[k], gb[k + 2]), fro, frs)
        top = 2.0 * rhs + off
        nr[k] = top
        rr[k + 1] = top / dr[k]
        return carry

    def put_first(side, carry):
        here = (nz - 1) * side
        send_a[side] = jnp.where(parity(plane, side), pltpu.roll(craw[here], 1, 0), graw[here])
        return carry

    def put_diagonal(side, carry):
        k = (pairs - 1) * side
        mine = parity(plane, side)
        send_d[side] = jnp.where(mine, dr[k], fpair[k])
        coef = craw[(nz - 1) * side]
        half = ny // 2
        send_h[side] = jnp.where(
            parity((half, nx), side), coef[:half], pltpu.roll(coef[half:], 1, 0)
        )
        return carry

    def put_tops(side, carry):
        k = (pairs - 1) * side
        rhs = even_first(braw[2 * k + 1], braw[2 * k])
        send_q[side] = jnp.where(parity(plane, side), nr[k], 2.0 * rhs + fpair[k] * rr[k + 1])
        return carry

    def at_ends(body):
        lax.fori_loop(0, 2, lambda i, carry: body((pairs - 1) * i, carry), 0)

    def enter(allowed):
        @pl.when(allowed)
        def _():
            pl.semaphore_wait(barrier, jnp.where(has[0] & has[1], 2, 1))

    odd = far == 1
    at_ends(faces)
    lax.fori_loop(0, 2, put_diagonal, 0)
    enter(odd)
    send(lambda side: send_h.at[side], halo_h, s_h, r_h, odd)
    send(lambda side: send_d.at[side], halo_d, s_d, r_d, odd)
    loads[1].wait()
    lax.fori_loop(0, 2, put_first, 0)
    send(lambda side: send_a.at[side], halo_a, s_a, r_a, odd)
    lax.fori_loop(0, pairs, pack_g, 0)
    loads[2].wait()
    at_ends(red)
    lax.fori_loop(0, 2, put_tops, 0)
    send(lambda side: send_q.at[side], halo_q, s_q, r_q, odd)
    even_core = far == 0
    enter(even_core)
    send(lambda side: send_a.at[side], halo_a, s_a, r_a, even_core)
    send(lambda side: send_h.at[side], halo_h, s_h, r_h, even_core)
    send(lambda side: send_d.at[side], halo_d, s_d, r_d, even_core)
    send(lambda side: send_q.at[side], halo_q, s_q, r_q, even_core)

    lax.fori_loop(1, pairs - 1, faces, 0)
    lax.fori_loop(1, pairs - 1, red, 0)

    def put_pressure(k, reds, blacks):
        p_ref[2 * k] = even_first(reds, blacks)
        p_ref[2 * k + 1] = even_first(blacks, reds)

    def black(k, carry):
        rhs = even_first(braw[2 * k + 1], braw[2 * k])
        reds = rr[k + 1]
        off = gather(k, reds, even_first(rr[k + 2], rr[k]), fbo, fbs)
        new = (2.0 * rhs + off) / db[k]
        dl[k + 1] = new - gb[k + 1]
        put_pressure(k, reds, new)
        return carry

    lax.fori_loop(1, pairs - 1, black, 0)

    def residual(k, carry):
        rho[k + 1] = gather(k, dl[k + 1], even_first(dl[k], dl[k + 2]), fro, frs)
        return carry

    lax.fori_loop(1, pairs - 1, residual, 0)

    ny1, ny2 = ny // 2, ny // 4
    rows = [
        get_rows(zbuf, k, 8, ny1) + get_rows(zbuf, k, 9, ny1)
        for k in range(pairs)
    ]
    sums = 0.125 * dot_parts(jnp.concatenate(rows, axis=0), wsum[...])
    c1 = [sums[k * ny1 : (k + 1) * ny1] for k in range(pairs)]

    def plane_sum(value):
        total = None
        for near, inside in zip(shifts(value), insides(value.shape)):
            near = jnp.where(inside, near, 0.0)
            total = near if total is None else total + near
        return total

    def diagonals(coefs):
        out = []
        for k, coef in enumerate(coefs):
            total = 6.0 * coef + plane_sum(coef)
            if k > 0:
                total = total + coefs[k - 1]
            if k < len(coefs) - 1:
                total = total + coefs[k + 1]
            out.append(total)
        return out

    d1 = diagonals(c1)
    for k in range(pairs):
        cof1[k] = c1[k]
        dia1[k] = d1[k]
    for k in range(pairs // 2):
        put_rows(zmid, k, c1[2 * k] + c1[2 * k + 1])
    rows = [
        get_rows(zmid, k, 8, ny2) + get_rows(zmid, k, 9, ny2)
        for k in range(pairs // 2)
    ]
    weights = wsum[0 : nx // 2, 0 : nx // 4]
    sums = 0.125 * dot_parts(jnp.concatenate(rows, axis=0), weights)
    c2 = [sums[k * ny2 : (k + 1) * ny2] for k in range(pairs // 2)]
    d2 = diagonals(c2)
    for k in range(2):
        cof2[k] = c2[k]
        dia2[k] = d2[k]
    for side in range(2):
        ends = (3 * side, 1 + side, 2 - side)
        for i, end in enumerate(ends):
            send_c1[side, i] = c1[end]
        send_c1[side, 3] = d1[ends[2]]
        send_c2[side, 0] = c2[side]
        send_c2[side, 1] = d2[side]
    send(lambda side: send_c1.at[side], halo_c1, s_c1, r_c1)
    send(lambda side: send_c2.at[side], halo_c2, s_c2, r_c2)

    def restrict(ref, first, count, out_rows, weights, scale):
        rows = [
            (get_rows(ref, k, 7, out_rows) + get_rows(ref, k, 10, out_rows))
            + 3.0 * (get_rows(ref, k, 8, out_rows) + get_rows(ref, k, 9, out_rows))
            for k in range(first, first + count)
        ]
        out = scale * dot_parts(jnp.concatenate(rows, axis=0), weights)
        return [out[k * out_rows : (k + 1) * out_rows] for k in range(count)]

    def first_stage(side, present, is_near):
        wait_recv(side, present, halo_a, s_a, r_a)
        k = (pairs - 1) * side
        mine = parity(plane, side)
        field = halo_a[side]
        coef = pltpu.roll(field, ny - 1, 0)
        face = craw[(nz - 1) * side] + coef
        value = (nr[k] + face * field) / (dr[k] + coef)
        reds = jnp.where(mine, value, rr[k + 1])
        rr[k + 1] = reds
        rhs = even_first(braw[2 * k + 1], braw[2 * k])
        top = 2.0 * rhs + gather(k, reds, even_first(rr[k + 2], rr[k]), fbo, fbs)
        topb[side] = top
        new = top / db[k]
        delta = new - gb[k + 1]
        dl[k + 1] = delta
        put_pressure(k, reds, new)
        own = gather(k, delta, even_first(dl[k], dl[k + 2]), fro, frs)
        rho[k + 1] = own
        inner = k + 1 - 2 * side
        more = (cr[inner + 1] + cb[k + 1]) * delta
        rho[inner + 1] = rho[inner + 1] + jnp.where(mine, more, 0.0)

        def along_z(at):
            return 3.0 * rho[at + 1] + even_first(rho[at + 2], rho[at])

        put_rows(zbuf, 0, along_z(k))
        put_rows(zbuf, 1, jnp.where(mine, own, 0.0))
        parts = restrict(zbuf, 0, 2, ny1, wres[...], 0.5 ** 10)
        send_2[side, 0] = parts[0]
        send_2[side, 1] = parts[1]

        @pl.when(present)
        def _():
            copy_out(side, send_2.at[side, 0:2], halo_2, s_2, r_2).start()

        v1[side, 0] = parts[0]
        v1[side, 2] = parts[1]
        put_rows(zbuf, 2, along_z(inner))
        (middle,) = restrict(zbuf, 2, 1, ny1, wres[...], 0.5 ** 10)
        v1[side, 1] = middle
        if is_near:
            send_2[side, 2] = (cof1[k] + cof1[inner]) * (8.0 * middle / dia1[inner])
            copy_out(side, send_2.at[side, 2], halo_n, s_n, r_n).start()

    def second_stage(side, present):
        wait_recv(side, present, halo_h, s_h, r_h)
        wait_recv(side, present, halo_d, s_d, r_d)
        wait_recv(side, present, halo_q, s_q, r_q)
        k = (pairs - 1) * side
        here = (nz - 1) * side
        mine = parity(plane, side)
        black_there = mine & present
        field = halo_a[side]
        half, mixed, tops = halo_h[side], halo_d[side], halo_q[side]
        c0, g0 = craw[here], graw[here]
        half = jnp.concatenate([half, pltpu.roll(half, ny // 2 - 1, 0)], axis=0)
        hc = jnp.where(mine, pltpu.roll(field, ny - 1, 0), half)
        face = c0 + hc
        value = jnp.where(present, (tops + face * g0) / (mixed + c0), 0.0)
        sides, around = side_faces(hc, hc)
        diagonal = 5.0 * hc + around + mixed
        short = tops
        for f, shifted in zip(sides, shifts(value)):
            short = short + f * shifted
        reds = rr[k + 1]
        new = (jnp.where(mine, short, topb[side]) + face * jnp.where(mine, reds, value)) / (
            jnp.where(mine, diagonal + c0, db[k] + hc)
        )
        old = dl[k + 1]
        delta = new - gb[k + 1]
        change = jnp.where(mine, 0.0, delta - old)
        dl[k + 1] = jnp.where(mine, old, delta)
        p_ref[here] = jnp.where(mine, reds, new)
        delta_there = jnp.where(black_there, new - field, 0.0)
        change_there = jnp.where(black_there, new - short / diagonal, 0.0)
        add = fpair[k] * change
        for i, shifted in enumerate(shifts(change)):
            add = add + frs[k, i] * shifted
        put_rows(zbuf, 0, jnp.where(mine, add + face * delta_there, 0.0))
        put_rows(zbuf, 1, jnp.where(mine, 0.0, add))
        add = face * delta
        for f, shifted in zip(sides, shifts(change_there)):
            add = add + f * shifted
        put_rows(zbuf, 2, jnp.where(mine | jnp.logical_not(present), 0.0, add))
        put_rows(zbuf, 3, jnp.where(black_there, mixed * change_there, 0.0))
        parts = restrict(zbuf, 0, 4, ny1, wres[...], 0.5 ** 10)
        v1[side, 0] = v1[side, 0] + 3.0 * (parts[0] + parts[1])
        v1[side, 1] = v1[side, 1] + parts[1]
        v1[side, 2] = v1[side, 2] + parts[0]
        v1[side, 3] = parts[2]
        v1[side, 4] = parts[3]

    true = me >= 0
    first_stage(near, true, True)
    second_stage(near, true)

    def mask1(j):
        return parity(plane1, j + far + 4)

    def at1(j):
        return 3 * far + j * (1 - 2 * far)

    cof = {j: cof1[at1(j)] for j in range(4)}
    dia = {j: dia1[at1(j)] for j in range(4)}
    fac, for_red, for_black = {}, {}, {}

    def prepare(j, mask, factor, present=None):
        fac[j] = side_faces(cof[j], cof[j])[0]
        if j in dia:
            for_red[j] = jnp.where(mask, factor / dia[j], 0.0)
            for_black[j] = jnp.where(mask, 0.0, 1.0 / dia[j])
            if present is not None:
                for_red[j] = jnp.where(present, for_red[j], 0.0)
                for_black[j] = jnp.where(present, for_black[j], 0.0)

    def flat(j, field):
        total = None
        for face, shifted in zip(fac[j], shifts(field)):
            term = face * shifted
            total = term if total is None else total + term
        return total

    def across(i, j, field):
        return (cof[i] + cof[j]) * field

    def red_of(j, right):
        return for_red[j] * right

    def black_of(j, top):
        return for_black[j] * top

    wait_recv(near, true, halo_c1, s_c1, r_c1)
    def diagonal_of(j):
        return 6.0 * cof[j] + plane_sum(cof[j]) + (cof[j - 1] + cof[j + 1])

    cof.update({4 + i: halo_c1[near, i] for i in range(3)})
    dia.update({3: dia[3] + cof[4], 4: diagonal_of(4), 5: diagonal_of(5)})
    for j in (1, 2, 3, 4, 5):
        prepare(j, mask1(j), 8.0)
    wait_recv(near, true, halo_2, s_2, r_2)
    wait_recv(near, true, halo_n, s_n, r_n)
    rhs = {
        4: halo_2[near, 0] + 3.0 * (v1[near, 3] + v1[near, 4]) + v1[near, 2],
        3: v1[near, 0] + (halo_2[near, 1] + v1[near, 3]),
        2: v1[near, 1],
    }
    red = {j: red_of(j, rhs[j]) for j in (2, 3, 4)}
    black = {}
    beyond = halo_n[near] + across(4, 5, red_of(5, v1[near, 4]))
    black[4] = black_of(4, 8.0 * rhs[4] + beyond + flat(4, red[4]) + across(4, 3, red[3]))
    black[3] = black_of(
        3, 8.0 * rhs[3] + flat(3, red[3]) + across(3, 4, red[4]) + across(3, 2, red[2])
    )
    base1 = across(1, 2, red[2])
    base2 = 8.0 * rhs[2] + flat(2, red[2]) + across(2, 3, red[3])
    base3 = across(2, 3, black[3])

    def middle():
        right = v1[far, 1]
        red1 = red_of(1, right)
        black2 = black_of(2, base2 + across(2, 1, red1))
        part1 = 8.0 * right + flat(1, red1) + base1
        part2 = flat(2, black2) + base3
        return red1, black2, part1, part2, across(1, 2, black2)

    first_stage(far, has_far, False)
    red1, black2, part1, part2, cross = middle()
    send_2[far, 2] = jnp.where(mask1(0), part2, across(0, 1, red1))
    send_2[far, 3] = jnp.where(mask1(1), cross, part1)

    @pl.when(has_far)
    def _():
        copy_out(far, send_2.at[far, 2:4], halo_f, s_f, r_f).start()

    second_stage(far, has_far)
    red[1], black[2], part1, part2, cross = middle()
    wait_recv(far, has_far, halo_c1, s_c1, r_c1)
    cof.update({-1 - i: halo_c1[far, i] for i in range(3)})
    dia.update({
        -1: diagonal_of(-1), -2: diagonal_of(-2), -3: halo_c1[far, 3], 0: dia[0] + cof[-1],
    })
    prepare(0, mask1(0), 8.0)
    for j in (-1, -2, -3):
        prepare(j, mask1(j), 8.0, has_far)
    there1, there2 = v1[far, 3], v1[far, 4]
    more_red = red_of(-2, there2)
    more_black = black_of(-3, across(-3, -2, more_red))
    fix1 = jnp.where(mask1(-1), flat(-3, more_black), across(-1, -2, more_red))
    fix2 = jnp.where(mask1(-2), across(-2, -3, more_black), 8.0 * there2 + flat(-2, more_red))
    base0 = across(0, 1, red[1])
    end0 = v1[far, 0] + there1
    end1 = 3.0 * (there1 + there2) + v1[far, 2]
    wait_recv(near, true, halo_c2, s_c2, r_c2)
    wait_recv(far, has_far, halo_c2, s_c2, r_c2)

    def mask2(j):
        return parity(plane2, j + far + 4)

    def at2(j):
        return far + j * (1 - 2 * far)

    levels = cof, dia, fac, for_red, for_black
    cof = {-1: halo_c2[far, 0], 0: cof2[at2(0)], 1: cof2[at2(1)], 2: halo_c2[near, 0]}
    dia = {
        -1: halo_c2[far, 1] + cof[0], 0: dia2[at2(0)] + cof[-1],
        1: dia2[at2(1)] + cof[2], 2: halo_c2[near, 1] + cof[1],
    }
    fac, for_red, for_black = {}, {}, {}
    for j in (0, 1, 2):
        prepare(j, mask2(j), 32.0)
    prepare(-1, mask2(-1), 32.0, has_far)
    low_cof, low_fac, low_red, low_black = cof, fac, for_red, for_black
    cof, dia, fac, for_red, for_black = levels

    wait_recv(far, has_far, halo_2, s_2, r_2)
    rhs[0] = halo_2[far, 1] + end0
    rhs[-1] = halo_2[far, 0] + end1
    red[0] = red_of(0, rhs[0])
    red[-1] = red_of(-1, rhs[-1])
    black[0] = black_of(0, 8.0 * rhs[0] + base0 + across(0, -1, red[-1]) + flat(0, red[0]))
    black[1] = black_of(1, part1 + across(1, 0, red[0]))
    res = {
        3: flat(3, black[3]) + across(3, 2, black[2]) + across(3, 4, black[4]),
        2: part2 + across(2, 1, black[1]),
        1: flat(1, black[1]) + across(1, 0, black[0]) + cross,
    }
    res = {j: jnp.where(mask1(j), value, 0.0) for j, value in res.items()}
    weights2 = wres[0 : nx // 2, 0 : nx // 4]
    put_rows(zmid, 0, 3.0 * (res[3] + res[2]) + res[1])
    put_rows(zmid, 1, res[3])
    parts = restrict(zmid, 0, 2, ny2, weights2, 0.5 ** 12)
    send_3[0] = parts[0]
    send_3[1] = parts[1]
    copy_out(near, send_3, halo_3, s_3, r_3).start()

    wait_recv(far, has_far, halo_f, s_f, r_f)
    seconds = (halo_f[far, 0] + fix1, halo_f[far, 1] + fix2)
    black[-1] = black_of(-1, 8.0 * rhs[-1] + seconds[0] + flat(-1, red[-1]) + across(-1, 0, red[0]))
    black[-2] = black_of(-2, seconds[1] + across(-2, -1, red[-1]))
    more = {
        0: flat(0, black[0]) + across(0, -1, black[-1]) + across(0, 1, black[1]),
        -1: flat(-1, black[-1]) + across(-1, -2, black[-2]) + across(-1, 0, black[0]),
        -2: seconds[1] + flat(-2, black[-2]) + across(-2, -1, black[-1]),
        -3: seconds[0] + across(-3, -2, black[-2]),
    }
    for j, value in more.items():
        res[j] = jnp.where(mask1(j) if j == 0 else mask1(j) & has_far, value, 0.0)

    put_rows(zmid, 2, 3.0 * (res[0] + res[1]) + (res[-1] + res[2]))
    put_rows(zmid, 3, 3.0 * (res[-1] + res[-2]) + (res[0] + res[-3]))
    parts = parts + restrict(zmid, 2, 2, ny2, weights2, 0.5 ** 12)
    for j in range(4):
        mid_ref[at1(j)] = red[j] + black[j]

    cof, fac, for_red, for_black = low_cof, low_fac, low_red, low_black
    rhs = {-1: parts[3], 0: parts[2]}
    red = {j: red_of(j, rhs[j]) for j in (-1, 0)}
    base0 = 32.0 * rhs[0] + flat(0, red[0]) + across(0, -1, red[-1])
    base1 = across(1, 0, red[0])
    wait_recv(near, true, halo_3, s_3, r_3)
    rhs.update({1: parts[0] + halo_3[near, 1], 2: halo_3[near, 0] + parts[1]})
    red.update({j: red_of(j, rhs[j]) for j in (1, 2)})
    low_ref[at2(0)] = red[0] + black_of(0, base0 + across(0, 1, red[1]))
    low_ref[at2(1)] = red[1] + black_of(
        1, 32.0 * rhs[1] + base1 + across(1, 2, red[2]) + flat(1, red[1])
    )

    def wait_sent(side, present, messages):
        @pl.when(present)
        def _():
            for src, dst, s_sem, r_sem in messages:
                copy_out(side, src, dst, s_sem, r_sem).wait_send()

    for side in range(2):
        wait_sent(side, has[side], (
            (send_a.at[side], halo_a, s_a, r_a),
            (send_h.at[side], halo_h, s_h, r_h),
            (send_d.at[side], halo_d, s_d, r_d),
            (send_q.at[side], halo_q, s_q, r_q),
            (send_c1.at[side], halo_c1, s_c1, r_c1),
            (send_c2.at[side], halo_c2, s_c2, r_c2),
            (send_2.at[side, 0:2], halo_2, s_2, r_2),
        ))
    wait_sent(near, true, (
        (send_2.at[near, 2], halo_n, s_n, r_n), (send_3, halo_3, s_3, r_3),
    ))
    wait_sent(far, has_far, ((send_2.at[far, 2:4], halo_f, s_f, r_f),))


def on_device(size, pressure_guess, source, conductance):
    nz, ny, nx = pressure_guess.shape
    pairs = nz // 2
    ny1, nx1, ny2, nx2 = ny // 2, nx // 2, ny // 4, nx // 4

    def vmem(*shape):
        return pltpu.VMEM(shape, F32)

    slab = [vmem(nz, ny, nx)] * 3
    padded = [vmem(pairs + 2, ny, nx)] * 6
    faces = [
        vmem(pairs, ny, nx), vmem(pairs, ny, nx), vmem(pairs, 4, ny, nx),
        vmem(pairs, ny, nx), vmem(pairs, 4, ny, nx),
    ]
    sums = [vmem(pairs, ny, nx)] * 3
    work = [
        vmem(pairs + 2, nx // 128, ny + 16, 128), vmem(4, nx1 // 128, ny1 + 16, 128),
        pltpu.VMEM((nx, nx1), BF16), pltpu.VMEM((nx, nx1), BF16),
        vmem(2, 5, ny1, nx1), vmem(2, ny, nx), vmem(pairs, ny1, nx1), vmem(pairs, ny1, nx1),
        vmem(2, ny2, nx2), vmem(2, ny2, nx2),
    ]
    messages = [
        vmem(2, ny, nx), vmem(2, ny1, nx), vmem(2, ny, nx), vmem(2, ny, nx), vmem(2, 4, ny1, nx1), vmem(2, 2, ny2, nx2),
    ]
    sent = messages + [vmem(2, 4, ny1, nx1), vmem(2, ny2, nx2)]
    halos = messages + [
        vmem(2, 2, ny1, nx1), vmem(2, ny1, nx1), vmem(2, 2, ny1, nx1), vmem(2, 2, ny2, nx2),
    ]
    sems = [pltpu.SemaphoreType.DMA((3,))] + [pltpu.SemaphoreType.DMA((2,))] * 20

    def run(*refs):
        kernel(size, *refs)

    shapes = ((nz, ny, nx), (pairs, ny1, nx1), (pairs // 2, ny2, nx2))
    inputs = [
        pltpu.with_memory_space_constraint(value, pltpu.HBM)
        for value in (pressure_guess, source, conductance)
    ]
    results = pl.pallas_call(
        run,
        out_shape=tuple(pltpu.VMEM(shape, F32) for shape in shapes),
        in_specs=[pl.BlockSpec(memory_space=pl.ANY)] * 3,
        out_specs=tuple([pl.BlockSpec(memory_space=pltpu.VMEM)] * 3),
        scratch_shapes=slab + padded + faces + sums + work + sent + halos + sems,
        compiler_params=pltpu.CompilerParams(
            collective_id=0, has_side_effects=True, vmem_limit_bytes=48 * 2 ** 20
        ),
    )(*inputs)
    return pl.pallas_call(
        write_out,
        out_shape=tuple(jax.ShapeDtypeStruct(shape, F32) for shape in shapes),
        in_specs=[pl.BlockSpec(memory_space=pl.ANY)] * 3,
        out_specs=tuple([pl.BlockSpec(memory_space=pl.ANY)] * 3),
        scratch_shapes=[pltpu.SemaphoreType.DMA((3,))],
    )(*[pltpu.with_memory_space_constraint(value, pltpu.VMEM) for value in results])


def write_out(p_src, mid_src, low_src, p_dst, mid_dst, low_dst, sem):
    copies = [
        pltpu.make_async_copy(src, dst, sem.at[i])
        for i, (src, dst) in enumerate(((p_src, p_dst), (mid_src, mid_dst), (low_src, low_dst)))
    ]
    for copy in copies:
        copy.start()
    for copy in copies:
        copy.wait()


def solution(mesh):
    size = mesh.shape["gz"]
    spec = P("gz", None, None)
    return jax.shard_map(
        lambda *args: on_device(size, *args), mesh=mesh,
        in_specs=(spec, spec, spec), out_specs=(spec, spec, spec), check_vma=False,
    )
```

```python
import jax
import jax.numpy as jnp
from jax import lax
from jax.experimental import pallas as pl
from jax.experimental.pallas import tpu as pltpu
from jax.sharding import PartitionSpec as P

F32 = jnp.float32
BF16 = jnp.bfloat16


def parity(shape, offset):
    rows = lax.broadcasted_iota(jnp.int32, shape, 0)
    cols = lax.broadcasted_iota(jnp.int32, shape, 1)
    return ((rows + cols + offset) & 1) == 0


def shifts(plane):
    ny, nx = plane.shape
    return (
        pltpu.roll(plane, ny - 1, 0),
        pltpu.roll(plane, 1, 0),
        pltpu.roll(plane, nx - 1, 1),
        pltpu.roll(plane, 1, 1),
    )


def insides(shape):
    rows = lax.broadcasted_iota(jnp.int32, shape, 0)
    cols = lax.broadcasted_iota(jnp.int32, shape, 1)
    return (rows < shape[0] - 1, rows > 0, cols < shape[1] - 1, cols > 0)


def side_faces(centre, other):
    faces, total = [], None
    for near, inside in zip(shifts(other), insides(centre.shape)):
        near = jnp.where(inside, near, 0.0)
        faces.append(jnp.where(inside, centre + near, 0.0))
        total = near if total is None else total + near
    return faces, total


def dot_parts(rows, weights):
    count = rows.shape[0]
    high = rows.astype(BF16)
    rest = rows - high.astype(F32)
    middle = rest.astype(BF16)
    low = (rest - middle.astype(F32)).astype(BF16)
    out = jnp.dot(
        jnp.concatenate([high, middle, low], axis=0), weights, preferred_element_type=F32
    )
    return out[:count] + (out[count : 2 * count] + out[2 * count :])


def weights_of(shape, inner, outer):
    fine = lax.broadcasted_iota(jnp.int32, shape, 0)
    coarse = lax.broadcasted_iota(jnp.int32, shape, 1)
    apart = fine - 2 * coarse
    near = (apart == 0) | (apart == 1)
    far = (apart == -1) | (apart == 2)
    return jnp.where(near, inner, jnp.where(far, outer, 0.0)).astype(BF16)


def kernel(
    size,
    g_hbm, b_hbm, c_hbm,
    p_ref, mid_ref, low_ref,
    craw, graw, braw,
    cr, cb, gb, rr, dl, rho,
    fpair, fro, frs, fbo, fbs,
    dr, db, nr,
    zbuf, zmid, wres, wsum,
    v1, topb, hsum, hside, c1_there, cof1, dia1,
    cof2, dia2,
    send_x, send_q, send_c1, send_c2, send_2, send_3,
    halo_c, halo_x, halo_q, halo_c1, halo_c2, halo_2, halo_n, halo_f, halo_3,
    load_sem,
    s_c, s_x, s_q, s_c1, s_c2, s_2, s_n, s_f, s_3,
    r_c, r_x, r_q, r_c1, r_c2, r_2, r_n, r_f, r_3,
):
    me = lax.axis_index("gz")
    nz, ny, nx = craw.shape
    pairs = nz // 2
    plane = (ny, nx)
    plane1 = (ny // 2, nx // 2)
    plane2 = (ny // 4, nx // 4)
    has = (me > 0, me < size - 1)
    far = me % 2
    near = 1 - far
    has_far = jnp.where(far == 0, me, size - 1 - me) > 0

    barrier = pltpu.get_barrier_semaphore()
    for side in range(2):
        @pl.when(has[side])
        def _(side=side):
            pl.semaphore_signal(
                barrier, inc=1, device_id=(me + 2 * side - 1,),
                device_id_type=pl.DeviceIdType.MESH,
            )

    loads = [
        pltpu.make_async_copy(src, dst, load_sem.at[i])
        for i, (src, dst) in enumerate(((c_hbm, craw), (g_hbm, graw), (b_hbm, braw)))
    ]
    for load in loads:
        load.start()

    def copy_out(side, src, dst, s_sem, r_sem):
        return pltpu.make_async_remote_copy(
            src_ref=src, dst_ref=dst.at[1 - side], send_sem=s_sem.at[side],
            recv_sem=r_sem.at[1 - side], device_id=(me + 2 * side - 1,),
            device_id_type=pl.DeviceIdType.MESH,
        )

    def send(src_of, dst, s_sem, r_sem, allowed=True):
        for side in range(2):
            @pl.when(has[side] & allowed)
            def _(side=side):
                copy_out(side, src_of(side), dst, s_sem, r_sem).start()

    def wait_recv(side, present, dst, s_sem, r_sem):
        @pl.when(present)
        def _():
            pltpu.make_async_remote_copy(
                src_ref=dst.at[side], dst_ref=dst.at[side], send_sem=s_sem.at[side],
                recv_sem=r_sem.at[side], device_id=(me + 2 * side - 1,),
                device_id_type=pl.DeviceIdType.MESH,
            ).wait_recv()

    def enter(allowed):
        @pl.when(allowed)
        def _():
            pl.semaphore_wait(barrier, jnp.where(has[0] & has[1], 2, 1))

    def send_coefficients(allowed):
        send(lambda side: c_hbm.at[pl.ds((nz - 2) * side, 2)], halo_c, s_c, r_c, allowed)

    odd, even_core = far == 1, far == 0
    enter(odd)
    send_coefficients(odd)

    for ref in (cr, cb, gb, rr, dl, rho):
        ref[0] = jnp.zeros(plane, F32)
        ref[pairs + 1] = jnp.zeros(plane, F32)
    for ref, depth in ((zbuf, ny), (zmid, ny // 2)):
        for i in range(ref.shape[0]):
            for j in range(ref.shape[1]):
                ref[i, j, 0:8] = jnp.zeros((8, 128), F32)
                ref[i, j, depth + 8 : depth + 16] = jnp.zeros((8, 128), F32)
    for side in range(2):
        @pl.when(jnp.logical_not(has[side]))
        def _(side=side):
            for ref in (halo_x, halo_q, halo_c2):
                ref[side] = jnp.zeros(ref.shape[1:], F32)
            for ref in (halo_c, halo_c1, halo_2, halo_f):
                for i in range(ref.shape[1]):
                    ref[side, i] = jnp.zeros(ref.shape[2:], F32)
    wres[...] = weights_of(wres.shape, 3.0, 1.0)
    wsum[...] = weights_of(wsum.shape, 1.0, 0.0)

    even = parity(plane, 0)

    def even_first(first, second):
        return jnp.where(parity(plane, 0), first, second)

    loads[0].wait()

    def put_rows(ref, k, value):
        for j in range(ref.shape[1]):
            ref[k, j, 8 : value.shape[0] + 8] = value[:, 128 * j : 128 * j + 128]

    def get_rows(ref, k, start, count):
        return jnp.concatenate(
            [ref[k, j, pl.ds(start, count, stride=2), :] for j in range(ref.shape[1])], axis=1
        )

    def pack(k, carry):
        low, high = craw[2 * k], craw[2 * k + 1]
        cr[k + 1] = even_first(low, high)
        cb[k + 1] = even_first(high, low)
        put_rows(zbuf, k, low + high)
        return carry

    lax.fori_loop(0, pairs, pack, 0)

    def faces(k, carry):
        own, other = cr[k + 1], cb[k + 1]
        fpair[k] = own + other
        outer = even_first(cb[k], cb[k + 2])
        sides, total = side_faces(own, other)
        fro[k] = own + outer
        for i in range(4):
            frs[k, i] = sides[i]
        dr[k] = 6.0 * own + other + outer + total
        outer = even_first(cr[k + 2], cr[k])
        sides, total = side_faces(other, own)
        fbo[k] = other + outer
        for i in range(4):
            fbs[k, i] = sides[i]
        db[k] = 6.0 * other + own + outer + total
        return carry

    def gather(k, centre, outer, f_outer, f_sides):
        total = fpair[k] * centre + f_outer[k] * outer
        for i, near in enumerate(shifts(centre)):
            total = total + f_sides[k, i] * near
        return total

    def pack_g(k, carry):
        gb[k + 1] = even_first(graw[2 * k + 1], graw[2 * k])
        return carry

    def red(k, carry):
        rhs = even_first(braw[2 * k], braw[2 * k + 1])
        off = gather(k, gb[k + 1], even_first(gb[k], gb[k + 2]), fro, frs)
        top = 2.0 * rhs + off
        nr[k] = top
        rr[k + 1] = top / dr[k]
        return carry

    def put_mixed(side, carry):
        send_x[side] = jnp.where(parity(plane, side), craw[2 + (nz - 5) * side], graw[(nz - 1) * side])
        return carry

    def put_tops(side, carry):
        k = (pairs - 1) * side
        rhs = even_first(braw[2 * k + 1], braw[2 * k])
        send_q[side] = jnp.where(parity(plane, side), nr[k], 2.0 * rhs + fpair[k] * rr[k + 1])
        return carry

    def at_ends(body):
        lax.fori_loop(0, 2, lambda i, carry: body((pairs - 1) * i, carry), 0)

    at_ends(faces)
    loads[1].wait()
    lax.fori_loop(0, 2, put_mixed, 0)
    send(lambda side: send_x.at[side], halo_x, s_x, r_x, odd)
    lax.fori_loop(0, pairs, pack_g, 0)
    loads[2].wait()
    at_ends(red)
    lax.fori_loop(0, 2, put_tops, 0)
    send(lambda side: send_q.at[side], halo_q, s_q, r_q, odd)
    enter(even_core)
    send_coefficients(even_core)
    send(lambda side: send_x.at[side], halo_x, s_x, r_x, even_core)
    send(lambda side: send_q.at[side], halo_q, s_q, r_q, even_core)

    lax.fori_loop(1, pairs - 1, faces, 0)
    lax.fori_loop(1, pairs - 1, red, 0)

    def put_pressure(k, reds, blacks):
        p_ref[2 * k] = even_first(reds, blacks)
        p_ref[2 * k + 1] = even_first(blacks, reds)

    def black(k, carry):
        rhs = even_first(braw[2 * k + 1], braw[2 * k])
        reds = rr[k + 1]
        top = 2.0 * rhs + gather(k, reds, even_first(rr[k + 2], rr[k]), fbo, fbs)
        topb[k] = top
        new = top / db[k]
        dl[k + 1] = new - gb[k + 1]
        put_pressure(k, reds, new)
        return carry

    lax.fori_loop(0, pairs, black, 0)

    def residual(k, carry):
        rho[k + 1] = gather(k, dl[k + 1], even_first(dl[k], dl[k + 2]), fro, frs)
        return carry

    lax.fori_loop(0, pairs, residual, 0)

    ny1, ny2 = ny // 2, ny // 4
    rows = [
        get_rows(zbuf, k, 8, ny1) + get_rows(zbuf, k, 9, ny1)
        for k in range(pairs)
    ]
    sums = 0.125 * dot_parts(jnp.concatenate(rows, axis=0), wsum[...])
    c1 = [sums[k * ny1 : (k + 1) * ny1] for k in range(pairs)]

    def plane_sum(value):
        total = None
        for near, inside in zip(shifts(value), insides(value.shape)):
            near = jnp.where(inside, near, 0.0)
            total = near if total is None else total + near
        return total

    def diagonals(coefs):
        out = []
        for k, coef in enumerate(coefs):
            total = 6.0 * coef + plane_sum(coef)
            if k > 0:
                total = total + coefs[k - 1]
            if k < len(coefs) - 1:
                total = total + coefs[k + 1]
            out.append(total)
        return out

    d1 = diagonals(c1)
    for k in range(pairs):
        cof1[k] = c1[k]
        dia1[k] = d1[k]
    for k in range(pairs // 2):
        put_rows(zmid, k, c1[2 * k] + c1[2 * k + 1])
    rows = [
        get_rows(zmid, k, 8, ny2) + get_rows(zmid, k, 9, ny2)
        for k in range(pairs // 2)
    ]
    weights = wsum[0 : nx // 2, 0 : nx // 4]
    sums = 0.125 * dot_parts(jnp.concatenate(rows, axis=0), weights)
    c2 = [sums[k * ny2 : (k + 1) * ny2] for k in range(pairs // 2)]
    d2 = diagonals(c2)
    for k in range(2):
        cof2[k] = c2[k]
        dia2[k] = d2[k]
    for side in range(2):
        send_c1[side, 0] = c1[1 + side]
        send_c1[side, 1] = c1[2 - side]
        diagonal = d1[2 - side]
        send_c2[side, :, 0 : nx // 2] = jnp.where(
            parity((ny2, nx // 2), side + 1), diagonal[:ny2], pltpu.roll(diagonal[ny2:], 1, 0)
        )
        send_c2[side, :, nx // 2 : 3 * nx // 4] = c2[side]
        send_c2[side, :, 3 * nx // 4 : nx] = d2[side]
    send(lambda side: send_c1.at[side], halo_c1, s_c1, r_c1)
    send(lambda side: send_c2.at[side], halo_c2, s_c2, r_c2)

    def restrict(ref, first, count, out_rows, weights, scale):
        rows = [
            (get_rows(ref, k, 7, out_rows) + get_rows(ref, k, 10, out_rows))
            + 3.0 * (get_rows(ref, k, 8, out_rows) + get_rows(ref, k, 9, out_rows))
            for k in range(first, first + count)
        ]
        out = scale * dot_parts(jnp.concatenate(rows, axis=0), weights)
        return [out[k * out_rows : (k + 1) * out_rows] for k in range(count)]

    def along_z(k, carry):
        put_rows(zbuf, k, 3.0 * rho[k + 1] + even_first(rho[k + 2], rho[k]))
        return carry

    lax.fori_loop(0, pairs, along_z, 0)
    put_rows(zbuf, pairs, even_first(rho[1], 0.0))
    put_rows(zbuf, pairs + 1, even_first(0.0, rho[pairs]))
    parts = restrict(zbuf, 0, pairs + 2, ny1, wres[...], 0.5 ** 10)
    for side in range(2):
        ends = (3 * side, 1 + side, 4 + side)
        for i, end in enumerate(ends):
            v1[side, i] = parts[end]
        send_2[side, 0] = parts[ends[0]]
        send_2[side, 1] = parts[ends[2]]
        send_2[side, 2] = (c1[ends[0]] + c1[ends[1]]) * (8.0 * parts[ends[1]] / d1[ends[1]])
    send(lambda side: send_2.at[side, 0:2], halo_2, s_2, r_2)
    copy_out(near, send_2.at[near, 2], halo_n, s_n, r_n).start()

    def planes_there(side, present):
        wait_recv(side, present, halo_c, s_c, r_c)
        mine = parity(plane, side)
        hc0, hc1 = halo_c[side, 1 - side], halo_c[side, side]
        sides0, around = side_faces(hc0, hc0)
        hsum[0] = 6.0 * hc0 + around + hc1
        sides1, around = side_faces(hc1, hc1)
        hsum[1] = 6.0 * hc1 + around + hc0
        for i, (f0, f1) in enumerate(zip(sides0, sides1)):
            hside[0, i] = f0
            hside[1, i] = jnp.where(mine, f1, f0)
        put_rows(zbuf, 0, hc0 + hc1)
        rows = get_rows(zbuf, 0, 8, ny1) + get_rows(zbuf, 0, 9, ny1)
        c1_there[side] = 0.125 * dot_parts(rows, wsum[...])

    def second_stage(side, present):
        planes_there(side, present)
        wait_recv(side, present, halo_x, s_x, r_x)
        wait_recv(side, present, halo_q, s_q, r_q)
        k = (pairs - 1) * side
        here = (nz - 1) * side
        inner = k + 1 - 2 * side
        mine = parity(plane, side)
        hc0, hc1 = halo_c[side, 1 - side], halo_c[side, side]
        mixed, tops = halo_x[side], halo_q[side]
        c0, g0 = craw[here], graw[here]
        face, pair = c0 + hc0, hc0 + hc1
        diagonal0, diagonal1 = hsum[0], hsum[1] + mixed

        new = (jnp.where(mine, nr[k], tops) + face * jnp.where(mine, mixed, g0)) / (
            jnp.where(mine, dr[k] + hc0, diagonal0 + c0)
        )
        there = jnp.where(present, new, 0.0)
        there_old = jnp.where(present, tops / diagonal0, 0.0)
        old = rr[k + 1]
        reds = jnp.where(mine, new, old)
        change = jnp.where(mine, new - old, 0.0)

        top = topb[k] + fpair[k] * change + jnp.where(mine, 0.0, face * there)
        for i, shifted in enumerate(shifts(change)):
            top = top + fbs[k, i] * shifted
        blacks = top / (db[k] + jnp.where(mine, 0.0, hc0))
        put_pressure(k, reds, blacks)
        delta = blacks - gb[k + 1]
        change = delta - dl[k + 1]

        short = tops
        for i, shifted in enumerate(shifts(there_old)):
            short = short + hside[0, i] * shifted
        full = tops + face * new
        for i, shifted in enumerate(shifts(there)):
            full = full + hside[0, i] * shifted
        blacks = full / (diagonal0 + c0)
        part = jnp.where(mine, short, pair * (there_old - there)) / jnp.where(mine, diagonal0, diagonal1)
        change_there = jnp.where(present, jnp.where(mine, blacks, 0.0) - part, 0.0)
        delta_there = jnp.where(present, blacks - mixed, 0.0)

        add = fpair[k] * change + jnp.where(mine, face * delta_there, 0.0)
        for i, shifted in enumerate(shifts(change)):
            add = add + frs[k, i] * shifted
        put_rows(zbuf, 0, jnp.where(mine, add, 0.0))
        put_rows(zbuf, 1, jnp.where(mine, 0.0, add))
        put_rows(zbuf, 2, jnp.where(mine, (cr[inner + 1] + cb[k + 1]) * change, 0.0))
        add = pair * change_there + jnp.where(mine | jnp.logical_not(present), 0.0, face * delta)
        for i, shifted in enumerate(shifts(change_there)):
            add = add + hside[1, i] * shifted
        put_rows(zbuf, 3, jnp.where(mine, 0.0, add))
        put_rows(zbuf, 4, jnp.where(mine, add, 0.0))
        put_rows(zbuf, 5, jnp.where(mine, 0.0, (mixed + hc1) * change_there))
        own0, own1, own2, end0, end1, end2 = restrict(zbuf, 0, 6, ny1, wres[...], 0.5 ** 10)
        v1[side, 0] = v1[side, 0] + (3.0 * (own0 + own1) + own2)
        v1[side, 1] = v1[side, 1] + (3.0 * own2 + own1)
        v1[side, 2] = v1[side, 2] + own0
        v1[side, 3] = end0
        v1[side, 4] = 3.0 * (end0 + end1) + end2
        v1[side, 5] = 3.0 * end2 + end1

    true = me >= 0
    second_stage(near, true)

    def mask1(j):
        return parity(plane1, j + far + 4)

    def at1(j):
        return 3 * far + j * (1 - 2 * far)

    cof = {j: cof1[at1(j)] for j in range(4)}
    dia = {j: dia1[at1(j)] for j in range(4)}
    fac, for_red, for_black = {}, {}, {}

    def prepare(j, mask, factor, present=None):
        fac[j] = side_faces(cof[j], cof[j])[0]
        if j in dia:
            for_red[j] = jnp.where(mask, factor / dia[j], 0.0)
            for_black[j] = jnp.where(mask, 0.0, 1.0 / dia[j])
            if present is not None:
                for_red[j] = jnp.where(present, for_red[j], 0.0)
                for_black[j] = jnp.where(present, for_black[j], 0.0)

    def flat(j, field):
        total = None
        for face, shifted in zip(fac[j], shifts(field)):
            term = face * shifted
            total = term if total is None else total + term
        return total

    def across(i, j, field):
        return (cof[i] + cof[j]) * field

    def red_of(j, right):
        return for_red[j] * right

    def black_of(j, top):
        return for_black[j] * top

    wait_recv(near, true, halo_c1, s_c1, r_c1)
    def diagonal_of(j):
        return 6.0 * cof[j] + plane_sum(cof[j]) + (cof[j - 1] + cof[j + 1])

    cof.update({4: c1_there[near], 5: halo_c1[near, 0], 6: halo_c1[near, 1]})
    dia.update({3: dia[3] + cof[4], 4: diagonal_of(4), 5: diagonal_of(5)})
    for j in (1, 2, 3, 4, 5):
        prepare(j, mask1(j), 8.0)
    wait_recv(near, true, halo_2, s_2, r_2)
    wait_recv(near, true, halo_n, s_n, r_n)
    rhs = {
        4: halo_2[near, 0] + v1[near, 4] + v1[near, 2],
        3: v1[near, 0] + (halo_2[near, 1] + v1[near, 3]),
        2: v1[near, 1],
    }
    red = {j: red_of(j, rhs[j]) for j in (2, 3, 4)}
    black = {}
    beyond = halo_n[near] + across(4, 5, red_of(5, v1[near, 5]))
    black[4] = black_of(4, 8.0 * rhs[4] + beyond + flat(4, red[4]) + across(4, 3, red[3]))
    black[3] = black_of(
        3, 8.0 * rhs[3] + flat(3, red[3]) + across(3, 4, red[4]) + across(3, 2, red[2])
    )
    base1 = across(1, 2, red[2])
    base2 = 8.0 * rhs[2] + flat(2, red[2]) + across(2, 3, red[3])
    base3 = across(2, 3, black[3])

    def middle():
        right = v1[far, 1]
        red1 = red_of(1, right)
        black2 = black_of(2, base2 + across(2, 1, red1))
        part1 = 8.0 * right + flat(1, red1) + base1
        part2 = flat(2, black2) + base3
        return red1, black2, part1, part2, across(1, 2, black2)

    red1, black2, part1, part2, cross = middle()
    send_2[far, 2] = jnp.where(mask1(0), part2, across(0, 1, red1))
    send_2[far, 3] = jnp.where(mask1(1), cross, part1)

    @pl.when(has_far)
    def _():
        copy_out(far, send_2.at[far, 2:4], halo_f, s_f, r_f).start()

    second_stage(far, has_far)
    red[1], black[2], part1, part2, cross = middle()
    wait_recv(far, has_far, halo_c1, s_c1, r_c1)
    wait_recv(near, true, halo_c2, s_c2, r_c2)
    wait_recv(far, has_far, halo_c2, s_c2, r_c2)
    cof.update({-1: c1_there[far], -2: halo_c1[far, 0], -3: halo_c1[far, 1]})
    packed = halo_c2[far, :, 0 : nx // 2]
    packed = jnp.concatenate([packed, pltpu.roll(packed, ny2 - 1, 0)], axis=0)
    dia.update({
        -1: diagonal_of(-1), -2: diagonal_of(-2), -3: packed, 0: dia[0] + cof[-1],
    })
    prepare(0, mask1(0), 8.0)
    for j in (-1, -2, -3):
        prepare(j, mask1(j), 8.0, has_far)
    there1, there2 = v1[far, 3], v1[far, 5]
    more_red = red_of(-2, there2)
    more_black = black_of(-3, across(-3, -2, more_red))
    fix1 = jnp.where(mask1(-1), flat(-3, more_black), across(-1, -2, more_red))
    fix2 = jnp.where(mask1(-2), across(-2, -3, more_black), 8.0 * there2 + flat(-2, more_red))
    base0 = across(0, 1, red[1])
    end0 = v1[far, 0] + there1
    end1 = v1[far, 4] + v1[far, 2]
    def mask2(j):
        return parity(plane2, j + far + 4)

    def at2(j):
        return far + j * (1 - 2 * far)

    levels = cof, dia, fac, for_red, for_black
    def coef2(side):
        return halo_c2[side, :, nx // 2 : 3 * nx // 4]

    def diagonal2(side):
        return halo_c2[side, :, 3 * nx // 4 : nx]

    cof = {-1: coef2(far), 0: cof2[at2(0)], 1: cof2[at2(1)], 2: coef2(near)}
    dia = {
        -1: diagonal2(far) + cof[0], 0: dia2[at2(0)] + cof[-1],
        1: dia2[at2(1)] + cof[2], 2: diagonal2(near) + cof[1],
    }
    fac, for_red, for_black = {}, {}, {}
    for j in (0, 1, 2):
        prepare(j, mask2(j), 32.0)
    prepare(-1, mask2(-1), 32.0, has_far)
    low_cof, low_fac, low_red, low_black = cof, fac, for_red, for_black
    cof, dia, fac, for_red, for_black = levels

    wait_recv(far, has_far, halo_2, s_2, r_2)
    rhs[0] = halo_2[far, 1] + end0
    rhs[-1] = halo_2[far, 0] + end1
    red[0] = red_of(0, rhs[0])
    red[-1] = red_of(-1, rhs[-1])
    black[0] = black_of(0, 8.0 * rhs[0] + base0 + across(0, -1, red[-1]) + flat(0, red[0]))
    black[1] = black_of(1, part1 + across(1, 0, red[0]))
    res = {
        3: flat(3, black[3]) + across(3, 2, black[2]) + across(3, 4, black[4]),
        2: part2 + across(2, 1, black[1]),
        1: flat(1, black[1]) + across(1, 0, black[0]) + cross,
    }
    res = {j: jnp.where(mask1(j), value, 0.0) for j, value in res.items()}
    weights2 = wres[0 : nx // 2, 0 : nx // 4]
    put_rows(zmid, 0, 3.0 * (res[3] + res[2]) + res[1])
    put_rows(zmid, 1, res[3])
    parts = restrict(zmid, 0, 2, ny2, weights2, 0.5 ** 12)
    send_3[0] = parts[0]
    send_3[1] = parts[1]
    copy_out(near, send_3, halo_3, s_3, r_3).start()

    wait_recv(far, has_far, halo_f, s_f, r_f)
    seconds = (halo_f[far, 0] + fix1, halo_f[far, 1] + fix2)
    black[-1] = black_of(-1, 8.0 * rhs[-1] + seconds[0] + flat(-1, red[-1]) + across(-1, 0, red[0]))
    black[-2] = black_of(-2, seconds[1] + across(-2, -1, red[-1]))
    more = {
        0: flat(0, black[0]) + across(0, -1, black[-1]) + across(0, 1, black[1]),
        -1: flat(-1, black[-1]) + across(-1, -2, black[-2]) + across(-1, 0, black[0]),
        -2: seconds[1] + flat(-2, black[-2]) + across(-2, -1, black[-1]),
        -3: seconds[0] + across(-3, -2, black[-2]),
    }
    for j, value in more.items():
        res[j] = jnp.where(mask1(j) if j == 0 else mask1(j) & has_far, value, 0.0)

    put_rows(zmid, 2, 3.0 * (res[0] + res[1]) + (res[-1] + res[2]))
    put_rows(zmid, 3, 3.0 * (res[-1] + res[-2]) + (res[0] + res[-3]))
    parts = parts + restrict(zmid, 2, 2, ny2, weights2, 0.5 ** 12)
    for j in range(4):
        mid_ref[at1(j)] = red[j] + black[j]

    cof, fac, for_red, for_black = low_cof, low_fac, low_red, low_black
    rhs = {-1: parts[3], 0: parts[2]}
    red = {j: red_of(j, rhs[j]) for j in (-1, 0)}
    base0 = 32.0 * rhs[0] + flat(0, red[0]) + across(0, -1, red[-1])
    base1 = across(1, 0, red[0])
    wait_recv(near, true, halo_3, s_3, r_3)
    rhs.update({1: parts[0] + halo_3[near, 1], 2: halo_3[near, 0] + parts[1]})
    red.update({j: red_of(j, rhs[j]) for j in (1, 2)})
    low_ref[at2(0)] = red[0] + black_of(0, base0 + across(0, 1, red[1]))
    low_ref[at2(1)] = red[1] + black_of(
        1, 32.0 * rhs[1] + base1 + across(1, 2, red[2]) + flat(1, red[1])
    )

    def wait_sent(side, present, messages):
        @pl.when(present)
        def _():
            for src, dst, s_sem, r_sem in messages:
                copy_out(side, src, dst, s_sem, r_sem).wait_send()

    for side in range(2):
        wait_sent(side, has[side], (
            (c_hbm.at[pl.ds((nz - 2) * side, 2)], halo_c, s_c, r_c),
            (send_x.at[side], halo_x, s_x, r_x),
            (send_q.at[side], halo_q, s_q, r_q),
            (send_c1.at[side], halo_c1, s_c1, r_c1),
            (send_c2.at[side], halo_c2, s_c2, r_c2),
            (send_2.at[side, 0:2], halo_2, s_2, r_2),
        ))
    wait_sent(near, true, (
        (send_2.at[near, 2], halo_n, s_n, r_n), (send_3, halo_3, s_3, r_3),
    ))
    wait_sent(far, has_far, ((send_2.at[far, 2:4], halo_f, s_f, r_f),))


def on_device(size, pressure_guess, source, conductance):
    nz, ny, nx = pressure_guess.shape
    pairs = nz // 2
    ny1, nx1, ny2, nx2 = ny // 2, nx // 2, ny // 4, nx // 4

    def vmem(*shape):
        return pltpu.VMEM(shape, F32)

    slab = [vmem(nz, ny, nx)] * 3
    padded = [vmem(pairs + 2, ny, nx)] * 6
    faces = [
        vmem(pairs, ny, nx), vmem(pairs, ny, nx), vmem(pairs, 4, ny, nx),
        vmem(pairs, ny, nx), vmem(pairs, 4, ny, nx),
    ]
    sums = [vmem(pairs, ny, nx)] * 3
    work = [
        vmem(pairs + 2, nx // 128, ny + 16, 128), vmem(4, nx1 // 128, ny1 + 16, 128),
        pltpu.VMEM((nx, nx1), BF16), pltpu.VMEM((nx, nx1), BF16),
        vmem(2, 6, ny1, nx1), vmem(pairs, ny, nx), vmem(2, ny, nx), vmem(2, 4, ny, nx),
        vmem(2, ny1, nx1), vmem(pairs, ny1, nx1), vmem(pairs, ny1, nx1),
        vmem(2, ny2, nx2), vmem(2, ny2, nx2),
    ]
    messages = [
        vmem(2, ny, nx), vmem(2, ny, nx), vmem(2, 2, ny1, nx1), vmem(2, ny2, nx),
    ]
    sent = messages + [vmem(2, 4, ny1, nx1), vmem(2, ny2, nx2)]
    halos = [vmem(2, 2, ny, nx)] + messages + [
        vmem(2, 2, ny1, nx1), vmem(2, ny1, nx1), vmem(2, 2, ny1, nx1), vmem(2, 2, ny2, nx2),
    ]
    sems = [pltpu.SemaphoreType.DMA((3,))] + [pltpu.SemaphoreType.DMA((2,))] * 18

    def run(*refs):
        kernel(size, *refs)

    shapes = ((nz, ny, nx), (pairs, ny1, nx1), (pairs // 2, ny2, nx2))
    inputs = [
        pltpu.with_memory_space_constraint(value, pltpu.HBM)
        for value in (pressure_guess, source, conductance)
    ]
    results = pl.pallas_call(
        run,
        out_shape=tuple(pltpu.VMEM(shape, F32) for shape in shapes),
        in_specs=[pl.BlockSpec(memory_space=pl.ANY)] * 3,
        out_specs=tuple([pl.BlockSpec(memory_space=pltpu.VMEM)] * 3),
        scratch_shapes=slab + padded + faces + sums + work + sent + halos + sems,
        compiler_params=pltpu.CompilerParams(
            collective_id=0, has_side_effects=True, vmem_limit_bytes=48 * 2 ** 20
        ),
    )(*inputs)
    return pl.pallas_call(
        write_out,
        out_shape=tuple(jax.ShapeDtypeStruct(shape, F32) for shape in shapes),
        in_specs=[pl.BlockSpec(memory_space=pl.ANY)] * 3,
        out_specs=tuple([pl.BlockSpec(memory_space=pl.ANY)] * 3),
        scratch_shapes=[pltpu.SemaphoreType.DMA((3,))],
    )(*[pltpu.with_memory_space_constraint(value, pltpu.VMEM) for value in results])


def write_out(p_src, mid_src, low_src, p_dst, mid_dst, low_dst, sem):
    copies = [
        pltpu.make_async_copy(src, dst, sem.at[i])
        for i, (src, dst) in enumerate(((p_src, p_dst), (mid_src, mid_dst), (low_src, low_dst)))
    ]
    for copy in copies:
        copy.start()
    for copy in copies:
        copy.wait()


def solution(mesh):
    size = mesh.shape["gz"]
    spec = P("gz", None, None)
    return jax.shard_map(
        lambda *args: on_device(size, *args), mesh=mesh,
        in_specs=(spec, spec, spec), out_specs=(spec, spec, spec), check_vma=False,
    )
```

```python
import jax
import jax.numpy as jnp
from jax import lax
from jax.experimental import pallas as pl
from jax.experimental.pallas import tpu as pltpu
from jax.sharding import PartitionSpec as P

F32 = jnp.float32
BF16 = jnp.bfloat16


def parity(shape, offset):
    rows = lax.broadcasted_iota(jnp.int32, shape, 0)
    cols = lax.broadcasted_iota(jnp.int32, shape, 1)
    return ((rows + cols + offset) & 1) == 0


def shifts(plane):
    ny, nx = plane.shape
    return (
        pltpu.roll(plane, ny - 1, 0),
        pltpu.roll(plane, 1, 0),
        pltpu.roll(plane, nx - 1, 1),
        pltpu.roll(plane, 1, 1),
    )


def insides(shape):
    rows = lax.broadcasted_iota(jnp.int32, shape, 0)
    cols = lax.broadcasted_iota(jnp.int32, shape, 1)
    return (rows < shape[0] - 1, rows > 0, cols < shape[1] - 1, cols > 0)


def side_faces(centre, other):
    faces, total = [], None
    for near, inside in zip(shifts(other), insides(centre.shape)):
        near = jnp.where(inside, near, 0.0)
        faces.append(jnp.where(inside, centre + near, 0.0))
        total = near if total is None else total + near
    return faces, total


def dot_parts(rows, weights):
    count = rows.shape[0]
    high = rows.astype(BF16)
    rest = rows - high.astype(F32)
    middle = rest.astype(BF16)
    low = (rest - middle.astype(F32)).astype(BF16)
    out = jnp.dot(
        jnp.concatenate([high, middle, low], axis=0), weights, preferred_element_type=F32
    )
    return out[:count] + (out[count : 2 * count] + out[2 * count :])


def weights_of(shape, inner, outer):
    fine = lax.broadcasted_iota(jnp.int32, shape, 0)
    coarse = lax.broadcasted_iota(jnp.int32, shape, 1)
    apart = fine - 2 * coarse
    near = (apart == 0) | (apart == 1)
    far = (apart == -1) | (apart == 2)
    return jnp.where(near, inner, jnp.where(far, outer, 0.0)).astype(BF16)


def kernel(
    size,
    g_hbm, b_hbm, c_hbm,
    p_ref, mid_ref, low_ref,
    craw, graw, braw,
    cr, cb, gb, rr, dl, rho,
    fpair, fro, frs, fbo, fbs,
    dr, db, nr,
    zbuf, zmid, wres, wsum,
    v1, topb, hsum, hside, c1_there, cof1, dia1,
    cof2, dia2,
    send_x, send_q, send_c1, send_d1, send_c2, send_2, send_3,
    halo_c, halo_x, halo_q, halo_c1, halo_d1, halo_c2, halo_2, halo_n, halo_f, halo_3,
    load_sem,
    s_c, s_x, s_q, s_c1, s_d1, s_c2, s_2, s_n, s_f, s_3,
    r_c, r_x, r_q, r_c1, r_d1, r_c2, r_2, r_n, r_f, r_3,
):
    me = lax.axis_index("gz")
    nz, ny, nx = craw.shape
    pairs = nz // 2
    plane = (ny, nx)
    plane1 = (ny // 2, nx // 2)
    plane2 = (ny // 4, nx // 4)
    has = (me > 0, me < size - 1)
    far = me % 2
    near = 1 - far
    has_far = jnp.where(far == 0, me, size - 1 - me) > 0

    barrier = pltpu.get_barrier_semaphore()
    for side in range(2):
        @pl.when(has[side])
        def _(side=side):
            pl.semaphore_signal(
                barrier, inc=1, device_id=(me + 2 * side - 1,),
                device_id_type=pl.DeviceIdType.MESH,
            )

    loads = [
        pltpu.make_async_copy(src, dst, load_sem.at[i])
        for i, (src, dst) in enumerate(((c_hbm, craw), (g_hbm, graw), (b_hbm, braw)))
    ]
    for load in loads:
        load.start()

    def copy_out(side, src, dst, s_sem, r_sem):
        return pltpu.make_async_remote_copy(
            src_ref=src, dst_ref=dst.at[1 - side], send_sem=s_sem.at[side],
            recv_sem=r_sem.at[1 - side], device_id=(me + 2 * side - 1,),
            device_id_type=pl.DeviceIdType.MESH,
        )

    def send(src_of, dst, s_sem, r_sem, allowed=True):
        for side in range(2):
            @pl.when(has[side] & allowed)
            def _(side=side):
                copy_out(side, src_of(side), dst, s_sem, r_sem).start()

    def wait_recv(side, present, dst, s_sem, r_sem):
        @pl.when(present)
        def _():
            pltpu.make_async_remote_copy(
                src_ref=dst.at[side], dst_ref=dst.at[side], send_sem=s_sem.at[side],
                recv_sem=r_sem.at[side], device_id=(me + 2 * side - 1,),
                device_id_type=pl.DeviceIdType.MESH,
            ).wait_recv()

    def enter(allowed):
        @pl.when(allowed)
        def _():
            pl.semaphore_wait(barrier, jnp.where(has[0] & has[1], 2, 1))

    def send_coefficients(allowed):
        send(lambda side: c_hbm.at[pl.ds((nz - 2) * side, 2)], halo_c, s_c, r_c, allowed)

    odd, even_core = far == 1, far == 0
    enter(odd)
    send_coefficients(odd)

    for ref in (cr, cb, gb, rr, dl, rho):
        ref[0] = jnp.zeros(plane, F32)
        ref[pairs + 1] = jnp.zeros(plane, F32)
    for ref, depth in ((zbuf, ny), (zmid, ny // 2)):
        for i in range(ref.shape[0]):
            for j in range(ref.shape[1]):
                ref[i, j, 0:8] = jnp.zeros((8, 128), F32)
                ref[i, j, depth + 8 : depth + 16] = jnp.zeros((8, 128), F32)
    for side in range(2):
        @pl.when(jnp.logical_not(has[side]))
        def _(side=side):
            for ref in (halo_x, halo_q, halo_c1, halo_d1, halo_c2):
                ref[side] = jnp.zeros(ref.shape[1:], F32)
            for ref in (halo_c, halo_2, halo_f):
                for i in range(ref.shape[1]):
                    ref[side, i] = jnp.zeros(ref.shape[2:], F32)
    wres[...] = weights_of(wres.shape, 3.0, 1.0)
    wsum[...] = weights_of(wsum.shape, 1.0, 0.0)

    even = parity(plane, 0)

    def even_first(first, second):
        return jnp.where(parity(plane, 0), first, second)

    loads[0].wait()

    def put_rows(ref, k, value):
        for j in range(ref.shape[1]):
            ref[k, j, 8 : value.shape[0] + 8] = value[:, 128 * j : 128 * j + 128]

    def get_rows(ref, k, start, count):
        return jnp.concatenate(
            [ref[k, j, pl.ds(start, count, stride=2), :] for j in range(ref.shape[1])], axis=1
        )

    def pack(k, carry):
        low, high = craw[2 * k], craw[2 * k + 1]
        cr[k + 1] = even_first(low, high)
        cb[k + 1] = even_first(high, low)
        put_rows(zbuf, k, low + high)
        return carry

    lax.fori_loop(0, pairs, pack, 0)

    def faces(k, carry):
        own, other = cr[k + 1], cb[k + 1]
        fpair[k] = own + other
        outer = even_first(cb[k], cb[k + 2])
        sides, total = side_faces(own, other)
        fro[k] = own + outer
        for i in range(4):
            frs[k, i] = sides[i]
        dr[k] = 6.0 * own + other + outer + total
        outer = even_first(cr[k + 2], cr[k])
        sides, total = side_faces(other, own)
        fbo[k] = other + outer
        for i in range(4):
            fbs[k, i] = sides[i]
        db[k] = 6.0 * other + own + outer + total
        return carry

    def gather(k, centre, outer, f_outer, f_sides):
        total = fpair[k] * centre + f_outer[k] * outer
        for i, near in enumerate(shifts(centre)):
            total = total + f_sides[k, i] * near
        return total

    def pack_g(k, carry):
        gb[k + 1] = even_first(graw[2 * k + 1], graw[2 * k])
        return carry

    def red(k, carry):
        rhs = even_first(braw[2 * k], braw[2 * k + 1])
        off = gather(k, gb[k + 1], even_first(gb[k], gb[k + 2]), fro, frs)
        top = 2.0 * rhs + off
        nr[k] = top
        rr[k + 1] = top / dr[k]
        return carry

    def put_mixed(side, carry):
        send_x[side] = jnp.where(parity(plane, side), craw[2 + (nz - 5) * side], graw[(nz - 1) * side])
        return carry

    def at_ends(body):
        lax.fori_loop(0, 2, lambda i, carry: body((pairs - 1) * i, carry), 0)

    at_ends(faces)
    loads[1].wait()
    lax.fori_loop(0, 2, put_mixed, 0)
    send(lambda side: send_x.at[side], halo_x, s_x, r_x, odd)
    lax.fori_loop(0, pairs, pack_g, 0)
    loads[2].wait()
    at_ends(red)
    enter(even_core)
    send_coefficients(even_core)
    send(lambda side: send_x.at[side], halo_x, s_x, r_x, even_core)

    lax.fori_loop(1, pairs - 1, faces, 0)
    lax.fori_loop(1, pairs - 1, red, 0)

    def put_pressure(k, reds, blacks):
        p_ref[2 * k] = even_first(reds, blacks)
        p_ref[2 * k + 1] = even_first(blacks, reds)

    def black(k, carry):
        rhs = even_first(braw[2 * k + 1], braw[2 * k])
        reds = rr[k + 1]
        top = 2.0 * rhs + gather(k, reds, even_first(rr[k + 2], rr[k]), fbo, fbs)
        topb[k] = top
        new = top / db[k]
        dl[k + 1] = new - gb[k + 1]
        put_pressure(k, reds, new)
        return carry

    at_ends(black)

    def put_tops(side, carry):
        k = (pairs - 1) * side
        send_q[side] = jnp.where(parity(plane, side), rr[k + 1], topb[k])
        return carry

    lax.fori_loop(0, 2, put_tops, 0)
    send(lambda side: send_q.at[side], halo_q, s_q, r_q)
    lax.fori_loop(1, pairs - 1, black, 0)

    def residual(k, carry):
        rho[k + 1] = gather(k, dl[k + 1], even_first(dl[k], dl[k + 2]), fro, frs)
        return carry

    lax.fori_loop(0, pairs, residual, 0)

    ny1, ny2 = ny // 2, ny // 4
    rows = [
        get_rows(zbuf, k, 8, ny1) + get_rows(zbuf, k, 9, ny1)
        for k in range(pairs)
    ]
    sums = 0.125 * dot_parts(jnp.concatenate(rows, axis=0), wsum[...])
    c1 = [sums[k * ny1 : (k + 1) * ny1] for k in range(pairs)]

    def plane_sum(value):
        total = None
        for near, inside in zip(shifts(value), insides(value.shape)):
            near = jnp.where(inside, near, 0.0)
            total = near if total is None else total + near
        return total

    def diagonals(coefs):
        out = []
        for k, coef in enumerate(coefs):
            total = 6.0 * coef + plane_sum(coef)
            if k > 0:
                total = total + coefs[k - 1]
            if k < len(coefs) - 1:
                total = total + coefs[k + 1]
            out.append(total)
        return out

    d1 = diagonals(c1)
    for k in range(pairs):
        cof1[k] = c1[k]
        dia1[k] = d1[k]
    for k in range(pairs // 2):
        put_rows(zmid, k, c1[2 * k] + c1[2 * k + 1])
    rows = [
        get_rows(zmid, k, 8, ny2) + get_rows(zmid, k, 9, ny2)
        for k in range(pairs // 2)
    ]
    weights = wsum[0 : nx // 2, 0 : nx // 4]
    sums = 0.125 * dot_parts(jnp.concatenate(rows, axis=0), weights)
    c2 = [sums[k * ny2 : (k + 1) * ny2] for k in range(pairs // 2)]
    d2 = diagonals(c2)
    for k in range(2):
        cof2[k] = c2[k]
        dia2[k] = d2[k]
    for side in range(2):
        send_c1[side] = c1[1 + side]
        send_d1[side] = c1[2 - side]
        diagonal = d1[2 - side]
        send_c2[side, :, 0 : nx // 2] = jnp.where(
            parity((ny2, nx // 2), side + 1), diagonal[:ny2], pltpu.roll(diagonal[ny2:], 1, 0)
        )
        send_c2[side, :, nx // 2 : 3 * nx // 4] = c2[side]
        send_c2[side, :, 3 * nx // 4 : nx] = d2[side]
    send(lambda side: send_c1.at[side], halo_c1, s_c1, r_c1)

    def restrict(ref, first, count, out_rows, weights, scale):
        rows = [
            (get_rows(ref, k, 7, out_rows) + get_rows(ref, k, 10, out_rows))
            + 3.0 * (get_rows(ref, k, 8, out_rows) + get_rows(ref, k, 9, out_rows))
            for k in range(first, first + count)
        ]
        out = scale * dot_parts(jnp.concatenate(rows, axis=0), weights)
        return [out[k * out_rows : (k + 1) * out_rows] for k in range(count)]

    def along_z(k, carry):
        put_rows(zbuf, k, 3.0 * rho[k + 1] + even_first(rho[k + 2], rho[k]))
        return carry

    lax.fori_loop(0, pairs, along_z, 0)
    put_rows(zbuf, pairs, even_first(rho[1], 0.0))
    put_rows(zbuf, pairs + 1, even_first(0.0, rho[pairs]))
    parts = restrict(zbuf, 0, pairs + 2, ny1, wres[...], 0.5 ** 10)
    for side in range(2):
        ends = (3 * side, 1 + side, 4 + side)
        for i, end in enumerate(ends):
            v1[side, i] = parts[end]
        send_2[side, 0] = parts[ends[0]]
        send_2[side, 1] = parts[ends[2]]
        send_2[side, 2] = (c1[ends[0]] + c1[ends[1]]) * (8.0 * parts[ends[1]] / d1[ends[1]])
    send(lambda side: send_2.at[side, 0:2], halo_2, s_2, r_2)
    copy_out(near, send_2.at[near, 2], halo_n, s_n, r_n).start()
    send(lambda side: send_d1.at[side], halo_d1, s_d1, r_d1)
    send(lambda side: send_c2.at[side], halo_c2, s_c2, r_c2)

    def planes_there(side, present):
        wait_recv(side, present, halo_c, s_c, r_c)
        mine = parity(plane, side)
        hc0, hc1 = halo_c[side, 1 - side], halo_c[side, side]
        sides0, around = side_faces(hc0, hc0)
        hsum[0] = 6.0 * hc0 + around + hc1
        sides1, around = side_faces(hc1, hc1)
        hsum[1] = 6.0 * hc1 + around + hc0
        for i, (f0, f1) in enumerate(zip(sides0, sides1)):
            hside[0, i] = f0
            hside[1, i] = jnp.where(mine, f1, f0)
        put_rows(zbuf, 0, hc0 + hc1)
        rows = get_rows(zbuf, 0, 8, ny1) + get_rows(zbuf, 0, 9, ny1)
        c1_there[side] = 0.125 * dot_parts(rows, wsum[...])

    def second_stage(side, present):
        planes_there(side, present)
        wait_recv(side, present, halo_x, s_x, r_x)
        k = (pairs - 1) * side
        here = (nz - 1) * side
        inner = k + 1 - 2 * side
        mine = parity(plane, side)
        hc0, hc1, mixed = halo_c[side, 1 - side], halo_c[side, side], halo_x[side]
        c0, g0 = craw[here], graw[here]
        face, pair = c0 + hc0, hc0 + hc1
        diagonal = hsum[0]
        for_new = 1.0 / (diagonal + c0)
        for_old = 1.0 / jnp.where(mine, diagonal, hsum[1] + mixed)
        for_own = 1.0 / (db[k] + jnp.where(mine, 0.0, hc0))

        old = rr[k + 1]
        new = (nr[k] + face * mixed) / (dr[k] + hc0)
        reds = jnp.where(mine, new, old)
        change = jnp.where(mine, new - old, 0.0)
        top = topb[k] + fpair[k] * change
        for i, shifted in enumerate(shifts(change)):
            top = top + fbs[k, i] * shifted

        wait_recv(side, present, halo_q, s_q, r_q)
        tops = halo_q[side]
        there = jnp.where(present, (tops * diagonal + face * g0) * for_new, 0.0)
        change_there = jnp.where(mine, 0.0, there - tops)

        blacks = (top + jnp.where(mine, 0.0, face * there)) * for_own
        put_pressure(k, reds, blacks)
        delta = blacks - gb[k + 1]
        change = delta - dl[k + 1]

        full = tops + face * new
        for i, shifted in enumerate(shifts(change_there)):
            full = full + hside[0, i] * shifted
        blacks = full * for_new
        part = jnp.where(mine, tops, -(pair * change_there)) * for_old
        change_there = jnp.where(present, jnp.where(mine, blacks, 0.0) - part, 0.0)
        delta_there = jnp.where(present, blacks - mixed, 0.0)

        add = fpair[k] * change + jnp.where(mine, face * delta_there, 0.0)
        for i, shifted in enumerate(shifts(change)):
            add = add + frs[k, i] * shifted
        put_rows(zbuf, 0, jnp.where(mine, add, 0.0))
        put_rows(zbuf, 1, jnp.where(mine, 0.0, add))
        put_rows(zbuf, 2, jnp.where(mine, (cr[inner + 1] + cb[k + 1]) * change, 0.0))
        add = pair * change_there + jnp.where(mine | jnp.logical_not(present), 0.0, face * delta)
        for i, shifted in enumerate(shifts(change_there)):
            add = add + hside[1, i] * shifted
        put_rows(zbuf, 3, jnp.where(mine, 0.0, add))
        put_rows(zbuf, 4, jnp.where(mine, add, 0.0))
        put_rows(zbuf, 5, jnp.where(mine, 0.0, (mixed + hc1) * change_there))
        own0, own1, own2, end0, end1, end2 = restrict(zbuf, 0, 6, ny1, wres[...], 0.5 ** 10)
        v1[side, 0] = v1[side, 0] + (3.0 * (own0 + own1) + own2)
        v1[side, 1] = v1[side, 1] + (3.0 * own2 + own1)
        v1[side, 2] = v1[side, 2] + own0
        v1[side, 3] = end0
        v1[side, 4] = 3.0 * (end0 + end1) + end2
        v1[side, 5] = 3.0 * end2 + end1

    true = me >= 0
    second_stage(near, true)

    def mask1(j):
        return parity(plane1, j + far + 4)

    def at1(j):
        return 3 * far + j * (1 - 2 * far)

    cof = {j: cof1[at1(j)] for j in range(4)}
    dia = {j: dia1[at1(j)] for j in range(4)}
    fac, for_red, for_black = {}, {}, {}

    def prepare(j, mask, factor, present=None):
        fac[j] = side_faces(cof[j], cof[j])[0]
        if j in dia:
            for_red[j] = jnp.where(mask, factor / dia[j], 0.0)
            for_black[j] = jnp.where(mask, 0.0, 1.0 / dia[j])
            if present is not None:
                for_red[j] = jnp.where(present, for_red[j], 0.0)
                for_black[j] = jnp.where(present, for_black[j], 0.0)

    def flat(j, field):
        total = None
        for face, shifted in zip(fac[j], shifts(field)):
            term = face * shifted
            total = term if total is None else total + term
        return total

    def across(i, j, field):
        return (cof[i] + cof[j]) * field

    def red_of(j, right):
        return for_red[j] * right

    def black_of(j, top):
        return for_black[j] * top

    wait_recv(near, true, halo_c1, s_c1, r_c1)
    wait_recv(near, true, halo_d1, s_d1, r_d1)
    def diagonal_of(j):
        return 6.0 * cof[j] + plane_sum(cof[j]) + (cof[j - 1] + cof[j + 1])

    cof.update({4: c1_there[near], 5: halo_c1[near], 6: halo_d1[near]})
    dia.update({3: dia[3] + cof[4], 4: diagonal_of(4), 5: diagonal_of(5)})
    for j in (1, 2, 3, 4, 5):
        prepare(j, mask1(j), 8.0)
    wait_recv(near, true, halo_2, s_2, r_2)
    wait_recv(near, true, halo_n, s_n, r_n)
    rhs = {
        4: halo_2[near, 0] + v1[near, 4] + v1[near, 2],
        3: v1[near, 0] + (halo_2[near, 1] + v1[near, 3]),
        2: v1[near, 1],
    }
    red = {j: red_of(j, rhs[j]) for j in (2, 3, 4)}
    black = {}
    beyond = halo_n[near] + across(4, 5, red_of(5, v1[near, 5]))
    black[4] = black_of(4, 8.0 * rhs[4] + beyond + flat(4, red[4]) + across(4, 3, red[3]))
    black[3] = black_of(
        3, 8.0 * rhs[3] + flat(3, red[3]) + across(3, 4, red[4]) + across(3, 2, red[2])
    )
    base1 = across(1, 2, red[2])
    base2 = 8.0 * rhs[2] + flat(2, red[2]) + across(2, 3, red[3])
    base3 = across(2, 3, black[3])

    def middle():
        right = v1[far, 1]
        red1 = red_of(1, right)
        black2 = black_of(2, base2 + across(2, 1, red1))
        part1 = 8.0 * right + flat(1, red1) + base1
        part2 = flat(2, black2) + base3
        return red1, black2, part1, part2, across(1, 2, black2)

    red1, black2, part1, part2, cross = middle()
    send_2[far, 2] = jnp.where(mask1(0), part2, across(0, 1, red1))
    send_2[far, 3] = jnp.where(mask1(1), cross, part1)

    @pl.when(has_far)
    def _():
        copy_out(far, send_2.at[far, 2:4], halo_f, s_f, r_f).start()

    def mask2(j):
        return parity(plane2, j + far + 4)

    def at2(j):
        return far + j * (1 - 2 * far)

    def coef2(side):
        return halo_c2[side, :, nx // 2 : 3 * nx // 4]

    def diagonal2(side):
        return halo_c2[side, :, 3 * nx // 4 : nx]

    wait_recv(near, true, halo_c2, s_c2, r_c2)
    levels = cof, dia, fac, for_red, for_black
    cof = {0: cof2[at2(0)], 1: cof2[at2(1)], 2: coef2(near)}
    dia = {1: dia2[at2(1)] + cof[2], 2: diagonal2(near) + cof[1]}
    fac, for_red, for_black = {}, {}, {}
    for j in (1, 2):
        prepare(j, mask2(j), 32.0)
    lows = cof, dia, fac, for_red, for_black
    cof, dia, fac, for_red, for_black = levels

    second_stage(far, has_far)
    red[1], black[2], part1, part2, cross = middle()
    wait_recv(far, has_far, halo_c1, s_c1, r_c1)
    cof.update({-1: c1_there[far], -2: halo_c1[far]})
    dia.update({-1: diagonal_of(-1), 0: dia[0] + cof[-1]})
    prepare(0, mask1(0), 8.0)
    prepare(-1, mask1(-1), 8.0, has_far)
    base0 = across(0, 1, red[1])
    end0 = v1[far, 0] + v1[far, 3]
    end1 = v1[far, 4] + v1[far, 2]
    wait_recv(far, has_far, halo_2, s_2, r_2)
    rhs[0] = halo_2[far, 1] + end0
    rhs[-1] = halo_2[far, 0] + end1
    red[0] = red_of(0, rhs[0])
    red[-1] = red_of(-1, rhs[-1])
    black[0] = black_of(0, 8.0 * rhs[0] + base0 + across(0, -1, red[-1]) + flat(0, red[0]))
    black[1] = black_of(1, part1 + across(1, 0, red[0]))
    res = {
        3: flat(3, black[3]) + across(3, 2, black[2]) + across(3, 4, black[4]),
        2: part2 + across(2, 1, black[1]),
        1: flat(1, black[1]) + across(1, 0, black[0]) + cross,
    }
    res = {j: jnp.where(mask1(j), value, 0.0) for j, value in res.items()}
    weights2 = wres[0 : nx // 2, 0 : nx // 4]
    put_rows(zmid, 0, 3.0 * (res[3] + res[2]) + res[1])
    put_rows(zmid, 1, res[3])
    parts = restrict(zmid, 0, 2, ny2, weights2, 0.5 ** 12)
    send_3[0] = parts[0]
    send_3[1] = parts[1]
    copy_out(near, send_3, halo_3, s_3, r_3).start()

    wait_recv(far, has_far, halo_d1, s_d1, r_d1)
    wait_recv(far, has_far, halo_c2, s_c2, r_c2)
    cof[-3] = halo_d1[far]
    packed = halo_c2[far, :, 0 : nx // 2]
    packed = jnp.concatenate([packed, pltpu.roll(packed, ny2 - 1, 0)], axis=0)
    dia.update({-2: diagonal_of(-2), -3: packed})
    for j in (-2, -3):
        prepare(j, mask1(j), 8.0, has_far)
    there2 = v1[far, 5]
    more_red = red_of(-2, there2)
    more_black = black_of(-3, across(-3, -2, more_red))
    fix1 = jnp.where(mask1(-1), flat(-3, more_black), across(-1, -2, more_red))
    fix2 = jnp.where(mask1(-2), across(-2, -3, more_black), 8.0 * there2 + flat(-2, more_red))

    cof, dia, fac, for_red, for_black = lows
    cof[-1] = coef2(far)
    dia.update({-1: diagonal2(far) + cof[0], 0: dia2[at2(0)] + cof[-1]})
    prepare(0, mask2(0), 32.0)
    prepare(-1, mask2(-1), 32.0, has_far)
    cof, dia, fac, for_red, for_black = levels

    before1 = 8.0 * rhs[-1] + fix1 + flat(-1, red[-1]) + across(-1, 0, red[0])
    before2 = fix2 + across(-2, -1, red[-1])
    before0 = flat(0, black[0]) + across(0, 1, black[1])
    before3 = across(-1, 0, black[0])
    inner_rows = 3.0 * res[1] + res[2]
    for j in range(4):
        mid_ref[at1(j)] = red[j] + black[j]
    wait_recv(far, has_far, halo_f, s_f, r_f)
    black[-1] = black_of(-1, before1 + halo_f[far, 0])
    black[-2] = black_of(-2, before2 + halo_f[far, 1])
    more = {
        0: before0 + across(0, -1, black[-1]),
        -1: flat(-1, black[-1]) + across(-1, -2, black[-2]) + before3,
        -2: (halo_f[far, 1] + fix2) + flat(-2, black[-2]) + across(-2, -1, black[-1]),
        -3: (halo_f[far, 0] + fix1) + across(-3, -2, black[-2]),
    }
    for j, value in more.items():
        res[j] = jnp.where(mask1(j) if j == 0 else mask1(j) & has_far, value, 0.0)

    put_rows(zmid, 2, 3.0 * res[0] + (res[-1] + inner_rows))
    put_rows(zmid, 3, 3.0 * (res[-1] + res[-2]) + (res[0] + res[-3]))
    parts = parts + restrict(zmid, 2, 2, ny2, weights2, 0.5 ** 12)

    cof, dia, fac, for_red, for_black = lows
    rhs = {-1: parts[3], 0: parts[2]}
    red = {j: red_of(j, rhs[j]) for j in (-1, 0)}
    base0 = 32.0 * rhs[0] + flat(0, red[0]) + across(0, -1, red[-1])
    base1 = across(1, 0, red[0])
    wait_recv(near, true, halo_3, s_3, r_3)
    rhs.update({1: parts[0] + halo_3[near, 1], 2: halo_3[near, 0] + parts[1]})
    red.update({j: red_of(j, rhs[j]) for j in (1, 2)})
    low_ref[at2(0)] = red[0] + black_of(0, base0 + across(0, 1, red[1]))
    low_ref[at2(1)] = red[1] + black_of(
        1, 32.0 * rhs[1] + base1 + across(1, 2, red[2]) + flat(1, red[1])
    )

    def wait_sent(side, present, messages):
        @pl.when(present)
        def _():
            for src, dst, s_sem, r_sem in messages:
                copy_out(side, src, dst, s_sem, r_sem).wait_send()

    for side in range(2):
        wait_sent(side, has[side], (
            (c_hbm.at[pl.ds((nz - 2) * side, 2)], halo_c, s_c, r_c),
            (send_x.at[side], halo_x, s_x, r_x),
            (send_q.at[side], halo_q, s_q, r_q),
            (send_c1.at[side], halo_c1, s_c1, r_c1),
            (send_d1.at[side], halo_d1, s_d1, r_d1),
            (send_c2.at[side], halo_c2, s_c2, r_c2),
            (send_2.at[side, 0:2], halo_2, s_2, r_2),
        ))
    wait_sent(near, true, (
        (send_2.at[near, 2], halo_n, s_n, r_n), (send_3, halo_3, s_3, r_3),
    ))
    wait_sent(far, has_far, ((send_2.at[far, 2:4], halo_f, s_f, r_f),))


def on_device(size, pressure_guess, source, conductance):
    nz, ny, nx = pressure_guess.shape
    pairs = nz // 2
    ny1, nx1, ny2, nx2 = ny // 2, nx // 2, ny // 4, nx // 4

    def vmem(*shape):
        return pltpu.VMEM(shape, F32)

    slab = [vmem(nz, ny, nx)] * 3
    padded = [vmem(pairs + 2, ny, nx)] * 6
    faces = [
        vmem(pairs, ny, nx), vmem(pairs, ny, nx), vmem(pairs, 4, ny, nx),
        vmem(pairs, ny, nx), vmem(pairs, 4, ny, nx),
    ]
    sums = [vmem(pairs, ny, nx)] * 3
    work = [
        vmem(pairs + 2, nx // 128, ny + 16, 128), vmem(4, nx1 // 128, ny1 + 16, 128),
        pltpu.VMEM((nx, nx1), BF16), pltpu.VMEM((nx, nx1), BF16),
        vmem(2, 6, ny1, nx1), vmem(pairs, ny, nx), vmem(2, ny, nx), vmem(2, 4, ny, nx),
        vmem(2, ny1, nx1), vmem(pairs, ny1, nx1), vmem(pairs, ny1, nx1),
        vmem(2, ny2, nx2), vmem(2, ny2, nx2),
    ]
    messages = [
        vmem(2, ny, nx), vmem(2, ny, nx), vmem(2, ny1, nx1), vmem(2, ny1, nx1), vmem(2, ny2, nx),
    ]
    sent = messages + [vmem(2, 4, ny1, nx1), vmem(2, ny2, nx2)]
    halos = [vmem(2, 2, ny, nx)] + messages + [
        vmem(2, 2, ny1, nx1), vmem(2, ny1, nx1), vmem(2, 2, ny1, nx1), vmem(2, 2, ny2, nx2),
    ]
    sems = [pltpu.SemaphoreType.DMA((3,))] + [pltpu.SemaphoreType.DMA((2,))] * 20

    def run(*refs):
        kernel(size, *refs)

    shapes = ((nz, ny, nx), (pairs, ny1, nx1), (pairs // 2, ny2, nx2))
    inputs = [
        pltpu.with_memory_space_constraint(value, pltpu.HBM)
        for value in (pressure_guess, source, conductance)
    ]
    results = pl.pallas_call(
        run,
        out_shape=tuple(pltpu.VMEM(shape, F32) for shape in shapes),
        in_specs=[pl.BlockSpec(memory_space=pl.ANY)] * 3,
        out_specs=tuple([pl.BlockSpec(memory_space=pltpu.VMEM)] * 3),
        scratch_shapes=slab + padded + faces + sums + work + sent + halos + sems,
        compiler_params=pltpu.CompilerParams(
            collective_id=0, has_side_effects=True, vmem_limit_bytes=48 * 2 ** 20
        ),
    )(*inputs)
    return pl.pallas_call(
        write_out,
        out_shape=tuple(jax.ShapeDtypeStruct(shape, F32) for shape in shapes),
        in_specs=[pl.BlockSpec(memory_space=pl.ANY)] * 3,
        out_specs=tuple([pl.BlockSpec(memory_space=pl.ANY)] * 3),
        scratch_shapes=[pltpu.SemaphoreType.DMA((3,))],
    )(*[pltpu.with_memory_space_constraint(value, pltpu.VMEM) for value in results])


def write_out(p_src, mid_src, low_src, p_dst, mid_dst, low_dst, sem):
    copies = [
        pltpu.make_async_copy(src, dst, sem.at[i])
        for i, (src, dst) in enumerate(((p_src, p_dst), (mid_src, mid_dst), (low_src, low_dst)))
    ]
    for copy in copies:
        copy.start()
    for copy in copies:
        copy.wait()


def solution(mesh):
    size = mesh.shape["gz"]
    spec = P("gz", None, None)
    return jax.shard_map(
        lambda *args: on_device(size, *args), mesh=mesh,
        in_specs=(spec, spec, spec), out_specs=(spec, spec, spec), check_vma=False,
    )
```

```python
import jax
import jax.numpy as jnp
from jax import lax
from jax.experimental import pallas as pl
from jax.experimental.pallas import tpu as pltpu
from jax.sharding import PartitionSpec as P

F32 = jnp.float32
BF16 = jnp.bfloat16


def parity(shape, offset):
    rows = lax.broadcasted_iota(jnp.int32, shape, 0)
    cols = lax.broadcasted_iota(jnp.int32, shape, 1)
    return ((rows + cols + offset) & 1) == 0


def shifts(plane):
    ny, nx = plane.shape
    return (
        pltpu.roll(plane, ny - 1, 0),
        pltpu.roll(plane, 1, 0),
        pltpu.roll(plane, nx - 1, 1),
        pltpu.roll(plane, 1, 1),
    )


def insides(shape):
    rows = lax.broadcasted_iota(jnp.int32, shape, 0)
    cols = lax.broadcasted_iota(jnp.int32, shape, 1)
    return (rows < shape[0] - 1, rows > 0, cols < shape[1] - 1, cols > 0)


def side_faces(centre, other):
    faces, total = [], None
    for near, inside in zip(shifts(other), insides(centre.shape)):
        near = jnp.where(inside, near, 0.0)
        faces.append(jnp.where(inside, centre + near, 0.0))
        total = near if total is None else total + near
    return faces, total


def dot_parts(rows, weights):
    count = rows.shape[0]
    high = rows.astype(BF16)
    rest = rows - high.astype(F32)
    middle = rest.astype(BF16)
    low = (rest - middle.astype(F32)).astype(BF16)
    out = jnp.dot(
        jnp.concatenate([high, middle, low], axis=0), weights, preferred_element_type=F32
    )
    return out[:count] + (out[count : 2 * count] + out[2 * count :])


def weights_of(shape, inner, outer):
    fine = lax.broadcasted_iota(jnp.int32, shape, 0)
    coarse = lax.broadcasted_iota(jnp.int32, shape, 1)
    apart = fine - 2 * coarse
    near = (apart == 0) | (apart == 1)
    far = (apart == -1) | (apart == 2)
    return jnp.where(near, inner, jnp.where(far, outer, 0.0)).astype(BF16)


def kernel(
    size,
    g_hbm, b_hbm, c_hbm,
    p_ref, mid_ref, low_ref,
    craw, graw, braw,
    cr, cb, gb, rr, dl, rho,
    fpair, fro, frs, fbo, fbs,
    dr, db, nr,
    zbuf, zmid, wres, wsum,
    v1, topb, hsum, hside, c1_there, cof1, dia1,
    cof2, dia2,
    send_x, send_q, send_c1, send_d1, send_c2, send_2, send_n, send_f, send_3,
    halo_c, halo_x, halo_q, halo_c1, halo_d1, halo_c2, halo_2, halo_n, halo_f, halo_3,
    load_sem,
    s_c, s_x, s_q, s_c1, s_d1, s_c2, s_2, s_n, s_f, s_3,
    r_c, r_x, r_q, r_c1, r_d1, r_c2, r_2, r_n, r_f, r_3,
):
    me = lax.axis_index("gz")
    nz, ny, nx = craw.shape
    pairs = nz // 2
    plane = (ny, nx)
    plane1 = (ny // 2, nx // 2)
    plane2 = (ny // 4, nx // 4)
    has = (me > 0, me < size - 1)
    far = me % 2
    near = 1 - far
    has_far = jnp.where(far == 0, me, size - 1 - me) > 0

    barrier = pltpu.get_barrier_semaphore()
    for side in range(2):
        @pl.when(has[side])
        def _(side=side):
            pl.semaphore_signal(
                barrier, inc=1, device_id=(me + 2 * side - 1,),
                device_id_type=pl.DeviceIdType.MESH,
            )

    loads = [
        pltpu.make_async_copy(src, dst, load_sem.at[i])
        for i, (src, dst) in enumerate(((c_hbm, craw), (g_hbm, graw), (b_hbm, braw)))
    ]
    for load in loads:
        load.start()

    def copy_out(side, src, dst, s_sem, r_sem):
        return pltpu.make_async_remote_copy(
            src_ref=src, dst_ref=dst.at[1 - side], send_sem=s_sem.at[side],
            recv_sem=r_sem.at[1 - side], device_id=(me + 2 * side - 1,),
            device_id_type=pl.DeviceIdType.MESH,
        )

    def send(src_of, dst, s_sem, r_sem, allowed=True):
        for side in range(2):
            @pl.when(has[side] & allowed)
            def _(side=side):
                copy_out(side, src_of(side), dst, s_sem, r_sem).start()

    def wait_recv(side, present, dst, s_sem, r_sem):
        @pl.when(present)
        def _():
            pltpu.make_async_remote_copy(
                src_ref=dst.at[side], dst_ref=dst.at[side], send_sem=s_sem.at[side],
                recv_sem=r_sem.at[side], device_id=(me + 2 * side - 1,),
                device_id_type=pl.DeviceIdType.MESH,
            ).wait_recv()

    def enter(allowed):
        @pl.when(allowed)
        def _():
            pl.semaphore_wait(barrier, jnp.where(has[0] & has[1], 2, 1))

    def send_coefficients(allowed):
        send(lambda side: c_hbm.at[pl.ds((nz - 2) * side, 2)], halo_c, s_c, r_c, allowed)

    odd, even_core = far == 1, far == 0
    enter(odd)
    send_coefficients(odd)

    for ref in (cr, cb, gb, rr, dl, rho):
        ref[0] = jnp.zeros(plane, F32)
        ref[pairs + 1] = jnp.zeros(plane, F32)
    for ref, depth in ((zbuf, ny), (zmid, ny // 2)):
        for i in range(ref.shape[0]):
            for j in range(ref.shape[1]):
                ref[i, j, 0:8] = jnp.zeros((8, 128), F32)
                ref[i, j, depth + 8 : depth + 16] = jnp.zeros((8, 128), F32)
    for side in range(2):
        @pl.when(jnp.logical_not(has[side]))
        def _(side=side):
            for ref in (halo_x, halo_q, halo_c1, halo_d1, halo_n):
                ref[side] = jnp.zeros(ref.shape[1:], F32)
            for ref in (halo_c, halo_c2, halo_2, halo_f):
                for i in range(ref.shape[1]):
                    ref[side, i] = jnp.zeros(ref.shape[2:], F32)
    wres[...] = weights_of(wres.shape, 3.0, 1.0)
    wsum[...] = weights_of(wsum.shape, 1.0, 0.0)

    even = parity(plane, 0)

    def even_first(first, second):
        return jnp.where(parity(plane, 0), first, second)

    loads[0].wait()

    def put_rows(ref, k, value):
        for j in range(ref.shape[1]):
            ref[k, j, 8 : value.shape[0] + 8] = value[:, 128 * j : 128 * j + 128]

    def get_rows(ref, k, start, count):
        return jnp.concatenate(
            [ref[k, j, pl.ds(start, count, stride=2), :] for j in range(ref.shape[1])], axis=1
        )

    def pack(k, carry):
        low, high = craw[2 * k], craw[2 * k + 1]
        cr[k + 1] = even_first(low, high)
        cb[k + 1] = even_first(high, low)
        put_rows(zbuf, k, low + high)
        return carry

    lax.fori_loop(0, pairs, pack, 0)

    def faces(k, carry):
        own, other = cr[k + 1], cb[k + 1]
        fpair[k] = own + other
        outer = even_first(cb[k], cb[k + 2])
        sides, total = side_faces(own, other)
        fro[k] = own + outer
        for i in range(4):
            frs[k, i] = sides[i]
        dr[k] = 6.0 * own + other + outer + total
        outer = even_first(cr[k + 2], cr[k])
        sides, total = side_faces(other, own)
        fbo[k] = other + outer
        for i in range(4):
            fbs[k, i] = sides[i]
        db[k] = 6.0 * other + own + outer + total
        return carry

    def gather(k, centre, outer, f_outer, f_sides):
        total = fpair[k] * centre + f_outer[k] * outer
        for i, near in enumerate(shifts(centre)):
            total = total + f_sides[k, i] * near
        return total

    def pack_g(k, carry):
        gb[k + 1] = even_first(graw[2 * k + 1], graw[2 * k])
        return carry

    def red(k, carry):
        rhs = even_first(braw[2 * k], braw[2 * k + 1])
        off = gather(k, gb[k + 1], even_first(gb[k], gb[k + 2]), fro, frs)
        top = 2.0 * rhs + off
        nr[k] = top
        rr[k + 1] = top / dr[k]
        return carry

    def put_mixed(side, carry):
        send_x[side] = jnp.where(parity(plane, side), craw[2 + (nz - 5) * side], graw[(nz - 1) * side])
        return carry

    def at_ends(body):
        lax.fori_loop(0, 2, lambda i, carry: body((pairs - 1) * i, carry), 0)

    lax.fori_loop(0, pairs, faces, 0)
    enter(even_core)
    send_coefficients(even_core)

    ny1, ny2 = ny // 2, ny // 4
    rows = [
        get_rows(zbuf, k, 8, ny1) + get_rows(zbuf, k, 9, ny1)
        for k in range(pairs)
    ]
    sums = 0.125 * dot_parts(jnp.concatenate(rows, axis=0), wsum[...])
    c1 = [sums[k * ny1 : (k + 1) * ny1] for k in range(pairs)]

    def plane_sum(value):
        total = None
        for near, inside in zip(shifts(value), insides(value.shape)):
            near = jnp.where(inside, near, 0.0)
            total = near if total is None else total + near
        return total

    def diagonals(coefs):
        out = []
        for k, coef in enumerate(coefs):
            total = 6.0 * coef + plane_sum(coef)
            if k > 0:
                total = total + coefs[k - 1]
            if k < len(coefs) - 1:
                total = total + coefs[k + 1]
            out.append(total)
        return out

    d1 = diagonals(c1)
    for k in range(pairs):
        cof1[k] = c1[k]
        dia1[k] = d1[k]
    for k in range(pairs // 2):
        put_rows(zmid, k, c1[2 * k] + c1[2 * k + 1])
    rows = [
        get_rows(zmid, k, 8, ny2) + get_rows(zmid, k, 9, ny2)
        for k in range(pairs // 2)
    ]
    weights = wsum[0 : nx // 2, 0 : nx // 4]
    sums = 0.125 * dot_parts(jnp.concatenate(rows, axis=0), weights)
    c2 = [sums[k * ny2 : (k + 1) * ny2] for k in range(pairs // 2)]
    d2 = diagonals(c2)
    for k in range(2):
        cof2[k] = c2[k]
        dia2[k] = d2[k]
    for side in range(2):
        send_c1[side] = c1[1 + side]
        send_d1[side] = c1[2 - side]
        send_c2[side, 0] = c2[side]
        send_c2[side, 1] = d2[side]

    loads[1].wait()
    lax.fori_loop(0, 2, put_mixed, 0)
    send(lambda side: send_x.at[side], halo_x, s_x, r_x)
    lax.fori_loop(0, pairs, pack_g, 0)
    loads[2].wait()
    at_ends(red)

    lax.fori_loop(1, pairs - 1, red, 0)

    def put_pressure(k, reds, blacks):
        p_ref[2 * k] = even_first(reds, blacks)
        p_ref[2 * k + 1] = even_first(blacks, reds)

    def black(k, carry):
        rhs = even_first(braw[2 * k + 1], braw[2 * k])
        reds = rr[k + 1]
        top = 2.0 * rhs + gather(k, reds, even_first(rr[k + 2], rr[k]), fbo, fbs)
        topb[k] = top
        new = top / db[k]
        dl[k + 1] = new - gb[k + 1]
        put_pressure(k, reds, new)
        return carry

    at_ends(black)

    def put_tops(side, carry):
        k = (pairs - 1) * side
        send_q[side] = jnp.where(parity(plane, side), rr[k + 1], topb[k])
        return carry

    lax.fori_loop(0, 2, put_tops, 0)
    send(lambda side: send_q.at[side], halo_q, s_q, r_q)
    lax.fori_loop(1, pairs - 1, black, 0)

    def residual(k, carry):
        rho[k + 1] = gather(k, dl[k + 1], even_first(dl[k], dl[k + 2]), fro, frs)
        return carry

    lax.fori_loop(0, pairs, residual, 0)

    def restrict(ref, first, count, out_rows, weights, scale):
        rows = [
            (get_rows(ref, k, 7, out_rows) + get_rows(ref, k, 10, out_rows))
            + 3.0 * (get_rows(ref, k, 8, out_rows) + get_rows(ref, k, 9, out_rows))
            for k in range(first, first + count)
        ]
        out = scale * dot_parts(jnp.concatenate(rows, axis=0), weights)
        return [out[k * out_rows : (k + 1) * out_rows] for k in range(count)]

    def along_z(k, carry):
        put_rows(zbuf, k, 3.0 * rho[k + 1] + even_first(rho[k + 2], rho[k]))
        return carry

    lax.fori_loop(0, pairs, along_z, 0)
    put_rows(zbuf, pairs, even_first(rho[1], 0.0))
    put_rows(zbuf, pairs + 1, even_first(0.0, rho[pairs]))
    parts = restrict(zbuf, 0, pairs + 2, ny1, wres[...], 0.5 ** 10)
    for side in range(2):
        for i, end in enumerate((3 * side, 1 + side, 4 + side)):
            v1[side, i] = parts[end]

    def mask1(j):
        return parity(plane1, j + far + 4)

    def at1(j):
        return 3 * far + j * (1 - 2 * far)

    cof = {j: cof1[at1(j)] for j in range(4)}
    dia = {j: dia1[at1(j)] for j in range(4)}
    fac, for_red, for_black = {}, {}, {}

    def prepare(j, mask, factor, present=None):
        fac[j] = side_faces(cof[j], cof[j])[0]
        if j in dia:
            for_red[j] = jnp.where(mask, factor / dia[j], 0.0)
            for_black[j] = jnp.where(mask, 0.0, 1.0 / dia[j])
            if present is not None:
                for_red[j] = jnp.where(present, for_red[j], 0.0)
                for_black[j] = jnp.where(present, for_black[j], 0.0)

    def flat(j, field):
        total = None
        for face, shifted in zip(fac[j], shifts(field)):
            term = face * shifted
            total = term if total is None else total + term
        return total

    def across(i, j, field):
        return (cof[i] + cof[j]) * field

    def red_of(j, right):
        return for_red[j] * right

    def black_of(j, top):
        return for_black[j] * top

    alone = dia[0]
    for j in (0, 1, 2):
        prepare(j, mask1(j), 8.0)
    alone_red, alone_black = for_red[0], for_black[0]
    right0, right1 = v1[far, 0], v1[far, 1]
    red0, red1 = alone_red * right0, red_of(1, right1)
    top0 = 8.0 * right0 + flat(0, red0) + across(0, 1, red1)
    send_2[near, 0] = v1[near, 0]
    send_2[near, 1] = v1[near, 2]
    send_n[near] = across(3, 2, red_of(2, v1[near, 1]))
    send_2[far, 0] = jnp.where(mask1(0), red0, pltpu.roll(alone, 1, 0))
    send_2[far, 1] = v1[far, 2]
    send_n[far] = jnp.where(mask1(0), pltpu.roll(dia[2], 1, 0), top0)
    send(lambda side: send_2.at[side], halo_2, s_2, r_2)
    send(lambda side: send_n.at[side], halo_n, s_n, r_n)
    send(lambda side: send_c1.at[side], halo_c1, s_c1, r_c1)
    send(lambda side: send_d1.at[side], halo_d1, s_d1, r_d1)
    send(lambda side: send_c2.at[side], halo_c2, s_c2, r_c2)

    def planes_there(side, present):
        wait_recv(side, present, halo_c, s_c, r_c)
        mine = parity(plane, side)
        hc0, hc1 = halo_c[side, 1 - side], halo_c[side, side]
        sides0, around = side_faces(hc0, hc0)
        hsum[0] = 6.0 * hc0 + around + hc1
        sides1, around = side_faces(hc1, hc1)
        hsum[1] = 6.0 * hc1 + around + hc0
        for i, (f0, f1) in enumerate(zip(sides0, sides1)):
            hside[0, i] = f0
            hside[1, i] = jnp.where(mine, f1, f0)
        put_rows(zbuf, 0, hc0 + hc1)
        rows = get_rows(zbuf, 0, 8, ny1) + get_rows(zbuf, 0, 9, ny1)
        c1_there[side] = 0.125 * dot_parts(rows, wsum[...])

    def second_stage(side, present):
        planes_there(side, present)
        wait_recv(side, present, halo_x, s_x, r_x)
        k = (pairs - 1) * side
        here = (nz - 1) * side
        inner = k + 1 - 2 * side
        mine = parity(plane, side)
        hc0, hc1, mixed = halo_c[side, 1 - side], halo_c[side, side], halo_x[side]
        c0, g0 = craw[here], graw[here]
        face, pair = c0 + hc0, hc0 + hc1
        diagonal = hsum[0]
        for_new = 1.0 / (diagonal + c0)
        for_old = 1.0 / jnp.where(mine, diagonal, hsum[1] + mixed)
        for_own = 1.0 / (db[k] + jnp.where(mine, 0.0, hc0))

        old = rr[k + 1]
        new = (nr[k] + face * mixed) / (dr[k] + hc0)
        reds = jnp.where(mine, new, old)
        change = jnp.where(mine, new - old, 0.0)
        top = topb[k] + fpair[k] * change
        for i, shifted in enumerate(shifts(change)):
            top = top + fbs[k, i] * shifted

        wait_recv(side, present, halo_q, s_q, r_q)
        tops = halo_q[side]
        there = jnp.where(present, (tops * diagonal + face * g0) * for_new, 0.0)
        change_there = jnp.where(mine, 0.0, there - tops)

        blacks = (top + jnp.where(mine, 0.0, face * there)) * for_own
        put_pressure(k, reds, blacks)
        delta = blacks - gb[k + 1]
        change = delta - dl[k + 1]

        full = tops + face * new
        for i, shifted in enumerate(shifts(change_there)):
            full = full + hside[0, i] * shifted
        blacks = full * for_new
        part = jnp.where(mine, tops, -(pair * change_there)) * for_old
        change_there = jnp.where(present, jnp.where(mine, blacks, 0.0) - part, 0.0)
        delta_there = jnp.where(present, blacks - mixed, 0.0)

        add = fpair[k] * change + jnp.where(mine, face * delta_there, 0.0)
        for i, shifted in enumerate(shifts(change)):
            add = add + frs[k, i] * shifted
        own, third = add, (cr[inner + 1] + cb[k + 1]) * change
        add = pair * change_there + jnp.where(mine | jnp.logical_not(present), 0.0, face * delta)
        for i, shifted in enumerate(shifts(change_there)):
            add = add + hside[1, i] * shifted
        beyond = (mixed + hc1) * change_there
        put_rows(zbuf, 0, 3.0 * own + jnp.where(mine, third, add))
        put_rows(zbuf, 1, 3.0 * add + jnp.where(mine, own, beyond))
        put_rows(zbuf, 2, jnp.where(mine, 3.0 * third, own))
        put_rows(zbuf, 3, jnp.where(mine, add, 3.0 * beyond))
        parts = restrict(zbuf, 0, 4, ny1, wres[...], 0.5 ** 10)
        v1[side, 0] = v1[side, 0] + parts[0]
        v1[side, 2] = v1[side, 2] + parts[1]
        v1[side, 1] = v1[side, 1] + parts[2]
        v1[side, 3] = parts[3]

    true = me >= 0
    second_stage(near, true)

    wait_recv(near, true, halo_c1, s_c1, r_c1)
    wait_recv(near, true, halo_d1, s_d1, r_d1)
    def diagonal_of(j):
        return 6.0 * cof[j] + plane_sum(cof[j]) + (cof[j - 1] + cof[j + 1])

    cof.update({4: c1_there[near], 5: halo_c1[near], 6: halo_d1[near]})
    dia.update({3: dia[3] + cof[4], 4: diagonal_of(4), 5: diagonal_of(5)})
    for j in (3, 4, 5):
        prepare(j, mask1(j), 8.0)
    wait_recv(near, true, halo_2, s_2, r_2)
    wait_recv(near, true, halo_n, s_n, r_n)
    rhs = {
        4: halo_2[near, 0] + v1[near, 2],
        3: v1[near, 0] + halo_2[near, 1],
        2: v1[near, 1],
    }
    red = {j: red_of(j, rhs[j]) for j in (2, 3, 4)}
    black = {}
    beyond = halo_n[near] + across(4, 5, red_of(5, v1[near, 3]))
    black[4] = black_of(4, 8.0 * rhs[4] + beyond + flat(4, red[4]) + across(4, 3, red[3]))
    black[3] = black_of(
        3, 8.0 * rhs[3] + flat(3, red[3]) + across(3, 4, red[4]) + across(3, 2, red[2])
    )
    base1 = across(1, 2, red[2])
    base2 = 8.0 * rhs[2] + flat(2, red[2]) + across(2, 3, red[3])
    base3 = across(2, 3, black[3])

    def middle():
        right = v1[far, 1]
        red1 = red_of(1, right)
        black2 = black_of(2, base2 + across(2, 1, red1))
        part1 = 8.0 * right + flat(1, red1) + base1
        part2 = flat(2, black2) + base3
        return red1, black2, part1, part2, across(1, 2, black2)

    red1, black2, part1, part2, cross = middle()
    black0 = alone_black * top0
    black1 = black_of(1, part1 + across(1, 0, red0))
    res0 = flat(0, black0) + across(0, 1, black1)
    res1 = flat(1, black1) + across(1, 0, black0) + cross
    res2 = part2 + across(2, 1, black1)
    res0 = jnp.where(mask1(0), res0, 0.0)
    weights2 = wres[0 : nx // 2, 0 : nx // 4]
    put_rows(zmid, 0, jnp.where(mask1(1), 3.0 * res1, 3.0 * res0 + jnp.where(mask1(2), res2, 0.0)))
    put_rows(zmid, 1, res0)
    parts = restrict(zmid, 0, 2, ny2, weights2, 0.5 ** 12)
    send_f[0] = parts[0]
    send_f[1] = parts[1]

    @pl.when(has_far)
    def _():
        copy_out(far, send_f, halo_f, s_f, r_f).start()

    def mask2(j):
        return parity(plane2, j + far + 4)

    def at2(j):
        return far + j * (1 - 2 * far)

    def coef2(side):
        return halo_c2[side, 0]

    def diagonal2(side):
        return halo_c2[side, 1]

    wait_recv(near, true, halo_c2, s_c2, r_c2)
    levels = cof, dia, fac, for_red, for_black
    cof = {0: cof2[at2(0)], 1: cof2[at2(1)], 2: coef2(near)}
    dia = {1: dia2[at2(1)] + cof[2], 2: diagonal2(near) + cof[1]}
    fac, for_red, for_black = {}, {}, {}
    for j in (1, 2):
        prepare(j, mask2(j), 32.0)
    lows = cof, dia, fac, for_red, for_black
    cof, dia, fac, for_red, for_black = levels

    second_stage(far, has_far)
    red[1], black[2], part1, part2, cross = middle()
    cof[-1] = c1_there[far]
    dia[0] = alone + cof[-1]
    prepare(0, mask1(0), 8.0)
    base0 = across(0, 1, red[1])
    end0 = v1[far, 0]
    end1 = 8.0 * v1[far, 2]
    wait_recv(far, has_far, halo_2, s_2, r_2)
    rhs[0] = halo_2[far, 1] + end0
    red[0] = red_of(0, rhs[0])
    first = halo_2[far, 0]
    diagonal = pltpu.roll(first, ny1 - 1, 0)
    red[-1] = jnp.where(mask1(-1) & has_far, (first * diagonal + end1) / (diagonal + cof[0]), 0.0)
    black[0] = black_of(0, 8.0 * rhs[0] + base0 + across(0, -1, red[-1]) + flat(0, red[0]))
    black[1] = black_of(1, part1 + across(1, 0, red[0]))
    res = {
        3: flat(3, black[3]) + across(3, 2, black[2]) + across(3, 4, black[4]),
        2: part2 + across(2, 1, black[1]),
        1: flat(1, black[1]) + across(1, 0, black[0]) + cross,
    }
    res = {j: jnp.where(mask1(j), value, 0.0) for j, value in res.items()}
    put_rows(zmid, 0, 3.0 * (res[3] + res[2]) + res[1])
    put_rows(zmid, 1, res[3])
    parts = restrict(zmid, 0, 2, ny2, weights2, 0.5 ** 12)
    send_3[0] = parts[0]
    send_3[1] = parts[1]
    copy_out(near, send_3, halo_3, s_3, r_3).start()

    wait_recv(far, has_far, halo_n, s_n, r_n)
    wait_recv(far, has_far, halo_c1, s_c1, r_c1)
    wait_recv(far, has_far, halo_d1, s_d1, r_d1)
    wait_recv(far, has_far, halo_c2, s_c2, r_c2)
    cof.update({-2: halo_c1[far], -3: halo_d1[far]})
    second = halo_n[far]
    diagonal = 6.0 * cof[-1] + plane_sum(cof[-1]) + cof[-2]
    dia.update({-1: diagonal + cof[0], -2: diagonal_of(-2), -3: pltpu.roll(second, ny1 - 1, 0)})
    for j in (-1, -2, -3):
        prepare(j, mask1(j), 8.0, has_far)
    there2 = v1[far, 3]
    more_red1 = jnp.where(mask1(-1) & has_far, red[-1] - first, 0.0)
    more_red2 = red_of(-2, there2)
    top = second + end1 + flat(-1, more_red1) + across(-1, -2, more_red2) + across(-1, 0, red[0])
    black[-1] = black_of(-1, top)
    more1 = jnp.where(mask1(-1) | jnp.logical_not(has_far), 0.0, black[-1] - second / diagonal)
    more2 = black_of(-2, 8.0 * there2 + flat(-2, more_red2) + across(-2, -1, more_red1))
    more3 = black_of(-3, across(-3, -2, more_red2))
    more = {
        0: flat(0, black[0]) + across(0, 1, black[1]) + across(0, -1, black[-1]),
        -1: flat(-1, more1) + across(-1, -2, more2) + across(-1, 0, black[0]),
        -2: flat(-2, more2) + across(-2, -1, more1) + across(-2, -3, more3),
        -3: flat(-3, more3) + across(-3, -2, more2),
    }
    for j, value in more.items():
        res[j] = jnp.where(mask1(j) if j == 0 else mask1(j) & has_far, value, 0.0)
    put_rows(zmid, 2, 3.0 * (res[0] + res[1]) + (res[-1] + res[2]))
    put_rows(zmid, 3, 3.0 * (res[-1] + res[-2]) + (res[0] + res[-3]))
    parts = parts + restrict(zmid, 2, 2, ny2, weights2, 0.5 ** 12)
    for j in range(4):
        mid_ref[at1(j)] = red[j] + black[j]

    cof, dia, fac, for_red, for_black = lows
    cof[-1] = coef2(far)
    dia.update({-1: diagonal2(far) + cof[0], 0: dia2[at2(0)] + cof[-1]})
    prepare(0, mask2(0), 32.0)
    prepare(-1, mask2(-1), 32.0, has_far)
    cof, dia, fac, for_red, for_black = levels

    wait_recv(far, has_far, halo_f, s_f, r_f)
    cof, dia, fac, for_red, for_black = lows
    rhs = {-1: parts[3] + halo_f[far, 0], 0: parts[2] + halo_f[far, 1]}
    red = {j: red_of(j, rhs[j]) for j in (-1, 0)}
    base0 = 32.0 * rhs[0] + flat(0, red[0]) + across(0, -1, red[-1])
    base1 = across(1, 0, red[0])
    wait_recv(near, true, halo_3, s_3, r_3)
    rhs.update({1: parts[0] + halo_3[near, 1], 2: halo_3[near, 0] + parts[1]})
    red.update({j: red_of(j, rhs[j]) for j in (1, 2)})
    low_ref[at2(0)] = red[0] + black_of(0, base0 + across(0, 1, red[1]))
    low_ref[at2(1)] = red[1] + black_of(
        1, 32.0 * rhs[1] + base1 + across(1, 2, red[2]) + flat(1, red[1])
    )

    def wait_sent(side, present, messages):
        @pl.when(present)
        def _():
            for src, dst, s_sem, r_sem in messages:
                copy_out(side, src, dst, s_sem, r_sem).wait_send()

    for side in range(2):
        wait_sent(side, has[side], (
            (c_hbm.at[pl.ds((nz - 2) * side, 2)], halo_c, s_c, r_c),
            (send_x.at[side], halo_x, s_x, r_x),
            (send_q.at[side], halo_q, s_q, r_q),
            (send_c1.at[side], halo_c1, s_c1, r_c1),
            (send_d1.at[side], halo_d1, s_d1, r_d1),
            (send_c2.at[side], halo_c2, s_c2, r_c2),
            (send_2.at[side], halo_2, s_2, r_2),
            (send_n.at[side], halo_n, s_n, r_n),
        ))
    wait_sent(near, true, ((send_3, halo_3, s_3, r_3),))
    wait_sent(far, has_far, ((send_f, halo_f, s_f, r_f),))


def on_device(size, pressure_guess, source, conductance):
    nz, ny, nx = pressure_guess.shape
    pairs = nz // 2
    ny1, nx1, ny2, nx2 = ny // 2, nx // 2, ny // 4, nx // 4

    def vmem(*shape):
        return pltpu.VMEM(shape, F32)

    slab = [vmem(nz, ny, nx)] * 3
    padded = [vmem(pairs + 2, ny, nx)] * 6
    faces = [
        vmem(pairs, ny, nx), vmem(pairs, ny, nx), vmem(pairs, 4, ny, nx),
        vmem(pairs, ny, nx), vmem(pairs, 4, ny, nx),
    ]
    sums = [vmem(pairs, ny, nx)] * 3
    work = [
        vmem(pairs + 2, nx // 128, ny + 16, 128), vmem(4, nx1 // 128, ny1 + 16, 128),
        pltpu.VMEM((nx, nx1), BF16), pltpu.VMEM((nx, nx1), BF16),
        vmem(2, 4, ny1, nx1), vmem(pairs, ny, nx), vmem(2, ny, nx), vmem(2, 4, ny, nx),
        vmem(2, ny1, nx1), vmem(pairs, ny1, nx1), vmem(pairs, ny1, nx1),
        vmem(2, ny2, nx2), vmem(2, ny2, nx2),
    ]
    messages = [
        vmem(2, ny, nx), vmem(2, ny, nx), vmem(2, ny1, nx1), vmem(2, ny1, nx1), vmem(2, 2, ny2, nx2),
        vmem(2, 2, ny1, nx1), vmem(2, ny1, nx1),
    ]
    sent = messages + [vmem(2, ny2, nx2), vmem(2, ny2, nx2)]
    halos = [vmem(2, 2, ny, nx)] + messages + [vmem(2, 2, ny2, nx2), vmem(2, 2, ny2, nx2)]
    sems = [pltpu.SemaphoreType.DMA((3,))] + [pltpu.SemaphoreType.DMA((2,))] * 20

    def run(*refs):
        kernel(size, *refs)

    shapes = ((nz, ny, nx), (pairs, ny1, nx1), (pairs // 2, ny2, nx2))
    inputs = [
        pltpu.with_memory_space_constraint(value, pltpu.HBM)
        for value in (pressure_guess, source, conductance)
    ]
    results = pl.pallas_call(
        run,
        out_shape=tuple(pltpu.VMEM(shape, F32) for shape in shapes),
        in_specs=[pl.BlockSpec(memory_space=pl.ANY)] * 3,
        out_specs=tuple([pl.BlockSpec(memory_space=pltpu.VMEM)] * 3),
        scratch_shapes=slab + padded + faces + sums + work + sent + halos + sems,
        compiler_params=pltpu.CompilerParams(
            collective_id=0, has_side_effects=True, vmem_limit_bytes=48 * 2 ** 20
        ),
    )(*inputs)
    return pl.pallas_call(
        write_out,
        out_shape=tuple(jax.ShapeDtypeStruct(shape, F32) for shape in shapes),
        in_specs=[pl.BlockSpec(memory_space=pl.ANY)] * 3,
        out_specs=tuple([pl.BlockSpec(memory_space=pl.ANY)] * 3),
        scratch_shapes=[pltpu.SemaphoreType.DMA((3,))],
    )(*[pltpu.with_memory_space_constraint(value, pltpu.VMEM) for value in results])


def write_out(p_src, mid_src, low_src, p_dst, mid_dst, low_dst, sem):
    copies = [
        pltpu.make_async_copy(src, dst, sem.at[i])
        for i, (src, dst) in enumerate(((p_src, p_dst), (mid_src, mid_dst), (low_src, low_dst)))
    ]
    for copy in copies:
        copy.start()
    for copy in copies:
        copy.wait()


def solution(mesh):
    size = mesh.shape["gz"]
    spec = P("gz", None, None)
    return jax.shard_map(
        lambda *args: on_device(size, *args), mesh=mesh,
        in_specs=(spec, spec, spec), out_specs=(spec, spec, spec), check_vma=False,
    )
```
